32 devices in a mesh: frame: 4 (over y, core), rows: 8 (over z, x).
Axes of the slice: x: 2, y: 2, z: 4, core: 2. Of those that a mesh axis runs over, the one named last changes fastest.
Arguments:
- latents: bfloat16 [16, 832, 640], P('frame', 'rows'), may hold values from -6 to 6
- cotangent: bfloat16 [16, 832, 640], P('frame', 'rows'), may hold values from -6 to 6
- timesteps: int32 [2], replicated, may hold values from 0 to 999
- prompt_ids: int32 [2, 77], replicated, may hold values from 0 to 49407
- embed_table: bfloat16 [49408, 768], P(('frame', 'rows')), may hold values from -6 to 6
- res_gain: bfloat16 [2, 640], replicated, may hold values from 0.5 to 1.5
- res_shift: bfloat16 [4, 640], replicated, may hold values from -4 to 4
- res_conv: bfloat16 [2, 3, 3, 640, 640], P(None, None, None, 'frame'), may hold values from -0.078125 to 0.078125
- temb_weight: bfloat16 [1280, 640], P('frame'), may hold values from -0.15625 to 0.15625
- st_gain: bfloat16 [4, 640], replicated, may hold values from 0.5 to 1.5
- st_shift: bfloat16 [9, 640], replicated, may hold values from -4 to 4
- st_proj: bfloat16 [2, 640, 640], P(None, 'frame'), may hold values from -0.25 to 0.25
- st_attn: bfloat16 [6, 640, 640], P(None, 'frame'), may hold values from -0.25 to 0.25
- st_cross_kv: bfloat16 [2, 768, 640], P(None, 'frame'), may hold values from -0.21875 to 0.21875
- st_ff_in: bfloat16 [640, 5120], P('frame'), may hold values from -0.25 to 0.25
- st_ff_bias: bfloat16 [5120], replicated, may hold values from -4 to 4
- st_ff_out: bfloat16 [2560, 640], P('frame'), may hold values from -0.125 to 0.125
- motion_gain: bfloat16 [4, 640], P(None, 'frame'), may hold values from 0.5 to 1.5
- motion_shift: bfloat16 [9, 640], P(None, 'frame'), may hold values from -4 to 4
- motion_proj: bfloat16 [2, 640, 640], P(None, 'frame'), may hold values from -0.25 to 0.25
- motion_attn: bfloat16 [2, 4, 640, 640], P(None, None, 'frame'), may hold values from -0.25 to 0.25
- motion_ff_in: bfloat16 [640, 2560], P('frame'), may hold values from -0.25 to 0.25
- motion_ff_bias: bfloat16 [2560], P('frame'), may hold values from -4 to 4
- motion_ff_out: bfloat16 [2560, 640], P('frame'), may hold values from -0.125 to 0.125
Outputs:
- output: bfloat16 [16, 832, 640], P('frame', 'rows')
- input_grad: float32 [16, 832, 640], P('frame', 'rows')
- motion_gain_grad: float32 [4, 640], P(None, 'frame')
- motion_shift_grad: float32 [9, 640], P(None, 'frame')
- motion_proj_grad: float32 [2, 640, 640], P(None, 'frame')
- motion_attn_grad: float32 [2, 4, 640, 640], P(None, None, 'frame')
- motion_ff_in_grad: float32 [640, 2560], P('frame')
- motion_ff_bias_grad: float32 [2560], P('frame')
- motion_ff_out_grad: float32 [2560, 640], P('frame')
The draws below stay inside these ranges and needn't reach their ends.
All inputs are finite; a program needn't handle non-finite values.
Results may differ from the reference program's by a relative error of at most 0.024.
Values may be sent and summed in bfloat16 or wider, within the bound.
A program may use at most 512 MiB of HBM per device.

```python
import math
import jax
import jax.numpy as jnp
import numpy as np
from jax import lax

C = 640
HEADS = 8
GROUPS = 32
FF_ST = 2560
FF_MO = 2560
CTX = 77
CTXW = 768
VOCAB = 49408
TEMB = 1280
FRAMES = 16
SIDE_BIG = 32
SIDE_MID = 24
SIDE_SMALL = 16
N_BIG = 0
N_MID = 1
N_SMALL = 1
NCLIP = 2
GRID_C = 4
GRID_R = 2
CELLS = 104
PIXELS = 832
N_ROWS = 8


def set_ends(drawn, stream_key, low, top_value):
    longest = drawn.shape.index(max(drawn.shape))
    spots = []
    for shift in (0, 1):
        where = [jax.random.randint(jax.random.fold_in(stream_key, axis), (), 0, length) for axis, length in enumerate(drawn.shape)]
        where[longest] = (where[longest] + shift) % drawn.shape[longest]
        spots.append(tuple(where))
    return drawn.at[spots[0]].set(low).at[spots[1]].set(top_value)


def shard_levels(own_key, dims, shards, least, top_value):
    level, own = 1.0, jax.random.fold_in(own_key, 6)
    for dim, blocks in shards:
        heights = jnp.exp(jax.random.uniform(jax.random.fold_in(own, dim), (blocks,), jnp.float32, least / len(shards), top_value / len(shards)))
        level = level * jnp.repeat(heights, dims[dim] // blocks).reshape([-1 if axis == dim else 1 for axis in range(len(dims))])
    return level


def rank_bounds(amount, slope):
    weights = [(1 << 20) // math.isqrt(grade ** slope) + 1 for grade in range(1, amount + 1)]
    scale = 1 + sum(weights) // (1 << 30)
    return np.cumsum(np.array([max(1, weight // scale) for weight in weights]))


def skewed_ids(own_key, dims, count, lean):
    listing = rank_bounds(count, lean)
    pick = jax.random.randint(jax.random.fold_in(own_key, 1), dims, 0, int(listing[count - 1]))
    rank = jnp.searchsorted(jnp.asarray(listing, jnp.int32), pick, side="right")
    return jax.random.permutation(jax.random.fold_in(own_key, 2), count)[rank].astype(jnp.int32)


def noise(key, dims, spread, bound, cuts=(), held_as=jnp.bfloat16):
    level = shard_levels(key, dims, cuts, -0.22, 0.18) if cuts else 1.0
    values = jax.random.normal(key, dims, jnp.float32) * spread * level
    return jnp.minimum(jnp.maximum(values, -bound), bound).astype(held_as)


def setup_inputs(seed: int = 0) -> dict:
    splits = jax.random.split(jax.random.key(seed), 25)
    latents = noise(splits[0], (FRAMES, PIXELS, C), 1.0, 6.0, ((0, 4), (1, 8)))
    cotangent = noise(splits[1], (FRAMES, PIXELS, C), 1.0, 6.0, ((0, 4), (1, 8)))
    timesteps = jax.random.randint(splits[2], (NCLIP,), 0, 1000).astype(jnp.int32)
    prompt_ids = set_ends(skewed_ids(splits[3], (NCLIP, CTX), VOCAB, 2), jax.random.fold_in(splits[3], 3), 0, VOCAB - 1).astype(jnp.int32)
    embed_table = noise(splits[4], (VOCAB, CTXW), 1.0, 6.0, ((0, 32),))
    res_gain = jnp.clip(1.0 + 0.1 * jax.random.normal(splits[5], (2, C), jnp.float32), 0.5, 1.5).astype(jnp.bfloat16)
    res_shift = noise(splits[6], (4, C), 0.3, 4.0)
    res_conv = noise(splits[7], (2, 3, 3, C, C), (9 * C) ** -0.5, 0.078125, ((3, 4),))
    temb_weight = noise(splits[8], (TEMB, C), TEMB ** -0.5, 0.15625, ((0, 4),))
    st_gain = jnp.clip(1.0 + 0.1 * jax.random.normal(splits[9], (4, C), jnp.float32), 0.5, 1.5).astype(jnp.bfloat16)
    st_shift = noise(splits[10], (9, C), 0.3, 4.0)
    st_proj = noise(splits[11], (2, C, C), C ** -0.5, 0.25, ((1, 4),))
    st_attn = noise(splits[12], (6, C, C), C ** -0.5, 0.25, ((1, 4),))
    st_cross_kv = noise(splits[13], (2, CTXW, C), CTXW ** -0.5, 0.21875, ((1, 4),))
    st_ff_in = noise(splits[14], (C, 2 * FF_ST), C ** -0.5, 0.25, ((0, 4),))
    st_ff_bias = noise(splits[15], (2 * FF_ST,), 0.3, 4.0)
    st_ff_out = noise(splits[16], (FF_ST, C), FF_ST ** -0.5, 0.125, ((0, 4),))
    motion_gain = jnp.clip(1.0 + 0.1 * jax.random.normal(splits[17], (4, C), jnp.float32), 0.5, 1.5).astype(jnp.bfloat16)
    motion_shift = noise(splits[18], (9, C), 0.3, 4.0, ((1, 4),))
    motion_proj = noise(splits[19], (2, C, C), C ** -0.5, 0.25, ((1, 4),))
    motion_attn = noise(splits[20], (2, 4, C, C), C ** -0.5, 0.25, ((2, 4),))
    motion_ff_in = noise(splits[21], (C, FF_MO), C ** -0.5, 0.25, ((0, 4),))
    motion_ff_bias = noise(splits[22], (FF_MO,), 0.3, 4.0, ((0, 4),))
    motion_ff_out = noise(splits[23], (FF_MO, C), FF_MO ** -0.5, 0.125, ((0, 4),))
    return {"latents": latents, "cotangent": cotangent, "timesteps": timesteps, "prompt_ids": prompt_ids, "embed_table": embed_table, "res_gain": res_gain, "res_shift": res_shift, "res_conv": res_conv, "temb_weight": temb_weight, "st_gain": st_gain, "st_shift": st_shift, "st_proj": st_proj, "st_attn": st_attn, "st_cross_kv": st_cross_kv, "st_ff_in": st_ff_in, "st_ff_bias": st_ff_bias, "st_ff_out": st_ff_out, "motion_gain": motion_gain, "motion_shift": motion_shift, "motion_proj": motion_proj, "motion_attn": motion_attn, "motion_ff_in": motion_ff_in, "motion_ff_bias": motion_ff_bias, "motion_ff_out": motion_ff_out}


HIGHEST = lax.Precision.HIGHEST
EPSILON = 1e-05

@jax.custom_vjp
def low(v):
    return lax.optimization_barrier(v.astype(jnp.bfloat16)).astype(jnp.float32)

@jax.custom_vjp
def low_back(v):
    return v

def low_keep(v):
    return (low(v), None)

def low_pass(kept, grad):
    return (grad,)

def back_keep(v):
    return (v, None)

def back_low(kept, grad):
    return (low(grad),)
low.defvjp(low_keep, low_pass)
low_back.defvjp(back_keep, back_low)

def clip_layout():
    sides = [SIDE_BIG] * N_BIG + [SIDE_MID] * N_MID + [SIDE_SMALL] * N_SMALL
    layout = []
    offset = 0
    for side in sides:
        layout.append((side, side // GRID_R, side // GRID_C, offset))
        offset = offset + side // GRID_R * (side // GRID_C)
    return layout

def unpack(field, entry):
    side, block_rows, block_cols, offset = entry
    channels = field.shape[-1]
    part = field.reshape(FRAMES, N_ROWS, CELLS, channels)[:, :, offset:offset + block_rows * block_cols]
    part = part.reshape(FRAMES, GRID_R, GRID_C, block_rows, block_cols, channels)
    return jnp.transpose(part, (0, 1, 3, 2, 4, 5)).reshape(FRAMES, side, side, channels)

def pack(images, layout):
    pieces = []
    for image, entry in zip(images, layout):
        side, block_rows, block_cols, offset = entry
        part = image.reshape(FRAMES, GRID_R, block_rows, GRID_C, block_cols, image.shape[-1])
        part = jnp.transpose(part, (0, 1, 3, 2, 4, 5))
        pieces.append(part.reshape(FRAMES, N_ROWS, block_rows * block_cols, image.shape[-1]))
    return jnp.concatenate(pieces, axis=2).reshape(FRAMES, PIXELS, -1)

def time_table(timesteps):
    half_count = TEMB // 2
    frequency = jnp.exp(jnp.arange(half_count, dtype=jnp.float32) * (-math.log(10000.0) / half_count))
    angles = timesteps.astype(jnp.float32)[:, None] * frequency[None, :]
    return jnp.concatenate([jnp.cos(angles), jnp.sin(angles)], axis=1)

def frame_table(frame_ids, channels):
    channel = jnp.arange(channels, dtype=jnp.int32)
    even_index = (channel - channel % 2).astype(jnp.float32)
    frequency = jnp.exp(even_index * (-math.log(10000.0) / channels))
    angles = frame_ids.astype(jnp.float32)[:, None] * frequency[None, :]
    return jnp.where((channel % 2 == 0)[None, :], jnp.sin(angles), jnp.cos(angles))

def group_norm(field, gain, shift):
    grouped = field.reshape(field.shape[:-1] + (GROUPS, field.shape[-1] // GROUPS))
    average = lax.optimization_barrier(jnp.mean(grouped, axis=(1, 2, 4), keepdims=True))
    inv_std = lax.rsqrt(lax.optimization_barrier(jnp.mean(grouped * grouped, axis=(1, 2, 4), keepdims=True)) - average * average + EPSILON)
    return ((grouped - average) * inv_std).reshape(field.shape) * gain + shift

def layer_norm(field, gain, shift):
    average = lax.optimization_barrier(jnp.mean(field, axis=-1, keepdims=True))
    centred = field - average
    variance = lax.optimization_barrier(jnp.mean(centred * centred, axis=-1, keepdims=True))
    return centred * lax.rsqrt(variance + EPSILON) * gain + shift

def project(field, weight):
    return low_back(jnp.dot(field, weight, precision=HIGHEST))

def convolve(field, weight):
    flat_weight = weight.reshape(9 * weight.shape[2], weight.shape[3])

    def per_frame(one_frame):
        padded = jnp.pad(one_frame, ((1, 1), (1, 1), (0, 0)))
        side = one_frame.shape[0]
        tap_list = [padded[row_tap:row_tap + side, col_tap:col_tap + side, :] for row_tap in range(3) for col_tap in range(3)]
        return project(jnp.concatenate(tap_list, axis=-1), flat_weight)
    return lax.map(jax.checkpoint(per_frame), field)

def geglu(pre_act):
    return pre_act[..., :FF_ST] * jax.nn.gelu(pre_act[..., FF_ST:], approximate=False)

def attend(queries, key_rows, value_rows):
    scores = low_back(jnp.dot(queries, key_rows.T, precision=HIGHEST) * queries.shape[-1] ** (-0.5))
    top_score = lax.optimization_barrier(jnp.max(scores, axis=-1, keepdims=True))
    powers = jnp.exp(scores - top_score)
    probs = powers / lax.optimization_barrier(jnp.sum(powers, axis=-1, keepdims=True))
    return jnp.dot(low(probs), value_rows, precision=HIGHEST)

def heads_first(field):
    return jnp.transpose(field.reshape(field.shape[0], HEADS, -1), (1, 0, 2))

def framewise(queries, key_rows, value_rows):

    def per_frame(triple):

        def per_head(head_triple):
            return attend(head_triple[0], head_triple[1], head_triple[2])
        result = lax.map(jax.checkpoint(per_head), (heads_first(triple[0]), heads_first(triple[1]), heads_first(triple[2])))
        return jnp.transpose(result, (1, 0, 2)).reshape(triple[0].shape[0], -1)
    return lax.map(per_frame, (queries, key_rows, value_rows))

def temporal(queries, key_rows, value_rows):
    head_shape = (queries.shape[0], queries.shape[1], HEADS, queries.shape[2] // HEADS)
    scale = (queries.shape[2] // HEADS) ** (-0.5)
    scores = low_back(jnp.einsum('fphd,gphd->phfg', queries.reshape(head_shape), key_rows.reshape(head_shape), precision=HIGHEST) * scale)
    top_score = lax.optimization_barrier(jnp.max(scores, axis=-1, keepdims=True))
    powers = jnp.exp(scores - top_score)
    probs = powers / lax.optimization_barrier(jnp.sum(powers, axis=-1, keepdims=True))
    result = jnp.einsum('phfg,gphd->fphd', low(probs), value_rows.reshape(head_shape), precision=HIGHEST)
    return result.reshape(queries.shape)

def reference(latents, cotangent, timesteps, prompt_ids, embed_table, res_gain, res_shift, res_conv, temb_weight, st_gain, st_shift, st_proj, st_attn, st_cross_kv, st_ff_in, st_ff_bias, st_ff_out, motion_gain, motion_shift, motion_proj, motion_attn, motion_ff_in, motion_ff_bias, motion_ff_out):
    layout = clip_layout()
    temb_proj = jnp.dot(low(jax.nn.silu(time_table(timesteps))), temb_weight.astype(jnp.float32), precision=HIGHEST)
    context = low(embed_table.astype(jnp.float32)[prompt_ids])
    cross_kv = st_cross_kv.astype(jnp.float32)
    cross_keys = low(jnp.einsum('ntw,wc->ntc', context, cross_kv[0], precision=HIGHEST))
    cross_values = low(jnp.einsum('ntw,wc->ntc', context, cross_kv[1], precision=HIGHEST))
    position = frame_table(jnp.arange(FRAMES, dtype=jnp.int32), C)[:, None, None, :]
    rgain, rshift, rconv = (res_gain.astype(jnp.float32), res_shift.astype(jnp.float32), res_conv.astype(jnp.float32))
    sgain, sshift, sproj = (st_gain.astype(jnp.float32), st_shift.astype(jnp.float32), st_proj.astype(jnp.float32))
    sattn, sff_in, sff_bias, sff_out = (st_attn.astype(jnp.float32), st_ff_in.astype(jnp.float32), st_ff_bias.astype(jnp.float32), st_ff_out.astype(jnp.float32))

    def one_clip(image, number, mgain, mshift, mproj, mattn, mff_in, mff_bias, mff_out):
        side = image.shape[1]
        token_shape = (FRAMES, side * side, C)
        h_one = group_norm(image, rgain[0], rshift[0])
        conv_one = convolve(low(jax.nn.silu(h_one)), rconv[0]) + rshift[2] + temb_proj[number]
        h_two = group_norm(conv_one, rgain[1], rshift[1])
        resid = image + convolve(low(jax.nn.silu(h_two)), rconv[1]) + rshift[3]
        proj = project(low(group_norm(resid, sgain[0], sshift[0])), sproj[0]) + sshift[4]
        ln_one = low(layer_norm(proj, sgain[1], sshift[1]))
        self_out = framewise(low(project(ln_one, sattn[0])).reshape(token_shape), low(project(ln_one, sattn[1])).reshape(token_shape), low(project(ln_one, sattn[2])).reshape(token_shape))
        proj = proj + project(low(low_back(self_out.reshape(image.shape))), sattn[3]) + sshift[5]
        ln_two = low(layer_norm(proj, sgain[2], sshift[2]))
        frame_keys = jnp.broadcast_to(cross_keys[number][None], (FRAMES, CTX, C))
        frame_values = jnp.broadcast_to(cross_values[number][None], (FRAMES, CTX, C))
        cross_out = framewise(low(project(ln_two, sattn[4])).reshape(token_shape), frame_keys, frame_values)
        proj = proj + project(low(low_back(cross_out.reshape(image.shape))), sattn[5]) + sshift[6]
        st_pre = project(low(layer_norm(proj, sgain[3], sshift[3])), sff_in) + sff_bias
        proj = proj + project(low(geglu(st_pre)), sff_out) + sshift[7]
        st_out = project(low(proj), sproj[1]) + sshift[8] + resid
        zed = project(low(group_norm(st_out, mgain[0], mshift[0])), mproj[0]) + mshift[4]
        for block in range(2):
            normed = low(layer_norm(zed, mgain[1 + block], mshift[1 + block]) + position)
            query_rows = low(project(normed, mattn[block, 0])).reshape(token_shape)
            key_rows = low(project(normed, mattn[block, 1])).reshape(token_shape)
            value_rows = low(project(normed, mattn[block, 2])).reshape(token_shape)
            time_out = temporal(query_rows, key_rows, value_rows)
            zed = zed + project(low(low_back(time_out.reshape(image.shape))), mattn[block, 3]) + mshift[5 + block]
        motion_pre = project(low(layer_norm(zed, mgain[3], mshift[3])), mff_in) + mff_bias
        zed = zed + project(low(jax.nn.gelu(motion_pre, approximate=False)), mff_out) + mshift[7]
        return st_out + project(low(zed), mproj[1]) + mshift[8]

    def forward(field, mgain, mshift, mproj, mattn, mff_in, mff_bias, mff_out):
        images = [one_clip(unpack(field, entry), number, mgain, mshift, mproj, mattn, mff_in, mff_bias, mff_out) for number, entry in enumerate(layout)]
        return pack(images, layout)
    result, back = jax.vjp(forward, latents.astype(jnp.float32), motion_gain.astype(jnp.float32), motion_shift.astype(jnp.float32), motion_proj.astype(jnp.float32), motion_attn.astype(jnp.float32), motion_ff_in.astype(jnp.float32), motion_ff_bias.astype(jnp.float32), motion_ff_out.astype(jnp.float32))
    grads = back(cotangent.astype(jnp.float32))
    return (result.astype(jnp.bfloat16), grads[0], grads[1], grads[2], grads[3], grads[4], grads[5], grads[6], grads[7])
```

```python
import math

import jax
import jax.numpy as jnp
from jax import lax
from jax.sharding import PartitionSpec as P

HEADS = 8
GROUPS = 32
FF_ST = 2560
TEMB = 1280
SIDE_BIG = 32
SIDE_MID = 24
SIDE_SMALL = 16


HIGHEST = lax.Precision.HIGHEST
EPSILON = 1e-05
FAR = -1e30


def to_low(value):
    return value.astype(jnp.bfloat16)


def matmul(left, weight):
    return jnp.dot(left, weight, preferred_element_type=jnp.float32)


def matmul_back(gradient, weight):
    return lax.dot_general(
        gradient, weight, (((1,), (1,)), ((), ())), preferred_element_type=jnp.float32
    )


def matmul_left(left, right):
    return lax.dot_general(left, right, (((0,), (0,)), ((), ())), preferred_element_type=jnp.float32)


def token_sum(gradient):
    return jnp.sum(gradient, axis=0)


def clip_layout(row_devices):
    grid_cols = min(8, row_devices // 2)
    grid_rows = row_devices // grid_cols
    sides = (
        [SIDE_BIG] * (3 * (row_devices // 64))
        + [SIDE_MID] * max(1, row_devices // 16)
        + [SIDE_SMALL] * max(1, row_devices // 16)
    )
    layout = []
    offset = 0
    for side in sides:
        layout.append((side, side // grid_rows, side // grid_cols, offset))
        offset = offset + side // grid_rows * (side // grid_cols)
    return (layout, grid_rows, grid_cols)


def time_table(timesteps):
    half_count = TEMB // 2
    frequency = jnp.exp(
        jnp.arange(half_count, dtype=jnp.float32) * (-math.log(10000.0) / half_count)
    )
    angles = timesteps.astype(jnp.float32)[:, None] * frequency[None, :]
    return jnp.concatenate([jnp.cos(angles), jnp.sin(angles)], axis=1)


def frame_table(frame_ids, channels):
    channel = jnp.arange(channels, dtype=jnp.int32)
    even_index = (channel - channel % 2).astype(jnp.float32)
    frequency = jnp.exp(even_index * (-math.log(10000.0) / channels))
    angles = frame_ids.astype(jnp.float32)[:, None] * frequency[None, :]
    return jnp.where((channel % 2 == 0)[None, :], jnp.sin(angles), jnp.cos(angles))


def exact_gelu(field):
    return jax.nn.gelu(field, approximate=False)


def geglu(pre_act):
    return pre_act[..., :FF_ST] * jax.nn.gelu(pre_act[..., FF_ST:], approximate=False)


def layer_norm(field, gain, shift):
    average = jnp.mean(field, axis=-1, keepdims=True)
    centred = field - average
    variance = jnp.mean(centred * centred, axis=-1, keepdims=True)
    return centred * lax.rsqrt(variance + EPSILON) * gain + shift


def group_table(channels):
    which = jnp.arange(channels, dtype=jnp.int32) // (channels // GROUPS)
    return (which[:, None] == jnp.arange(GROUPS, dtype=jnp.int32)[None, :]).astype(jnp.float32)


def group_means(first, second, table, count):
    sums = jnp.stack([jnp.sum(first, axis=0), jnp.sum(second, axis=0)])
    means = jnp.dot(sums, table, precision=HIGHEST) / count
    return means


def spread(stats, table):
    return jnp.dot(stats, table.T, precision=HIGHEST)


def norm_groups(field, gain, shift, valid, table, count):
    kept = field * valid
    means = group_means(kept, kept * field, table, count)
    inv_std = lax.rsqrt(means[1] - means[0] * means[0] + EPSILON)
    average, inv_std = spread(jnp.stack([means[0], inv_std]), table)
    normed = (field - average[None]) * inv_std[None]
    return (normed * gain + shift, (normed, inv_std))


def norm_groups_back(gradient, saved, gain, valid, table, count):
    normed, inv_std = saved
    grad_normed = gradient * gain * valid
    means = spread(group_means(grad_normed, grad_normed * normed, table, count), table)
    return inv_std[None] * (grad_normed - means[0][None] - normed * means[1][None]) * valid


def shifted_taps(field, side):
    image = field.reshape(side, side, field.shape[-1])
    padded = jnp.pad(image, ((1, 1), (1, 1), (0, 0)))
    return [
        padded[row_tap : row_tap + side, col_tap : col_tap + side].reshape(field.shape)
        for row_tap in range(3)
        for col_tap in range(3)
    ]


def convolve(field_low, weight, side):
    columns = jnp.concatenate(shifted_taps(field_low, side), axis=1)
    return matmul(columns, weight.reshape(-1, weight.shape[-1]))


def convolve_back(field_low, weight, side):
    total = None
    for tap, shifted in enumerate(shifted_taps(field_low, side)):
        part = matmul_back(shifted, weight[8 - tap])
        total = part if total is None else total + part
    return total


def heads_view(field):
    return field.reshape(field.shape[:-1] + (HEADS, field.shape[-1] // HEADS))


def attend_forward(queries, key_rows, value_rows, bias):
    scale = queries.shape[-1] ** (-0.5)
    scores = (
        jnp.einsum("gqhd,gkhd->ghqk", queries, key_rows, preferred_element_type=jnp.float32) * scale
        + bias
    )
    top_score = jnp.max(scores, axis=-1, keepdims=True)
    powers = jnp.exp(scores - top_score)
    totals = jnp.sum(powers, axis=-1, keepdims=True)
    weights = to_low(powers / totals)
    result = jnp.einsum("ghqk,gkhd->gqhd", weights, value_rows, preferred_element_type=jnp.float32)
    return (result, top_score + jnp.log(totals))


def attend_backward(queries, key_rows, value_rows, bias, log_total, gradient, keys_too):
    scale = queries.shape[-1] ** (-0.5)
    scores = (
        jnp.einsum("gqhd,gkhd->ghqk", queries, key_rows, preferred_element_type=jnp.float32) * scale
        + bias
    )
    probs = jnp.exp(scores - log_total)
    grad_probs = jnp.einsum(
        "gqhd,gkhd->ghqk", gradient, value_rows, preferred_element_type=jnp.float32
    )
    inner = jnp.sum(probs * grad_probs, axis=-1, keepdims=True)
    grad_scores = to_low(probs * (grad_probs - inner))
    grad_query = (
        jnp.einsum("ghqk,gkhd->gqhd", grad_scores, key_rows, preferred_element_type=jnp.float32)
        * scale
    )
    if not keys_too:
        return grad_query
    grad_key = (
        jnp.einsum("ghqk,gqhd->gkhd", grad_scores, queries, preferred_element_type=jnp.float32)
        * scale
    )
    grad_value = jnp.einsum(
        "ghqk,gqhd->gkhd", to_low(probs), gradient, preferred_element_type=jnp.float32
    )
    return (grad_query, grad_key, grad_value)


def onehot(indices, width):
    return (indices[:, None] == jnp.arange(width, dtype=jnp.int32)[None, :]).astype(jnp.bfloat16)


class Places:
    def __init__(self, frames_here, channels):
        self.rows = lax.axis_size("rows")
        self.frames = lax.axis_size("frame")
        self.row = lax.axis_index("rows")
        self.frame = lax.axis_index("frame")
        self.frames_here = frames_here
        self.layout, self.grid_rows, self.grid_cols = clip_layout(self.rows)
        self.clips = len(self.layout)
        self.units = frames_here * self.clips
        assert self.units <= self.rows
        self.channels = channels
        self.side = max(entry[0] for entry in self.layout)
        self.block_max = max(entry[1] * entry[2] for entry in self.layout)
        self.shares = [-(-entry[1] * entry[2] // self.frames) for entry in self.layout]
        self.share_max = max(self.shares)
        self.share_total = sum(self.shares)
        self.clip = self.row % self.clips
        sides = jnp.array([entry[0] for entry in self.layout], jnp.int32)
        self.my_side = jnp.where(self.row < self.units, sides[self.clip], 0)
        self.safe_side = jnp.maximum(self.my_side, self.grid_rows * self.grid_cols)
        cells = jnp.arange(self.side * self.side, dtype=jnp.int32)
        self.cell_row, self.cell_col = cells // self.side, cells % self.side
        self.valid = (self.cell_row < self.my_side) & (self.cell_col < self.my_side)
        block_rows = sides[self.clip] // self.grid_rows
        block_cols = sides[self.clip] // self.grid_cols
        self.device = self.cell_row // block_rows * self.grid_cols + self.cell_col // block_cols
        self.in_block = self.cell_row % block_rows * block_cols + self.cell_col % block_cols
        shares = jnp.array(self.shares, jnp.int32)
        share = shares[self.clip]
        block_index = jnp.where(self.valid, self.device * self.block_max + self.in_block, -1)
        self.block_table = onehot(block_index, self.rows * self.block_max)
        column_index = (
            (self.in_block // share * self.rows + self.device) * self.share_max
            + self.in_block % share
        )
        column_index = jnp.where(self.valid, column_index, -1)
        self.column_table = onehot(column_index, self.frames * self.rows * self.share_max)
        picks = []
        for number in range(self.clips):
            cell = jnp.arange(self.shares[number], dtype=jnp.int32)[:, None]
            when = jnp.arange(self.frames * frames_here, dtype=jnp.int32)[None, :]
            source = (
                when // frames_here * self.rows + when % frames_here * self.clips + number
            ) * self.share_max + cell
            picks.append(source.reshape(-1))
        self.pick_table = onehot(
            jnp.concatenate(picks), self.frames * self.rows * self.share_max
        )

    def blocks_to_unit(self, blocks):
        pieces = []
        for frame in range(self.frames_here):
            for side, height, width, offset in self.layout:
                piece = blocks[frame, offset : offset + height * width]
                pieces.append(jnp.pad(piece, ((0, self.block_max - height * width), (0, 0))))
        for _ in range(self.units, self.rows):
            pieces.append(jnp.zeros_like(pieces[0]))
        received = lax.all_to_all(jnp.stack(pieces), "rows", 0, 0)
        return matmul(self.block_table, received.reshape(-1, self.channels))

    def unit_to_blocks(self, field_low):
        send = to_low(matmul_left(self.block_table, field_low))
        send = send.reshape(self.rows, self.block_max, self.channels)
        received = lax.all_to_all(send, "rows", 0, 0)
        frames = []
        for frame in range(self.frames_here):
            frames.append(
                jnp.concatenate(
                    [
                        received[frame * self.clips + number, : entry[1] * entry[2]]
                        for number, entry in enumerate(self.layout)
                    ]
                )
            )
        return jnp.stack(frames)

    def unit_to_columns(self, fields_low):
        width = sum(field.shape[-1] for field in fields_low)
        joined = jnp.concatenate(fields_low, axis=1)
        send = to_low(matmul_left(self.column_table, joined))
        send = send.reshape(self.frames * self.rows, self.share_max, width)
        received = lax.all_to_all(send, ("frame", "rows"), 0, 0)
        return matmul(self.pick_table, received.reshape(-1, width))

    def columns_to_unit(self, field_low):
        send = to_low(matmul_left(self.pick_table, field_low))
        send = send.reshape(self.frames * self.rows, self.share_max, self.channels)
        received = lax.all_to_all(send, ("frame", "rows"), 0, 0)
        return matmul(self.column_table, received.reshape(-1, self.channels))

    def blocks_to_columns(self, blocks):
        parts = []
        for number, (side, height, width, offset) in enumerate(self.layout):
            share = self.shares[number]
            part = blocks[:, offset : offset + height * width]
            part = jnp.pad(part, ((0, 0), (0, share * self.frames - height * width), (0, 0)))
            parts.append(part.reshape(self.frames_here, self.frames, share, self.channels))
        send = jnp.transpose(jnp.concatenate(parts, axis=2), (1, 0, 2, 3))
        received = lax.all_to_all(send, "frame", 0, 0)
        received = received.reshape(-1, self.share_total, self.channels)
        return jnp.transpose(received, (1, 0, 2)).reshape(-1, self.channels)

    def columns_to_blocks(self, field_low):
        send = jnp.transpose(field_low.reshape(self.share_total, -1, self.channels), (1, 0, 2))
        send = send.reshape(self.frames, self.frames_here, self.share_total, self.channels)
        received = lax.all_to_all(send, "frame", 0, 0)
        parts = []
        start = 0
        for number, (side, height, width, offset) in enumerate(self.layout):
            share = self.shares[number]
            part = jnp.transpose(received[:, :, start : start + share], (1, 0, 2, 3))
            part = part.reshape(self.frames_here, self.frames * share, self.channels)
            parts.append(part[:, : height * width])
            start = start + share
        return jnp.concatenate(parts, axis=1)


def gather_rows(shard, lead):
    gathered = lax.all_gather(shard, "frame", axis=0, tiled=False)
    if lead == 0:
        return gathered.reshape(-1, shard.shape[-1])
    return jnp.moveaxis(gathered, 0, lead).reshape(
        shard.shape[:lead] + (-1, shard.shape[-1])
    )


def on_device(
    latents,
    cotangent,
    timesteps,
    prompt_ids,
    embed_table,
    res_gain,
    res_shift,
    res_conv,
    temb_weight,
    st_gain,
    st_shift,
    st_proj,
    st_attn,
    st_cross_kv,
    st_ff_in,
    st_ff_bias,
    st_ff_out,
    motion_gain,
    motion_shift,
    motion_proj,
    motion_attn,
    motion_ff_in,
    motion_ff_bias,
    motion_ff_out,
):
    frames_here, cell_count, channels = latents.shape
    places = Places(frames_here, channels)
    side = places.side
    valid = places.valid.astype(jnp.float32)[:, None]
    table = group_table(channels)
    count = (places.safe_side * places.safe_side * (channels // GROUPS)).astype(jnp.float32)

    conv_one_all = gather_rows(res_conv[0].reshape(9, -1, channels), 1)
    conv_two_all = gather_rows(res_conv[1].reshape(9, -1, channels), 1)
    sproj_all = [gather_rows(st_proj[i], 0) for i in range(2)]
    sattn_all = [gather_rows(st_attn[i], 0) for i in range(6)]
    cross_all = [gather_rows(st_cross_kv[i], 0) for i in range(2)]
    sffin_all = gather_rows(st_ff_in, 0)
    sffout_all = gather_rows(st_ff_out, 0)
    mproj_all = [gather_rows(motion_proj[i], 0) for i in range(2)]
    mattn_all = [[gather_rows(motion_attn[b, i], 0) for i in range(4)] for b in range(2)]
    mffin_all = gather_rows(motion_ff_in, 0)
    mffout_all = gather_rows(motion_ff_out, 0)
    small = jnp.concatenate(
        [motion_gain.reshape(-1), motion_shift.reshape(-1), motion_ff_bias.reshape(-1)]
    )
    small_all = lax.all_gather(small, "frame", axis=0, tiled=False)
    own = channels // places.frames
    mgain = jnp.transpose(
        small_all[:, : 4 * own].reshape(places.frames, 4, own), (1, 0, 2)
    ).reshape(4, channels).astype(jnp.float32)
    mshift = jnp.transpose(
        small_all[:, 4 * own : 13 * own].reshape(places.frames, 9, own), (1, 0, 2)
    ).reshape(9, channels).astype(jnp.float32)
    mffbias = small_all[:, 13 * own :].reshape(-1).astype(jnp.float32)

    field = places.blocks_to_unit(latents)
    grad_unit = places.blocks_to_unit(cotangent)
    grad_columns = places.blocks_to_columns(cotangent)

    rgain, rshift = (res_gain.astype(jnp.float32), res_shift.astype(jnp.float32))
    sgain, sshift, sffbias = (
        st_gain.astype(jnp.float32),
        st_shift.astype(jnp.float32),
        st_ff_bias.astype(jnp.float32),
    )
    own_temb = TEMB // places.frames
    time_low = to_low(jax.nn.silu(time_table(timesteps)))
    time_mine = lax.dynamic_slice_in_dim(time_low, places.frame * own_temb, own_temb, 1)
    temb_proj = lax.psum(matmul(time_mine, temb_weight), "frame")
    time_row = lax.dynamic_index_in_dim(temb_proj, places.clip, 0, keepdims=False)

    vocab_rows = embed_table.shape[0]
    local_ids = prompt_ids - lax.axis_index(("frame", "rows")) * vocab_rows
    clip_count, prompt_count = prompt_ids.shape
    ids_table = onehot(local_ids.reshape(-1), vocab_rows)
    context = lax.psum(to_low(matmul(ids_table, embed_table)), ("frame", "rows"))
    context = context.reshape(clip_count, prompt_count, -1)
    context_low = lax.dynamic_index_in_dim(context, places.clip, 0, keepdims=False)
    cross_keys = to_low(matmul(context_low, cross_all[0]))
    cross_values = to_low(matmul(context_low, cross_all[1]))

    h_one, saved_one = norm_groups(field, rgain[0], rshift[0], valid, table, count)
    conv_one = (
        convolve(to_low(jax.nn.silu(h_one) * valid), conv_one_all, side) + rshift[2] + time_row
    )
    h_two, saved_two = norm_groups(conv_one, rgain[1], rshift[1], valid, table, count)
    resid = (
        field
        + convolve(to_low(jax.nn.silu(h_two) * valid), conv_two_all, side)
        + rshift[3]
    )
    st_norm, saved_three = norm_groups(resid, sgain[0], sshift[0], valid, table, count)
    proj_one = matmul(to_low(st_norm), sproj_all[0]) + sshift[4]
    ln_one = to_low(layer_norm(proj_one, sgain[1], sshift[1]))
    key_bias = jnp.where(places.valid, 0.0, FAR)[None, None, None, :]
    space_query, space_key, space_value = (
        heads_view(to_low(matmul(ln_one, sattn_all[i])))[None] for i in range(3)
    )
    space_out, space_total = attend_forward(space_query, space_key, space_value, key_bias)
    space_low = to_low(space_out.reshape(-1, channels))
    proj_two = proj_one + matmul(space_low, sattn_all[3]) + sshift[5]
    ln_two = to_low(layer_norm(proj_two, sgain[2], sshift[2]))
    cross_query = heads_view(to_low(matmul(ln_two, sattn_all[4])))[None]
    cross_key, cross_value = (heads_view(cross_keys)[None], heads_view(cross_values)[None])
    cross_out, cross_total = attend_forward(cross_query, cross_key, cross_value, 0.0)
    cross_low = to_low(cross_out.reshape(-1, channels))
    proj_three = proj_two + matmul(cross_low, sattn_all[5]) + sshift[6]
    ln_three = to_low(layer_norm(proj_three, sgain[3], sshift[3]))
    st_pre = matmul(ln_three, sffin_all) + sffbias
    proj_four = proj_three + matmul(to_low(geglu(st_pre)), sffout_all) + sshift[7]
    st_out = matmul(to_low(proj_four), sproj_all[1]) + sshift[8] + resid
    motion_norm, saved_motion = norm_groups(st_out, mgain[0], mshift[0], valid, table, count)

    moved = places.unit_to_columns([to_low(motion_norm), to_low(st_out)])
    motion_in = to_low(moved[:, :channels])
    st_columns = moved[:, channels:]
    frame_total = places.frames * frames_here
    position = frame_table(jnp.arange(frame_total, dtype=jnp.int32), channels)
    position = jnp.broadcast_to(
        position[None], (places.share_total, frame_total, channels)
    ).reshape(-1, channels)
    per_group = max(n for n in range(1, 14) if places.share_total % n == 0)
    group_len = per_group * frame_total
    cell_of = jnp.arange(group_len, dtype=jnp.int32) // frame_total
    cell_bias = jnp.where(cell_of[:, None] == cell_of[None, :], 0.0, FAR)[None, None]

    def grouped(tokens):
        return heads_view(tokens.reshape(-1, group_len, channels))

    zed = matmul(motion_in, mproj_all[0]) + mshift[4]
    zed_list = []
    block_saved = []
    for block in range(2):
        zed_list.append(zed)
        normed = to_low(layer_norm(zed, mgain[1 + block], mshift[1 + block]) + position)
        queries, key_rows, value_rows = (
            grouped(to_low(matmul(normed, mattn_all[block][i]))) for i in range(3)
        )
        result, log_total = attend_forward(queries, key_rows, value_rows, cell_bias)
        time_out = to_low(result.reshape(-1, channels))
        block_saved.append((normed, queries, key_rows, value_rows, log_total, time_out))
        zed = zed + matmul(time_out, mattn_all[block][3]) + mshift[5 + block]
    zed_last = zed
    ln_last = to_low(layer_norm(zed_last, mgain[3], mshift[3]))
    motion_pre = matmul(ln_last, mffin_all) + mffbias
    hidden_low = to_low(exact_gelu(motion_pre))
    zed = zed_last + matmul(hidden_low, mffout_all) + mshift[7]
    zed_low = to_low(zed)
    out_columns = to_low(st_columns + matmul(zed_low, mproj_all[1]) + mshift[8])
    output = places.columns_to_blocks(out_columns)

    grad_low = grad_columns
    grad_out = grad_columns.astype(jnp.float32)
    d_shift = [None] * 9
    d_gain = [None] * 4
    d_proj_out = matmul_left(zed_low, grad_low)
    d_shift[8] = token_sum(grad_out)
    grad_zed = matmul_back(grad_low, mproj_all[1])
    grad_low = to_low(grad_zed)
    d_ff_out = matmul_left(hidden_low, grad_low)
    d_shift[7] = token_sum(grad_zed)
    grad_pre = jax.vjp(exact_gelu, motion_pre)[1](matmul_back(grad_low, mffout_all))[0]
    pre_low = to_low(grad_pre)
    d_ff_in = matmul_left(ln_last, pre_low)
    d_ff_bias = token_sum(grad_pre)
    grad_in, d_gain[3], d_shift[3] = jax.vjp(layer_norm, zed_last, mgain[3], mshift[3])[1](
        matmul_back(pre_low, mffin_all)
    )
    grad_zed = grad_zed + grad_in
    d_attn = [[None] * 4, [None] * 4]
    for block in (1, 0):
        normed, queries, key_rows, value_rows, log_total, time_out = block_saved[block]
        grad_low = to_low(grad_zed)
        d_attn[block][3] = matmul_left(time_out, grad_low)
        d_shift[5 + block] = token_sum(grad_zed)
        grad_time = grouped(to_low(matmul_back(grad_low, mattn_all[block][3])))
        members = attend_backward(
            queries, key_rows, value_rows, cell_bias, log_total, grad_time, True
        )
        grad_norm = 0.0
        for which, member in enumerate(members):
            member_low = to_low(member.reshape(-1, channels))
            d_attn[block][which] = matmul_left(normed, member_low)
            grad_norm = grad_norm + matmul_back(member_low, mattn_all[block][which])
        grad_in, d_gain[1 + block], d_shift[1 + block] = jax.vjp(
            layer_norm, zed_list[block], mgain[1 + block], mshift[1 + block]
        )[1](grad_norm)
        grad_zed = grad_zed + grad_in
    grad_low = to_low(grad_zed)
    d_proj_in = matmul_left(motion_in, grad_low)
    d_shift[4] = token_sum(grad_zed)
    grad_motion = matmul_back(grad_low, mproj_all[0])

    def share_rows(gradient):
        mine = lax.psum_scatter(to_low(gradient), "frame", scatter_dimension=0, tiled=True)
        return lax.psum(mine, "rows").astype(jnp.float32)

    ff_out_grad = share_rows(d_ff_out)
    ff_in_grad = share_rows(d_ff_in)
    proj_grad = jnp.stack([share_rows(d_proj_in), share_rows(d_proj_out)])
    attn_grad = jnp.stack([jnp.stack([share_rows(d) for d in d_attn[b]]) for b in range(2)])

    grad_gn = places.columns_to_unit(to_low(grad_motion))
    d_gain[0] = token_sum(grad_gn * saved_motion[0])
    d_shift[0] = token_sum(grad_gn)
    small_grads = jnp.concatenate(
        [
            jnp.stack(d_gain).reshape(4, places.frames, own),
            jnp.stack(d_shift).reshape(9, places.frames, own),
            jnp.transpose(
                d_ff_bias.reshape(places.frames, -1, own), (1, 0, 2)
            ),
        ]
    )
    small_grads = lax.psum(small_grads, ("frame", "rows"))
    small_mine = lax.dynamic_index_in_dim(small_grads, places.frame, 1, keepdims=False)
    gain_grad, shift_grad = (small_mine[:4], small_mine[4:13])
    ff_bias_grad = small_mine[13:].reshape(-1)

    grad_st = grad_unit + norm_groups_back(grad_gn, saved_motion, mgain[0], valid, table, count)
    grad_res = grad_st
    grad_four = matmul_back(to_low(grad_st), sproj_all[1])
    grad_act = matmul_back(to_low(grad_four), sffout_all)
    grad_pre_st = jax.vjp(geglu, st_pre)[1](grad_act)[0]
    grad_ln = matmul_back(to_low(grad_pre_st), sffin_all)
    grad_three = (
        grad_four
        + jax.vjp(lambda field_in: layer_norm(field_in, sgain[3], sshift[3]), proj_three)[1](
            grad_ln
        )[0]
    )
    grad_cross = heads_view(to_low(matmul_back(to_low(grad_three), sattn_all[5])))[None]
    grad_query = attend_backward(
        cross_query, cross_key, cross_value, 0.0, cross_total, grad_cross, False
    )
    grad_ln = matmul_back(to_low(grad_query.reshape(-1, channels)), sattn_all[4])
    grad_two = (
        grad_three
        + jax.vjp(lambda field_in: layer_norm(field_in, sgain[2], sshift[2]), proj_two)[1](grad_ln)[
            0
        ]
    )
    grad_space = heads_view(to_low(matmul_back(to_low(grad_two), sattn_all[3])))[None]
    members = attend_backward(
        space_query, space_key, space_value, key_bias, space_total, grad_space, True
    )
    grad_ln = 0.0
    for which, member in enumerate(members):
        grad_ln = grad_ln + matmul_back(to_low(member.reshape(-1, channels)), sattn_all[which])
    grad_one = (
        grad_two
        + jax.vjp(lambda field_in: layer_norm(field_in, sgain[1], sshift[1]), proj_one)[1](grad_ln)[
            0
        ]
    )
    grad_gn = matmul_back(to_low(grad_one), sproj_all[0])
    grad_res = grad_res + norm_groups_back(grad_gn, saved_three, sgain[0], valid, table, count)
    grad_act = convolve_back(to_low(grad_res), conv_two_all, side)
    grad_h = jax.vjp(jax.nn.silu, h_two)[1](grad_act)[0]
    grad_conv = norm_groups_back(grad_h, saved_two, rgain[1], valid, table, count)
    grad_act = convolve_back(to_low(grad_conv), conv_one_all, side)
    grad_h = jax.vjp(jax.nn.silu, h_one)[1](grad_act)[0]
    grad_field = grad_res + norm_groups_back(grad_h, saved_one, rgain[0], valid, table, count)
    input_grad = places.unit_to_blocks(to_low(grad_field)).astype(jnp.float32)

    return (
        output,
        input_grad,
        gain_grad,
        shift_grad,
        proj_grad,
        attn_grad,
        ff_in_grad,
        ff_bias_grad,
        ff_out_grad,
    )
def solution(mesh):
    return jax.shard_map(
        on_device,
        mesh=mesh,
        in_specs=(
            P("frame", "rows", None),
            P("frame", "rows", None),
            P(),
            P(),
            P(("frame", "rows"), None),
            P(),
            P(),
            P(None, None, None, "frame", None),
            P("frame", None),
            P(),
            P(),
            P(None, "frame", None),
            P(None, "frame", None),
            P(None, "frame", None),
            P("frame", None),
            P(),
            P("frame", None),
            P(None, "frame"),
            P(None, "frame"),
            P(None, "frame", None),
            P(None, None, "frame", None),
            P("frame", None),
            P("frame"),
            P("frame", None),
        ),
        out_specs=(
            P("frame", "rows", None),
            P("frame", "rows", None),
            P(None, "frame"),
            P(None, "frame"),
            P(None, "frame", None),
            P(None, None, "frame", None),
            P("frame", None),
            P("frame"),
            P("frame", None),
        ),
        check_vma=False,
    )
```

```python
import functools
import math

import jax
import jax.numpy as jnp
from jax import lax
from jax.experimental import pallas as pl
from jax.experimental.pallas import tpu as pltpu
from jax.sharding import PartitionSpec as P

HEADS = 8
GROUPS = 32
FF_ST = 2560
TEMB = 1280
SIDE_BIG = 32
SIDE_MID = 24
SIDE_SMALL = 16


HIGHEST = lax.Precision.HIGHEST
EPSILON = 1e-05
FAR = -1e30
MESH = pl.DeviceIdType.MESH


def to_low(value):
    return value.astype(jnp.bfloat16)


def matmul(left, weight):
    return jnp.dot(left, weight, preferred_element_type=jnp.float32)


def matmul_back(gradient, weight):
    return lax.dot_general(
        gradient, weight, (((1,), (1,)), ((), ())), preferred_element_type=jnp.float32
    )


def matmul_left(left, right):
    return lax.dot_general(left, right, (((0,), (0,)), ((), ())), preferred_element_type=jnp.float32)


def token_sum(gradient):
    return jnp.sum(gradient, axis=0)


def clip_layout(row_devices):
    grid_cols = min(8, row_devices // 2)
    grid_rows = row_devices // grid_cols
    sides = (
        [SIDE_BIG] * (3 * (row_devices // 64))
        + [SIDE_MID] * max(1, row_devices // 16)
        + [SIDE_SMALL] * max(1, row_devices // 16)
    )
    layout = []
    offset = 0
    for side in sides:
        layout.append((side, side // grid_rows, side // grid_cols, offset))
        offset = offset + side // grid_rows * (side // grid_cols)
    return (layout, grid_rows, grid_cols)


def time_table(timesteps):
    half_count = TEMB // 2
    frequency = jnp.exp(
        jnp.arange(half_count, dtype=jnp.float32) * (-math.log(10000.0) / half_count)
    )
    angles = timesteps.astype(jnp.float32)[:, None] * frequency[None, :]
    return jnp.concatenate([jnp.cos(angles), jnp.sin(angles)], axis=1)


def frame_table(frame_ids, channels):
    channel = jnp.arange(channels, dtype=jnp.int32)
    even_index = (channel - channel % 2).astype(jnp.float32)
    frequency = jnp.exp(even_index * (-math.log(10000.0) / channels))
    angles = frame_ids.astype(jnp.float32)[:, None] * frequency[None, :]
    return jnp.where((channel % 2 == 0)[None, :], jnp.sin(angles), jnp.cos(angles))


def group_table(channels):
    which = jnp.arange(channels, dtype=jnp.int32) // (channels // GROUPS)
    return (which[:, None] == which[None, :]).astype(jnp.float32)


def onehot(indices, width):
    return (indices[:, None] == jnp.arange(width, dtype=jnp.int32)[None, :]).astype(jnp.bfloat16)


class Places:
    def __init__(self, frames_here, channels):
        self.rows = lax.axis_size("rows")
        self.frames = lax.axis_size("frame")
        self.row = lax.axis_index("rows")
        self.frame = lax.axis_index("frame")
        self.frames_here = frames_here
        self.layout, self.grid_rows, self.grid_cols = clip_layout(self.rows)
        self.clips = len(self.layout)
        self.units = frames_here * self.clips
        assert self.units <= self.rows
        self.channels = channels
        self.side = max(entry[0] for entry in self.layout)
        self.block_max = max(entry[1] * entry[2] for entry in self.layout)
        self.shares = [-(-entry[1] * entry[2] // self.frames) for entry in self.layout]
        self.share_max = max(self.shares)
        self.share_total = sum(self.shares)
        self.clip = self.row % self.clips
        sides = jnp.array([entry[0] for entry in self.layout], jnp.int32)
        self.my_side = jnp.where(self.row < self.units, sides[self.clip], 0)
        self.safe_side = jnp.maximum(self.my_side, self.grid_rows * self.grid_cols)
        cells = jnp.arange(self.side * self.side, dtype=jnp.int32)
        self.cell_row, self.cell_col = cells // self.side, cells % self.side
        self.valid = (self.cell_row < self.my_side) & (self.cell_col < self.my_side)
        block_rows = sides[self.clip] // self.grid_rows
        block_cols = sides[self.clip] // self.grid_cols
        self.device = self.cell_row // block_rows * self.grid_cols + self.cell_col // block_cols
        self.in_block = self.cell_row % block_rows * block_cols + self.cell_col % block_cols
        shares = jnp.array(self.shares, jnp.int32)
        share = shares[self.clip]
        block_index = jnp.where(self.valid, self.device * self.block_max + self.in_block, -1)
        self.block_table = onehot(block_index, self.rows * self.block_max)
        column_index = (
            (self.in_block // share * self.rows + self.device) * self.share_max
            + self.in_block % share
        )
        column_index = jnp.where(self.valid, column_index, -1)
        self.column_table = onehot(column_index, self.frames * self.rows * self.share_max)
        picks = []
        for number in range(self.clips):
            cell = jnp.arange(self.shares[number], dtype=jnp.int32)[:, None]
            when = jnp.arange(self.frames * frames_here, dtype=jnp.int32)[None, :]
            source = (
                when // frames_here * self.rows + when % frames_here * self.clips + number
            ) * self.share_max + cell
            picks.append(source.reshape(-1))
        self.pick_table = onehot(
            jnp.concatenate(picks), self.frames * self.rows * self.share_max
        )

    def blocks_to_unit(self, blocks):
        pieces = []
        for frame in range(self.frames_here):
            for side, height, width, offset in self.layout:
                piece = blocks[frame, offset : offset + height * width]
                pieces.append(jnp.pad(piece, ((0, self.block_max - height * width), (0, 0))))
        for _ in range(self.units, self.rows):
            pieces.append(jnp.zeros_like(pieces[0]))
        received = lax.all_to_all(jnp.stack(pieces), "rows", 0, 0)
        return matmul(self.block_table, received.reshape(-1, self.channels))

    def unit_to_blocks(self, field_low):
        send = to_low(matmul_left(self.block_table, field_low))
        send = send.reshape(self.rows, self.block_max, self.channels)
        received = lax.all_to_all(send, "rows", 0, 0)
        frames = []
        for frame in range(self.frames_here):
            frames.append(
                jnp.concatenate(
                    [
                        received[frame * self.clips + number, : entry[1] * entry[2]]
                        for number, entry in enumerate(self.layout)
                    ]
                )
            )
        return jnp.stack(frames)

    def unit_to_columns(self, fields_low):
        width = sum(field.shape[-1] for field in fields_low)
        joined = jnp.concatenate(fields_low, axis=1)
        send = to_low(matmul_left(self.column_table, joined))
        send = send.reshape(self.frames * self.rows, self.share_max, width)
        received = lax.all_to_all(send, ("frame", "rows"), 0, 0)
        return matmul(self.pick_table, received.reshape(-1, width))

    def columns_to_unit(self, field_low):
        send = to_low(matmul_left(self.pick_table, field_low))
        send = send.reshape(self.frames * self.rows, self.share_max, self.channels)
        received = lax.all_to_all(send, ("frame", "rows"), 0, 0)
        return matmul(self.column_table, received.reshape(-1, self.channels))

    def blocks_to_columns(self, blocks):
        parts = []
        for number, (side, height, width, offset) in enumerate(self.layout):
            share = self.shares[number]
            part = blocks[:, offset : offset + height * width]
            part = jnp.pad(part, ((0, 0), (0, share * self.frames - height * width), (0, 0)))
            parts.append(part.reshape(self.frames_here, self.frames, share, self.channels))
        send = jnp.transpose(jnp.concatenate(parts, axis=2), (1, 0, 2, 3))
        received = lax.all_to_all(send, "frame", 0, 0)
        received = received.reshape(-1, self.share_total, self.channels)
        return jnp.transpose(received, (1, 0, 2)).reshape(-1, self.channels)

    def columns_to_blocks(self, field_low):
        send = jnp.transpose(field_low.reshape(self.share_total, -1, self.channels), (1, 0, 2))
        send = send.reshape(self.frames, self.frames_here, self.share_total, self.channels)
        received = lax.all_to_all(send, "frame", 0, 0)
        parts = []
        start = 0
        for number, (side, height, width, offset) in enumerate(self.layout):
            share = self.shares[number]
            part = jnp.transpose(received[:, :, start : start + share], (1, 0, 2, 3))
            part = part.reshape(self.frames_here, self.frames * share, self.channels)
            parts.append(part[:, : height * width])
            start = start + share
        return jnp.concatenate(parts, axis=1)


def swap(value, axis, bit):
    count = lax.axis_size(axis)
    return lax.ppermute(value, axis, [(i, i ^ bit) for i in range(count)])


def exchange_pieces(shard, near, half):
    first = swap(half, "frame", 2)
    second = swap(first, "rows", 1)
    return (shard, near, first, second, swap(first, "frame", 1), swap(second, "frame", 1))


def piece_places():
    frame = lax.axis_index("frame")
    odd_row = lax.axis_index("rows") % 2
    far, corner = 2 * (frame ^ 2), 2 * (frame ^ 3)
    return jnp.stack(
        [
            2 * frame,
            2 * (frame ^ 1),
            far + odd_row,
            far + 1 - odd_row,
            corner + odd_row,
            corner + 1 - odd_row,
        ]
    ).astype(jnp.int32)


def start_load(places_ref, pieces, lead, target, sem):
    if len(pieces) == 1:
        source = pieces[0] if lead is None else pieces[0].at[lead]
        pltpu.make_async_copy(source, target, sem).start()
        return
    half = pieces[0].shape[-2] // 2
    for number, piece in enumerate(pieces):
        start = pl.multiple_of(places_ref[number] * half, 16)
        source = piece if lead is None else piece.at[lead]
        where = target.at[pl.ds(start, piece.shape[-2])]
        pltpu.make_async_copy(source, where, sem).start()


def pair_load(places_ref, groups, lead, target, sem):
    if lead < 2:
        start_load(places_ref, groups[0], lead, target, sem)
    else:
        start_load(places_ref, groups[1], lead - 2, target, sem)


def finish_load(target, sem):
    pltpu.make_async_copy(target, target, sem).wait()


def run_kernel(body, places_row, arrays, groups, outs, scratch, flops):
    count, pieces = len(arrays), sum(len(group) for group in groups)
    out_count = len(outs)

    def kernel(*refs):
        held = list(refs[1 + count : 1 + count + pieces])
        grouped = [[held.pop(0) for _ in group] for group in groups]
        outputs = refs[1 + count + pieces : 1 + count + pieces + out_count]
        body(
            refs[0],
            refs[1 : 1 + count],
            grouped,
            outputs,
            refs[1 + count + pieces + out_count :],
        )

    whole = pl.BlockSpec(memory_space=pltpu.VMEM)
    flat = [piece for group in groups for piece in group]
    moved = sum(a.size * a.dtype.itemsize for a in list(arrays) + flat)
    moved += sum(math.prod(o.shape) * o.dtype.itemsize for o in outs)
    return pl.pallas_call(
        kernel,
        out_shape=outs,
        in_specs=[pl.BlockSpec(memory_space=pltpu.SMEM)]
        + [whole] * count
        + [pl.BlockSpec(memory_space=pl.ANY)] * pieces,
        out_specs=[whole] * out_count,
        scratch_shapes=scratch,
        compiler_params=pltpu.CompilerParams(vmem_limit_bytes=56 * 2**20),
        cost_estimate=pl.CostEstimate(flops=flops, bytes_accessed=moved, transcendentals=0),
    )(places_row, *arrays, *flat)


def f32(*shape):
    return jax.ShapeDtypeStruct(shape, jnp.float32)


def b16(*shape):
    return jax.ShapeDtypeStruct(shape, jnp.bfloat16)


def dot_nn(left, right):
    return jnp.dot(left, right, preferred_element_type=jnp.float32)


def dot_nt(left, right):
    return lax.dot_general(left, right, (((1,), (1,)), ((), ())), preferred_element_type=jnp.float32)


def dot_tn(left, right):
    return lax.dot_general(left, right, (((0,), (0,)), ((), ())), preferred_element_type=jnp.float32)


def spread_means(first, second, table, inv_count):
    rows = jnp.concatenate(
        [
            jnp.sum(first, axis=0, keepdims=True),
            jnp.sum(second, axis=0, keepdims=True),
            jnp.zeros((6, first.shape[1]), jnp.float32),
        ]
    )
    means = jnp.dot(rows, table, precision=HIGHEST, preferred_element_type=jnp.float32) * inv_count
    return (means[0:1], means[1:2])


def group_normed(field, valid, table, inv_count):
    kept = field * valid
    average, square = spread_means(kept, kept * field, table, inv_count)
    inv_std = lax.rsqrt(square - average * average + EPSILON)
    return ((field - average) * inv_std, inv_std)


def group_back(gradient, normed, inv_std, gain, valid, table, inv_count):
    scaled = gradient * gain * valid
    mean_one, mean_two = spread_means(scaled, scaled * normed, table, inv_count)
    return inv_std * (scaled - mean_one - normed * mean_two) * valid


def layer_normed(field):
    centred = field - jnp.mean(field, axis=1, keepdims=True)
    inv_std = lax.rsqrt(jnp.mean(centred * centred, axis=1, keepdims=True) + EPSILON)
    return (centred * inv_std, inv_std)


def layer_back(gradient, normed, inv_std, gain):
    scaled = gradient * gain
    mean_one = jnp.mean(scaled, axis=1, keepdims=True)
    mean_two = jnp.mean(scaled * normed, axis=1, keepdims=True)
    return inv_std * (scaled - mean_one - normed * mean_two)


def half_erf(field):
    return 0.5 + 0.5 * lax.erf(field * (0.5**0.5))


def gelu_slope(field, half):
    return half + field * (jnp.exp(-0.5 * field * field) * (1.0 / math.sqrt(2.0 * math.pi)))


def head_windows(channels):
    width = channels // HEADS
    windows = []
    for head in range(HEADS):
        start = head * width // 128 * 128
        stop = -(-(head + 1) * width // 128) * 128
        windows.append((start, stop, head * width - start, (head + 1) * width - start))
    return windows


def head_mask(window):
    start, stop, low, high = window
    lane = lax.broadcasted_iota(jnp.int32, (1, stop - start), 1)
    return ((lane >= low) & (lane < high)).astype(jnp.float32).astype(jnp.bfloat16)


def attend_into(query_ref, key_ref, value_ref, bias, out_ref, rows):
    channels = query_ref.shape[1]
    factor = (channels // HEADS) ** (-0.5) * math.log2(math.e)
    out_ref[rows, :] = jnp.zeros((query_ref[rows, :].shape[0], channels), jnp.float32)
    for window in head_windows(channels):
        lanes = slice(window[0], window[1])
        mask = head_mask(window)
        scores = dot_nt(query_ref[rows, lanes] * mask, key_ref[rows if bias.shape[0] > 1 else slice(None), lanes])
        scores = scores * factor + bias
        powers = jnp.exp2(scores - jnp.max(scores, axis=1, keepdims=True))
        inverse = 1.0 / jnp.sum(powers, axis=1, keepdims=True)
        values = value_ref[rows if bias.shape[0] > 1 else slice(None), lanes] * mask
        out_ref[rows, lanes] += dot_nn(to_low(powers), values) * inverse


def attend_back_into(query_ref, key_ref, value_ref, grad_ref, bias, outs, rows, key_rows):
    channels = query_ref.shape[1]
    scale = (channels // HEADS) ** (-0.5)
    factor = scale * math.log2(math.e)
    for number, out_ref in enumerate(outs):
        size = (rows if number == 0 else key_rows)
        out_ref[size, :] = jnp.zeros(
            ((query_ref if number == 0 else key_ref)[size, :].shape[0], channels), jnp.float32
        )
    for window in head_windows(channels):
        lanes = slice(window[0], window[1])
        mask = head_mask(window)
        queries = query_ref[rows, lanes] * mask
        keys = key_ref[key_rows, lanes] * mask
        grads = grad_ref[rows, lanes] * mask
        scores = dot_nt(keys, queries) * factor + bias
        powers = jnp.exp2(scores - jnp.max(scores, axis=0, keepdims=True))
        probs = powers * (1.0 / jnp.sum(powers, axis=0, keepdims=True))
        grad_probs = dot_nt(value_ref[key_rows, lanes], grads)
        inner = jnp.sum(probs * grad_probs, axis=0, keepdims=True)
        grad_scores = to_low(probs * (grad_probs - inner))
        outs[0][rows, lanes] += dot_tn(grad_scores, keys) * scale
        if len(outs) > 1:
            outs[1][key_rows, lanes] += dot_nn(grad_scores, queries) * scale
            outs[2][key_rows, lanes] += dot_nn(to_low(probs), grads)


ALL = slice(None)


def fill_taps(field, masks, pads, side):
    cells = field.shape[0]
    border = jnp.zeros((side, field.shape[1]), jnp.float32)
    left = pltpu.roll(field, 1, 0) * masks[:, 1:2]
    right = pltpu.roll(field, cells - 1, 0) * masks[:, 2:3]
    for number, moved in enumerate((left, field, right)):
        pads[number, :side, :] = border
        pads[number, side : side + cells, :] = moved
        pads[number, side + cells :, :] = border


def conv_forward(places_row, side, field, masks, vectors, table, weights, which, residual):
    cells, channels = field.shape

    def body(places_ref, ins, groups, outs, scratch):
        field_ref, masks_ref, vec_ref, table_ref = ins[:4]
        weight, pads, sem = scratch
        (out_ref,) = outs
        start_load(places_ref, groups[0], pl.ds(9 * which, 9), weight, sem.at[0])
        masks = masks_ref[...]
        valid = masks[:, 0:1]
        vec = vec_ref[...]
        normed, _ = group_normed(
            field_ref[...].astype(jnp.float32), valid, table_ref[...], vec[3:4]
        )
        pre = normed * vec[0:1] + vec[1:2]
        act = pre / (1.0 + jnp.exp(-pre)) * valid
        fill_taps(act, masks, pads, side)
        out_ref[...] = jnp.broadcast_to(vec[2:3], (cells, channels))
        if residual:
            out_ref[...] += field_resid(ins)
        finish_load(weight, sem.at[0])

        def row_tap(step, carry):
            rows = pl.ds(pl.multiple_of(step * side, 8), cells)
            total = out_ref[...]
            for col in range(3):
                total += dot_nn(to_low(pads[col, rows, :]), weight[step * 3 + col])
            out_ref[...] = total
            return carry

        lax.fori_loop(0, 3, row_tap, 0)

    def field_resid(ins):
        return ins[4][...].astype(jnp.float32)

    arrays = [field, masks, vectors, table] + ([residual[0]] if residual else [])
    return run_kernel(
        body,
        places_row,
        arrays,
        [(weights,)],
        [f32(cells, channels)],
        [
            pltpu.VMEM((9, channels, channels), jnp.bfloat16),
            pltpu.VMEM((3, cells + 2 * side, channels), jnp.float32),
            pltpu.SemaphoreType.DMA((1,)),
        ],
        18 * cells * channels * channels,
    )[0]


def conv_backward(places_row, side, gradient, field, masks, vectors, table, weights, which, extra):
    cells, channels = field.shape

    def body(places_ref, ins, groups, outs, scratch):
        grad_ref, field_ref, masks_ref, vec_ref, table_ref = ins[:5]
        weight, pads, total_ref, sem = scratch
        (out_ref,) = outs
        start_load(places_ref, groups[0], pl.ds(9 * which, 9), weight, sem.at[0])
        masks = masks_ref[...]
        valid = masks[:, 0:1]
        vec = vec_ref[...]
        fill_taps(grad_ref[...], masks, pads, side)
        total_ref[...] = jnp.zeros((cells, channels), jnp.float32)
        finish_load(weight, sem.at[0])

        def row_tap(step, carry):
            rows = pl.ds(pl.multiple_of(step * side, 8), cells)
            total = total_ref[...]
            for col in range(3):
                total += dot_nt(to_low(pads[col, rows, :]), weight[8 - (step * 3 + col)])
            total_ref[...] = total
            return carry

        lax.fori_loop(0, 3, row_tap, 0)
        normed, inv_std = group_normed(
            field_ref[...].astype(jnp.float32), valid, table_ref[...], vec[3:4]
        )
        pre = normed * vec[0:1] + vec[1:2]
        gate = 1.0 / (1.0 + jnp.exp(-pre))
        grad_pre = total_ref[...] * (gate * (1.0 + pre * (1.0 - gate)))
        result = group_back(
            grad_pre, normed, inv_std, vec[0:1], valid, table_ref[...], vec[3:4]
        )
        if extra:
            result += ins[5][...]
        out_ref[...] = result

    return run_kernel(
        body,
        places_row,
        [gradient, field, masks, vectors, table] + list(extra),
        [(weights,)],
        [f32(cells, channels)],
        [
            pltpu.VMEM((9, channels, channels), jnp.bfloat16),
            pltpu.VMEM((3, cells + 2 * side, channels), jnp.float32),
            pltpu.VMEM((cells, channels), jnp.float32),
            pltpu.SemaphoreType.DMA((1,)),
        ],
        18 * cells * channels * channels,
    )[0]


def self_forward(places_row, resid, masks, bias, vectors, table, proj, attn):
    cells, channels = resid.shape
    needed = (0, 2, 3, 4, 5)

    def body(places_ref, ins, groups, outs, scratch):
        resid_ref, masks_ref, bias_ref, vec_ref, table_ref = ins
        proj_ref, query_ref, key_ref, value_ref, two_ref = outs
        weight, att, sem = scratch
        for slot, lead in enumerate(needed):
            pair_load(places_ref, groups, lead, weight.at[slot], sem.at[slot])
        vec = vec_ref[...]
        normed, _ = group_normed(resid_ref[...], masks_ref[:, 0:1], table_ref[...], vec[7:8])
        low = to_low(normed * vec[0:1] + vec[1:2])
        finish_load(weight.at[0], sem.at[0])
        entered = dot_nn(low, weight[0]) + vec[2:3]
        proj_ref[...] = entered
        normed, _ = layer_normed(entered)
        low = to_low(normed * vec[3:4] + vec[4:5])
        for slot, out_ref in ((1, query_ref), (2, key_ref), (3, value_ref)):
            finish_load(weight.at[slot], sem.at[slot])
            out_ref[...] = to_low(dot_nn(low, weight[slot]))
        attend_into(query_ref, key_ref, value_ref, bias_ref[0:1, :], att, ALL)
        finish_load(weight.at[4], sem.at[4])
        two_ref[...] = proj_ref[...] + dot_nn(to_low(att[...]), weight[4]) + vec[5:6]

    return run_kernel(
        body,
        places_row,
        [resid, masks, bias, vectors, table],
        [(proj,), (attn,)],
        [f32(cells, channels)] + [b16(cells, channels)] * 3 + [f32(cells, channels)],
        [
            pltpu.VMEM((5, channels, channels), jnp.bfloat16),
            pltpu.VMEM((cells, channels), jnp.float32),
            pltpu.SemaphoreType.DMA((5,)),
        ],
        10 * cells * channels * channels + 4 * cells * cells * channels,
    )


def self_backward(places_row, grad_two, proj_one, query, key, value, resid, grad_st, masks, vectors, table, proj, attn):
    cells, channels = resid.shape
    needed = (5, 2, 3, 4, 0)

    def body(places_ref, ins, groups, outs, scratch):
        grad_ref, proj_ref, query_ref, key_ref, value_ref, resid_ref, st_ref, masks_ref, vec_ref, table_ref = ins
        (out_ref,) = outs
        weight, grad_att, grad_q, grad_k, grad_v, sem = scratch
        for slot, lead in enumerate(needed):
            pair_load(places_ref, groups, lead, weight.at[slot], sem.at[slot])
        vec = vec_ref[...]
        valid = masks_ref[:, 0:1]
        finish_load(weight.at[0], sem.at[0])
        grad_att[...] = to_low(dot_nt(to_low(grad_ref[...]), weight[0]))
        attend_back_into(
            query_ref, key_ref, value_ref, grad_att, (valid - 1.0) * -FAR,
            (grad_q, grad_k, grad_v), ALL, ALL,
        )
        total = None
        for slot, member in ((1, grad_q), (2, grad_k), (3, grad_v)):
            finish_load(weight.at[slot], sem.at[slot])
            part = dot_nt(to_low(member[...]), weight[slot])
            total = part if total is None else total + part
        normed, inv_std = layer_normed(proj_ref[...])
        grad_one = grad_ref[...] + layer_back(total, normed, inv_std, vec[3:4])
        finish_load(weight.at[4], sem.at[4])
        grad_gn = dot_nt(to_low(grad_one), weight[4])
        normed, inv_std = group_normed(resid_ref[...], valid, table_ref[...], vec[7:8])
        out_ref[...] = st_ref[...] + group_back(
            grad_gn, normed, inv_std, vec[0:1], valid, table_ref[...], vec[7:8]
        )

    return run_kernel(
        body,
        places_row,
        [grad_two, proj_one, query, key, value, resid, grad_st, masks, vectors, table],
        [(proj,), (attn,)],
        [f32(cells, channels)],
        [
            pltpu.VMEM((5, channels, channels), jnp.bfloat16),
            pltpu.VMEM((cells, channels), jnp.bfloat16),
            pltpu.VMEM((cells, channels), jnp.float32),
            pltpu.VMEM((cells, channels), jnp.float32),
            pltpu.VMEM((cells, channels), jnp.float32),
            pltpu.SemaphoreType.DMA((5,)),
        ],
        10 * cells * channels * channels + 10 * cells * cells * channels,
    )[0]


CHUNK = 512


def cross_forward(places_row, two, resid, context, masks, bias, vectors, wide_bias, table, proj, attn, cross, w_in_all, w_out_all):
    cells, channels = resid.shape
    prompt, width = context.shape

    def body(places_ref, ins, groups, outs, scratch):
        two_ref, resid_ref, context_ref, masks_ref, bias_ref, vec_ref, wide_ref, table_ref = ins
        query_ref, key_ref, value_ref, three_ref, out_ref, motion_ref = outs
        weight, kv, w_in, w_out, att, total, sem = scratch
        for slot, lead in enumerate((6, 7, 1)):
            pair_load(places_ref, groups, lead, weight.at[slot], sem.at[slot])
        for slot in range(2):
            start_load(places_ref, groups[2], slot, kv.at[slot], sem.at[3 + slot])
        start_load(places_ref, groups[3], None, w_in, sem.at[5])
        start_load(places_ref, groups[4], None, w_out, sem.at[6])
        vec = vec_ref[...]
        normed, _ = layer_normed(two_ref[...])
        low = to_low(normed * vec[0:1] + vec[1:2])
        finish_load(weight.at[0], sem.at[0])
        query_ref[...] = to_low(dot_nn(low, weight[0]))
        for slot, ref in ((0, key_ref), (1, value_ref)):
            finish_load(kv.at[slot], sem.at[3 + slot])
            ref[...] = to_low(dot_nn(context_ref[...], kv[slot]))
        attend_into(query_ref, key_ref, value_ref, bias_ref[0:1, :], att, ALL)
        finish_load(weight.at[1], sem.at[1])
        three_ref[...] = two_ref[...] + dot_nn(to_low(att[...]), weight[1]) + vec[2:3]
        normed, _ = layer_normed(three_ref[...])
        low = to_low(normed * vec[3:4] + vec[4:5])
        finish_load(w_in, sem.at[5])
        finish_load(w_out, sem.at[6])
        total[...] = three_ref[...] + vec[5:6]

        def chunk(step, carry):
            lanes = pl.ds(pl.multiple_of(step * CHUNK, 128), CHUNK)
            gates = pl.ds(pl.multiple_of(FF_ST + step * CHUNK, 128), CHUNK)
            hidden = dot_nn(low_ref(att), w_in[:, lanes]) + wide_ref[0:1, lanes]
            gate = dot_nn(low_ref(att), w_in[:, gates]) + wide_ref[0:1, gates]
            act = to_low(hidden * (gate * half_erf(gate)))
            total[...] += dot_nn(act, w_out[lanes, :])
            return carry

        def low_ref(ref):
            return to_low(ref[...])

        att[...] = low.astype(jnp.float32)
        lax.fori_loop(0, FF_ST // CHUNK, chunk, 0)
        finish_load(weight.at[2], sem.at[2])
        st_out = dot_nn(to_low(total[...]), weight[2]) + vec[6:7] + resid_ref[...]
        out_ref[...] = st_out
        normed, _ = group_normed(st_out, masks_ref[:, 0:1], table_ref[...], vec[9:10])
        motion_ref[...] = to_low(normed * vec[7:8] + vec[8:9])

    return run_kernel(
        body,
        places_row,
        [two, resid, context, masks, bias, vectors, wide_bias, table],
        [(proj,), (attn,), (cross,), (w_in_all,), (w_out_all,)],
        [
            b16(cells, channels),
            b16(prompt, channels),
            b16(prompt, channels),
            f32(cells, channels),
            f32(cells, channels),
            b16(cells, channels),
        ],
        [
            pltpu.VMEM((3, channels, channels), jnp.bfloat16),
            pltpu.VMEM((2, width, channels), jnp.bfloat16),
            pltpu.VMEM((channels, 2 * FF_ST), jnp.bfloat16),
            pltpu.VMEM((FF_ST, channels), jnp.bfloat16),
            pltpu.VMEM((cells, channels), jnp.float32),
            pltpu.VMEM((cells, channels), jnp.float32),
            pltpu.SemaphoreType.DMA((7,)),
        ],
        2 * cells * channels * (3 * channels + 3 * FF_ST),
    )


def cross_backward(places_row, grad_gn, grad_out, st_out, three, two, query, key, value, masks, bias_col, vectors, wide_bias, table, proj, attn, w_in_all, w_out_all):
    cells, channels = st_out.shape
    prompt = key.shape[0]

    def body(places_ref, ins, groups, outs, scratch):
        gn_ref, cot_ref, st_ref, three_ref, two_ref, query_ref, key_ref, value_ref, masks_ref, bias_ref, vec_ref, wide_ref, table_ref = ins
        grad_two_ref, grad_st_ref, small_ref = outs
        weight, w_in, w_out, low, grad_low, total, grad_att, grad_q, sem = scratch
        pair_load(places_ref, groups, 1, weight.at[0], sem.at[0])
        start_load(places_ref, groups[3], None, w_out, sem.at[4])
        start_load(places_ref, groups[2], None, w_in, sem.at[3])
        pair_load(places_ref, groups, 7, weight.at[1], sem.at[1])
        pair_load(places_ref, groups, 6, weight.at[2], sem.at[2])
        vec = vec_ref[...]
        valid = masks_ref[:, 0:1]
        grad_motion = gn_ref[...].astype(jnp.float32)
        normed, inv_std = group_normed(st_ref[...], valid, table_ref[...], vec[9:10])
        small_ref[...] = jnp.concatenate(
            [
                jnp.sum(grad_motion * normed, axis=0, keepdims=True),
                jnp.sum(grad_motion, axis=0, keepdims=True),
                jnp.zeros((6, channels), jnp.float32),
            ]
        )
        grad_st_ref[...] = cot_ref[...].astype(jnp.float32) + group_back(
            grad_motion, normed, inv_std, vec[7:8], valid, table_ref[...], vec[9:10]
        )
        finish_load(weight.at[0], sem.at[0])
        grad_two_ref[...] = dot_nt(to_low(grad_st_ref[...]), weight[0])
        grad_low[...] = to_low(grad_two_ref[...])
        normed, inv_std = layer_normed(three_ref[...])
        low[...] = to_low(normed * vec[3:4] + vec[4:5])
        total[...] = jnp.zeros((cells, channels), jnp.float32)
        finish_load(w_out, sem.at[4])
        finish_load(w_in, sem.at[3])

        def chunk(step, carry):
            lanes = pl.ds(pl.multiple_of(step * CHUNK, 128), CHUNK)
            gates = pl.ds(pl.multiple_of(FF_ST + step * CHUNK, 128), CHUNK)
            hidden = dot_nn(low[...], w_in[:, lanes]) + wide_ref[0:1, lanes]
            gate = dot_nn(low[...], w_in[:, gates]) + wide_ref[0:1, gates]
            grad_act = dot_nt(grad_low[...], w_out[lanes, :])
            half = half_erf(gate)
            grad_hidden = to_low(grad_act * (gate * half))
            grad_gate = to_low(grad_act * hidden * gelu_slope(gate, half))
            total[...] += dot_nt(grad_hidden, w_in[:, lanes]) + dot_nt(grad_gate, w_in[:, gates])
            return carry

        lax.fori_loop(0, FF_ST // CHUNK, chunk, 0)
        normed, inv_std = layer_normed(three_ref[...])
        grad_two_ref[...] += layer_back(total[...], normed, inv_std, vec[3:4])
        finish_load(weight.at[1], sem.at[1])
        grad_att[...] = to_low(dot_nt(to_low(grad_two_ref[...]), weight[1]))
        attend_back_into(
            query_ref, key_ref, value_ref, grad_att, bias_ref[:, 0:1], (grad_q,), ALL, ALL
        )
        finish_load(weight.at[2], sem.at[2])
        grad_ln = dot_nt(to_low(grad_q[...]), weight[2])
        normed, inv_std = layer_normed(two_ref[...])
        grad_two_ref[...] += layer_back(grad_ln, normed, inv_std, vec[0:1])

    return run_kernel(
        body,
        places_row,
        [grad_gn, grad_out, st_out, three, two, query, key, value, masks, bias_col, vectors, wide_bias, table],
        [(proj,), (attn,), (w_in_all,), (w_out_all,)],
        [f32(cells, channels), f32(cells, channels), f32(8, channels)],
        [
            pltpu.VMEM((3, channels, channels), jnp.bfloat16),
            pltpu.VMEM((channels, 2 * FF_ST), jnp.bfloat16),
            pltpu.VMEM((FF_ST, channels), jnp.bfloat16),
            pltpu.VMEM((cells, channels), jnp.bfloat16),
            pltpu.VMEM((cells, channels), jnp.bfloat16),
            pltpu.VMEM((cells, channels), jnp.float32),
            pltpu.VMEM((cells, channels), jnp.bfloat16),
            pltpu.VMEM((cells, channels), jnp.float32),
            pltpu.SemaphoreType.DMA((5,)),
        ],
        2 * cells * channels * (3 * channels + 6 * FF_ST),
    )


def group_rows(step, group_len):
    return pl.ds(pl.multiple_of(step * group_len, 16), group_len)


def motion_forward(places_row, motion_in, position, bias, vectors, proj, attn):
    tokens, channels = motion_in.shape
    group_len = bias.shape[0]

    def body(places_ref, ins, groups, outs, scratch):
        in_ref, pos_ref, bias_ref, vec_ref = ins
        weight, att, sem = scratch
        for slot, lead in enumerate((0, 2, 3, 4, 5, 6, 7, 8, 9)):
            pair_load(places_ref, groups, lead, weight.at[slot], sem.at[slot])
        vec = vec_ref[...]
        finish_load(weight.at[0], sem.at[0])
        outs[0][...] = dot_nn(in_ref[...], weight[0]) + vec[0:1]
        for block in range(2):
            zed_ref, next_ref = outs[block], outs[block + 1]
            qkv = outs[3 + 4 * block : 6 + 4 * block]
            time_ref = outs[6 + 4 * block]
            normed, _ = layer_normed(zed_ref[...])
            low = to_low(normed * vec[1 + 3 * block : 2 + 3 * block] + vec[2 + 3 * block : 3 + 3 * block] + pos_ref[...])
            for which in range(3):
                slot = 1 + 4 * block + which
                finish_load(weight.at[slot], sem.at[slot])
                qkv[which][...] = to_low(dot_nn(low, weight[slot]))

            def group(step, carry):
                attend_into(*qkv, bias_ref[...], att, group_rows(step, group_len))
                return carry

            lax.fori_loop(0, tokens // group_len, group, 0)
            time_ref[...] = to_low(att[...])
            slot = 4 + 4 * block
            finish_load(weight.at[slot], sem.at[slot])
            next_ref[...] = zed_ref[...] + dot_nn(time_ref[...], weight[slot]) + vec[3 + 3 * block : 4 + 3 * block]

    return run_kernel(
        body,
        places_row,
        [motion_in, position, bias, vectors],
        [proj, attn],
        [f32(tokens, channels)] * 3 + [b16(tokens, channels)] * 8,
        [
            pltpu.VMEM((9, channels, channels), jnp.bfloat16),
            pltpu.VMEM((tokens, channels), jnp.float32),
            pltpu.SemaphoreType.DMA((9,)),
        ],
        18 * tokens * channels * channels,
    )


def motion_ff(places_row, zed, st_columns, cotangent, vectors, wide_bias, proj, in_pieces, out_pieces):
    tokens, channels = zed.shape
    hidden_width = wide_bias.shape[1]

    def body(places_ref, ins, groups, outs, scratch):
        zed_ref, st_ref, cot_ref, vec_ref, wide_ref = ins
        out_ref, grad_ref, d_proj, d_in, d_out, small_ref, wide_out = outs
        weight, w_in, w_out, pre, low, grad_low, total, sem = scratch
        start_load(places_ref, groups[1], None, w_in, sem.at[0])
        start_load(places_ref, groups[2], None, w_out, sem.at[1])
        start_load(places_ref, groups[0], 1, weight, sem.at[2])
        vec = vec_ref[...]
        normed, inv_std = layer_normed(zed_ref[...])
        low[...] = to_low(normed * vec[0:1] + vec[1:2])
        total[...] = zed_ref[...] + vec[2:3]
        finish_load(w_in, sem.at[0])
        finish_load(w_out, sem.at[1])

        def forward(step, carry):
            lanes = pl.ds(pl.multiple_of(step * CHUNK, 128), CHUNK)
            before = dot_nn(low[...], w_in[:, lanes]) + wide_ref[0:1, lanes]
            pre[:, lanes] = before
            total[...] += dot_nn(to_low(before * half_erf(before)), w_out[lanes, :])
            return carry

        lax.fori_loop(0, hidden_width // CHUNK, forward, 0)
        finish_load(weight, sem.at[2])
        zed_low = to_low(total[...])
        out_ref[...] = to_low(st_ref[...].astype(jnp.float32) + dot_nn(zed_low, weight[...]) + vec[3:4])
        d_proj[...] = to_low(dot_tn(zed_low, cot_ref[...]))
        grad_ref[...] = dot_nt(cot_ref[...], weight[...])
        grad_low[...] = to_low(grad_ref[...])
        total[...] = jnp.zeros((tokens, channels), jnp.float32)

        def backward(step, carry):
            lanes = pl.ds(pl.multiple_of(step * CHUNK, 128), CHUNK)
            before = pre[:, lanes]
            half = half_erf(before)
            d_out[lanes, :] = to_low(dot_tn(to_low(before * half), grad_low[...]))
            grad_pre = dot_nt(grad_low[...], w_out[lanes, :]) * gelu_slope(before, half)
            wide_out[0:1, lanes] = jnp.sum(grad_pre, axis=0, keepdims=True)
            pre_low = to_low(grad_pre)
            d_in[:, lanes] = to_low(dot_tn(low[...], pre_low))
            total[...] += dot_nt(pre_low, w_in[:, lanes])
            return carry

        wide_out[...] = jnp.zeros((8, hidden_width), jnp.float32)
        lax.fori_loop(0, hidden_width // CHUNK, backward, 0)
        normed, inv_std = layer_normed(zed_ref[...])
        grad_ln = total[...]
        small_ref[...] = jnp.concatenate(
            [
                jnp.sum(cot_ref[...].astype(jnp.float32), axis=0, keepdims=True),
                jnp.sum(grad_ref[...], axis=0, keepdims=True),
                jnp.sum(grad_ln * normed, axis=0, keepdims=True),
                jnp.sum(grad_ln, axis=0, keepdims=True),
                jnp.zeros((4, channels), jnp.float32),
            ]
        )
        grad_ref[...] += layer_back(grad_ln, normed, inv_std, vec[0:1])

    return run_kernel(
        body,
        places_row,
        [zed, st_columns, cotangent, vectors, wide_bias],
        [proj, in_pieces, out_pieces],
        [
            b16(tokens, channels),
            f32(tokens, channels),
            b16(channels, channels),
            b16(channels, hidden_width),
            b16(hidden_width, channels),
            f32(8, channels),
            f32(8, hidden_width),
        ],
        [
            pltpu.VMEM((channels, channels), jnp.bfloat16),
            pltpu.VMEM((channels, hidden_width), jnp.bfloat16),
            pltpu.VMEM((hidden_width, channels), jnp.bfloat16),
            pltpu.VMEM((tokens, hidden_width), jnp.float32),
            pltpu.VMEM((tokens, channels), jnp.bfloat16),
            pltpu.VMEM((tokens, channels), jnp.bfloat16),
            pltpu.VMEM((tokens, channels), jnp.float32),
            pltpu.SemaphoreType.DMA((3,)),
        ],
        12 * tokens * channels * hidden_width,
    )


def motion_back(places_row, block, grad_zed, zed, query, key, value, time_out, motion_in, position, bias, vectors, proj, attn):
    tokens, channels = zed.shape
    group_len = bias.shape[0]
    leads = [5 + 4 * block, 2 + 4 * block, 3 + 4 * block, 4 + 4 * block] + ([0] if motion_in is not None else [])
    last = motion_in is not None

    def body(places_ref, ins, groups, outs, scratch):
        grad_ref, zed_ref, query_ref, key_ref, value_ref, time_ref, pos_ref, bias_ref, vec_ref = ins[:9]
        out_ref, d_query, d_key, d_value, d_output, small_ref = outs[:6]
        weight, grad_att, grad_q, grad_k, grad_v, sem = scratch
        for slot, lead in enumerate(leads):
            pair_load(places_ref, groups, lead, weight.at[slot], sem.at[slot])
        vec = vec_ref[...]
        grad_low = to_low(grad_ref[...])
        d_output[...] = to_low(dot_tn(time_ref[...], grad_low))
        finish_load(weight.at[0], sem.at[0])
        grad_att[...] = to_low(dot_nt(grad_low, weight[0]))

        def group(step, carry):
            rows = group_rows(step, group_len)
            attend_back_into(
                query_ref, key_ref, value_ref, grad_att, bias_ref[...], (grad_q, grad_k, grad_v), rows, rows
            )
            return carry

        lax.fori_loop(0, tokens // group_len, group, 0)
        normed, inv_std = layer_normed(zed_ref[...])
        low = to_low(normed * vec[0:1] + vec[1:2] + pos_ref[...])
        grad_ln = None
        for slot, member, d_ref in ((1, grad_q, d_query), (2, grad_k, d_key), (3, grad_v, d_value)):
            member_low = to_low(member[...])
            d_ref[...] = to_low(dot_tn(low, member_low))
            finish_load(weight.at[slot], sem.at[slot])
            part = dot_nt(member_low, weight[slot])
            grad_ln = part if grad_ln is None else grad_ln + part
        total = grad_ref[...] + layer_back(grad_ln, normed, inv_std, vec[0:1])
        small_ref[...] = jnp.concatenate(
            [
                jnp.sum(grad_ref[...], axis=0, keepdims=True),
                jnp.sum(grad_ln * normed, axis=0, keepdims=True),
                jnp.sum(grad_ln, axis=0, keepdims=True),
                jnp.sum(total, axis=0, keepdims=True),
                jnp.zeros((4, channels), jnp.float32),
            ]
        )
        if last:
            total_low = to_low(total)
            outs[6][...] = to_low(dot_tn(ins[9][...], total_low))
            finish_load(weight.at[4], sem.at[4])
            out_ref[...] = to_low(dot_nt(total_low, weight[4]))
        else:
            out_ref[...] = total

    arrays = [grad_zed, zed, query, key, value, time_out, position, bias, vectors]
    outs = [b16(tokens, channels) if last else f32(tokens, channels)] + [b16(channels, channels)] * 4 + [f32(8, channels)]
    if last:
        arrays.append(motion_in)
        outs.append(b16(channels, channels))
    return run_kernel(
        body,
        places_row,
        arrays,
        [proj, attn],
        outs,
        [
            pltpu.VMEM((len(leads), channels, channels), jnp.bfloat16),
            pltpu.VMEM((tokens, channels), jnp.bfloat16),
            pltpu.VMEM((tokens, channels), jnp.float32),
            pltpu.VMEM((tokens, channels), jnp.float32),
            pltpu.VMEM((tokens, channels), jnp.float32),
            pltpu.SemaphoreType.DMA((len(leads),)),
        ],
        18 * tokens * channels * channels,
    )


def part_rows(count, turn):
    units = count // 16
    sizes = [units // 3 + (1 if (part - turn) % 3 < units % 3 else 0) for part in range(3)]
    starts = [16 * sum(sizes[:part]) for part in range(3)]
    return [(start, 16 * size) for start, size in zip(starts, sizes)]


def gather_plan(shards):
    plan = []
    for number, (shape, pieces) in enumerate(shards):
        if len(shape) == 2:
            plan.append((number, None, None, part_rows(shape[0], len(plan))))
            continue
        step = shape[0] // pieces
        for piece in range(pieces):
            if step % 3 == 0:
                third = step // 3
                parts = [(piece * step + part * third, third) for part in range(3)]
                plan.append((number, "lead", None, parts))
            else:
                plan.append((number, "rows", (piece * step, step), part_rows(shape[1], len(plan))))
    return plan


def gather_all(shards, small, carried):
    arrays = [array for array, _ in shards]
    plan = gather_plan([(array.shape, pieces) for array, pieces in shards])
    frames = lax.axis_size("frame")
    count, extra = len(arrays), len(carried)
    steps = len(plan)
    roles = ((0, 1, 2), (1, 0, 2), (2, 1, 0), (2, 0, 1))

    def kernel(*refs):
        sources, small_ref = refs[:count], refs[count]
        carried_in = refs[count + 1 : count + 1 + extra]
        base = count + 1 + extra
        targets, small_out = refs[base : base + count], refs[base + count]
        near_out = refs[base + count + 1 : base + count + 1 + extra]
        half_out = refs[base + count + 1 + extra : base + count + 1 + 2 * extra]
        send, recv, small_send, small_recv, near_send, near_recv, own_sem, half_sem = refs[
            base + count + 1 + 2 * extra :
        ]
        frame, row = lax.axis_index("frame"), lax.axis_index("rows")
        frame_bit, core_bit = frame // 2, frame % 2
        across = (1 - frame_bit) * 2 + core_bit
        beside = frame_bit * 2 + 1 - core_bit
        corner = (1 - frame_bit) * 2 + 1 - core_bit
        x_bit, z_bit = row % 2, row // 2 % 2
        over_x = row + 1 - 2 * x_bit
        over_z = row + 2 - 4 * z_bit
        over = {
            "y": (across, row),
            "core": (beside, row),
            "corner": (corner, row),
            "x": (frame, over_x),
            "z": (frame, over_z),
        }
        barrier = pltpu.get_barrier_semaphore()
        for place in over.values():
            pl.semaphore_signal(barrier, inc=1, device_id=place, device_id_type=MESH)
        pl.semaphore_wait(barrier, len(over))

        def view(ref, step, part, shard):
            number, kind, leads, parts = plan[step]
            rows = arrays[number].shape[-2]
            begin = 0 if shard is None else pl.multiple_of(shard * rows, 16)
            if kind == "lead":
                first, size = parts[0][0], sum(length for _, length in parts)
                if part is not None:
                    first, size = parts[part]
                where = pl.ds(first, size)
                return ref.at[where] if shard is None else ref.at[where, pl.ds(begin, rows)]
            start, size = (0, rows) if part is None else parts[part]
            where = pl.ds(begin + start, size)
            if kind is None:
                return ref.at[where]
            return ref.at[pl.ds(*leads), where]

        def move(step, part, shard, source, target, way, slot):
            number = plan[step][0]
            return pltpu.make_async_remote_copy(
                src_ref=source,
                dst_ref=view(targets[number], step, part, shard),
                send_sem=send.at[step, slot],
                recv_sem=recv.at[step, slot],
                device_id=over[way],
                device_id_type=MESH,
            )

        own = [
            pltpu.make_async_copy(
                view(sources[plan[step][0]], step, None, None),
                view(targets[plan[step][0]], step, None, frame),
                own_sem.at[step],
            )
            for step in range(steps)
        ]
        smalls = [
            pltpu.make_async_remote_copy(
                src_ref=small_ref,
                dst_ref=small_out.at[frame],
                send_sem=small_send.at[slot],
                recv_sem=small_recv.at[slot],
                device_id=over[way],
                device_id_type=MESH,
            )
            for slot, way in enumerate(("y", "core", "corner"))
        ]
        small_own = pltpu.make_async_copy(small_ref, small_out.at[frame], half_sem.at[extra])
        nears = [
            pltpu.make_async_remote_copy(
                src_ref=carried_in[number],
                dst_ref=near_out[number],
                send_sem=near_send.at[number],
                recv_sem=near_recv.at[number],
                device_id=over["core"],
                device_id_type=MESH,
            )
            for number in range(extra)
        ]
        halves = []
        for number, array in enumerate(carried):
            half = array.shape[-2] // 2
            where = pl.ds(pl.multiple_of(x_bit * half, 16), half)
            source = carried_in[number]
            source = source.at[where] if array.ndim == 2 else source.at[:, where]
            halves.append(pltpu.make_async_copy(source, half_out[number], half_sem.at[number]))

        def run(role):
            part_y, part_x, part_z = roles[role]
            forward = role >= 2

            def first(step):
                number = plan[step][0]
                return [
                    move(step, part_y, frame, view(sources[number], step, part_y, None), None, "y", 0),
                    move(step, None, frame, view(sources[number], step, None, None), None, "core", 3),
                ]

            def passed(step, part, way, slot):
                number = plan[step][0]
                return move(
                    step, part, across, view(targets[number], step, part, across), None, way, slot
                )

            started = [first(step) for step in range(steps)]
            for step in range(steps):
                started[step][0].start()
            for copy in smalls:
                copy.start()
            small_own.start()
            for step in range(steps):
                started[step][1].start()
                own[step].start()
            for copy in nears + halves:
                copy.start()
            later = []
            for turn in range(steps + 2):
                if turn < steps:
                    started[turn][0].wait_recv()
                    sends = [passed(turn, part_y, "z", 2), passed(turn, part_y, "core", 4)]
                    if not forward:
                        sends.insert(1, passed(turn, part_y, "x", 1))
                    for copy in sends:
                        copy.start()
                    later.append(sends)
                if 1 <= turn <= steps:
                    step = turn - 1
                    arrival = passed(step, part_z, "z", 2)
                    arrival.wait_recv()
                    sends = [passed(step, part_z, "core", 6)]
                    if forward:
                        sends.insert(0, passed(step, part_z, "x", 1))
                    for copy in sends:
                        copy.start()
                    later.append(sends)
                if turn >= 2:
                    step = turn - 2
                    arrival = passed(step, part_x, "x", 1)
                    arrival.wait_recv()
                    sends = [passed(step, part_x, "core", 5)]
                    for copy in sends:
                        copy.start()
                    later.append(sends)
            for step in range(steps):
                for copy in started[step]:
                    copy.wait_send()
                move(step, None, frame, view(sources[plan[step][0]], step, None, None), None, "core", 3).wait_recv()
                for part, slot in ((part_y, 4), (part_x, 5), (part_z, 6)):
                    passed(step, part, "core", slot).wait_recv()
                own[step].wait()
            for sends in later:
                for copy in sends:
                    copy.wait_send()
            for copy in smalls + nears:
                copy.wait()
            for copy in halves + [small_own]:
                copy.wait()

        for role in range(4):
            pl.when((z_bit == role // 2) & (x_bit == role % 2))(functools.partial(run, role))

    anywhere = pl.BlockSpec(memory_space=pl.ANY)
    outs = [
        b16(*array.shape[:-2], array.shape[-2] * frames, array.shape[-1]) for array in arrays
    ]
    outs.append(jax.ShapeDtypeStruct((frames,) + small.shape, small.dtype))
    outs += [b16(*array.shape) for array in carried]
    outs += [b16(*array.shape[:-2], array.shape[-2] // 2, array.shape[-1]) for array in carried]
    dma = pltpu.SemaphoreType.DMA
    results = pl.pallas_call(
        kernel,
        out_shape=outs,
        in_specs=[anywhere] * (count + 1 + extra),
        out_specs=[anywhere] * len(outs),
        scratch_shapes=[
            dma((steps, 7)),
            dma((steps, 7)),
            dma((3,)),
            dma((3,)),
            dma((extra,)),
            dma((extra,)),
            dma((steps,)),
            dma((extra + 1,)),
        ],
        compiler_params=pltpu.CompilerParams(collective_id=0, has_side_effects=True),
        cost_estimate=pl.CostEstimate(
            flops=0, bytes_accessed=200 * 2**20, transcendentals=0
        ),
    )(*arrays, small, *carried)
    return (
        results[:count],
        results[count],
        results[count + 1 : count + 1 + extra],
        results[count + 1 + extra :],
    )


def stack_rows(rows):
    filler = [jnp.zeros_like(rows[0])] * (-len(rows) % 8)
    return jnp.stack(list(rows) + filler)


def on_device(
    latents,
    cotangent,
    timesteps,
    prompt_ids,
    embed_table,
    res_gain,
    res_shift,
    res_conv,
    temb_weight,
    st_gain,
    st_shift,
    st_proj,
    st_attn,
    st_cross_kv,
    st_ff_in,
    st_ff_bias,
    st_ff_out,
    motion_gain,
    motion_shift,
    motion_proj,
    motion_attn,
    motion_ff_in,
    motion_ff_bias,
    motion_ff_out,
):
    frames_here, cell_count, channels = latents.shape
    places = Places(frames_here, channels)
    side = places.side
    cells = side * side
    valid = places.valid.astype(jnp.float32)
    table = group_table(channels)
    count = (places.safe_side * places.safe_side * (channels // GROUPS)).astype(jnp.float32)
    inv_count = jnp.broadcast_to(1.0 / count, (channels,))
    lanes = jnp.arange(128, dtype=jnp.int32)[None, :]
    masks = jnp.where(
        lanes == 0,
        valid[:, None],
        jnp.where(lanes == 1, places.cell_col[:, None] > 0, places.cell_col[:, None] < side - 1),
    ).astype(jnp.float32)
    key_bias = jnp.broadcast_to(((valid - 1.0) * -FAR)[None, :], (8, cells))
    places_row = piece_places()

    own = channels // places.frames
    clip_count, prompt_count = prompt_ids.shape
    own_temb = TEMB // places.frames
    time_low = to_low(jax.nn.silu(time_table(timesteps)))
    time_mine = lax.dynamic_slice_in_dim(time_low, places.frame * own_temb, own_temb, 1)
    time_part = matmul(time_mine, temb_weight)
    small = jnp.concatenate(
        [
            motion_gain.astype(jnp.float32),
            motion_shift.astype(jnp.float32),
            motion_ff_bias.astype(jnp.float32).reshape(-1, own),
            time_part.reshape(-1, own),
        ]
    )
    small_count = small.shape[0]
    small = jnp.pad(small, ((0, -small_count % 8), (0, -own % 128)))
    flat_attn = motion_attn.reshape((-1,) + motion_attn.shape[2:])
    carried = [motion_proj, flat_attn, motion_ff_in, motion_ff_out]
    whole, small_all, near, half = gather_all(
        [
            (res_conv.reshape((-1,) + res_conv.shape[3:]), 2),
            (st_proj, 1),
            (st_attn, 1),
            (st_cross_kv, 1),
            (st_ff_in, 1),
            (st_ff_out, 1),
        ],
        small,
        carried,
    )
    conv_all, sproj_all, sattn_all, cross_all, sffin_all, sffout_all = whole
    mproj_pieces, mattn_pieces, mffin_pieces, mffout_pieces = (
        exchange_pieces(*triple) for triple in zip(carried, near, half)
    )
    small_all = small_all[:, :small_count, :own]

    def gathered_rows(first, last):
        rows = jnp.transpose(small_all[:, first:last], (1, 0, 2))
        return rows.reshape(last - first, channels)

    bias_rows = motion_ff_bias.shape[0] // own
    mgain, mshift = (gathered_rows(0, 4), gathered_rows(4, 13))
    mffbias = small_all[:, 13 : 13 + bias_rows].reshape(-1)
    temb_proj = jnp.sum(small_all[:, 13 + bias_rows :], axis=0).reshape(clip_count, channels)
    time_row = lax.dynamic_index_in_dim(temb_proj, places.clip, 0, keepdims=False)

    field = to_low(places.blocks_to_unit(latents))
    grad_unit = to_low(places.blocks_to_unit(cotangent))
    grad_columns = places.blocks_to_columns(cotangent)

    rgain, rshift = (res_gain.astype(jnp.float32), res_shift.astype(jnp.float32))
    sgain, sshift, sffbias = (
        st_gain.astype(jnp.float32),
        st_shift.astype(jnp.float32),
        st_ff_bias.astype(jnp.float32),
    )
    vocab_rows = embed_table.shape[0]
    local_ids = prompt_ids - lax.axis_index(("frame", "rows")) * vocab_rows
    ids_table = onehot(local_ids.reshape(-1), vocab_rows)
    context = lax.psum(to_low(matmul(ids_table, embed_table)), ("frame", "rows"))
    context = context.reshape(clip_count, prompt_count, -1)
    context_low = lax.dynamic_index_in_dim(context, places.clip, 0, keepdims=False)
    prompt_pad = -(-prompt_count // 128) * 128
    context_low = jnp.pad(context_low, ((0, prompt_pad - prompt_count), (0, 0)))
    prompt_bias = jnp.where(jnp.arange(prompt_pad) < prompt_count, 0.0, FAR)
    prompt_row = jnp.broadcast_to(prompt_bias[None, :], (8, prompt_pad))
    prompt_col = jnp.broadcast_to(prompt_bias[:, None], (prompt_pad, 128))

    def wide(row):
        return jnp.broadcast_to(row[None, :], (8, row.shape[0]))

    vec_one = stack_rows([rgain[0], rshift[0], rshift[2] + time_row, inv_count])
    vec_two = stack_rows([rgain[1], rshift[1], rshift[3], inv_count])
    conv_one = conv_forward(
        places_row, side, field, masks, vec_one, table, conv_all, 0, None
    )
    resid = conv_forward(
        places_row, side, conv_one, masks, vec_two, table, conv_all, 1, [field]
    )
    vec_self = stack_rows(
        [
            sgain[0], sshift[0], sshift[4], sgain[1], sshift[1], sshift[5], sshift[5], inv_count,
        ]
    )
    proj_one, query, key, value, proj_two = self_forward(
        places_row, resid, masks, key_bias, vec_self, table, sproj_all, sattn_all
    )
    vec_cross = stack_rows(
        [
            sgain[2], sshift[2], sshift[6], sgain[3], sshift[3], sshift[7], sshift[8],
            mgain[0], mshift[0], inv_count,
        ]
    )
    cross_query, cross_key, cross_value, proj_three, st_out, motion_low = cross_forward(
        places_row, proj_two, resid, context_low, masks, prompt_row, vec_cross, wide(sffbias),
        table, sproj_all, sattn_all, cross_all, sffin_all, sffout_all,
    )

    moved = to_low(places.unit_to_columns([motion_low, to_low(st_out)]))
    motion_in, st_columns = (moved[:, :channels], moved[:, channels:])
    frame_total = places.frames * frames_here
    position = frame_table(jnp.arange(frame_total, dtype=jnp.int32), channels)
    position = jnp.broadcast_to(
        position[None], (places.share_total, frame_total, channels)
    ).reshape(-1, channels)
    per_group = max(n for n in range(1, 14) if places.share_total % n == 0)
    cell_of = jnp.arange(per_group * frame_total, dtype=jnp.int32) // frame_total
    cell_bias = jnp.where(cell_of[:, None] == cell_of[None, :], 0.0, FAR)
    vec_motion = stack_rows(
        [mshift[4], mgain[1], mshift[1], mshift[5], mgain[2], mshift[2], mshift[6]]
    )
    kept = motion_forward(
        places_row, motion_in, position, cell_bias, vec_motion, mproj_pieces, mattn_pieces
    )
    zeds = kept[:3]
    out_columns, grad_zed, d_proj_out, d_ff_in, d_ff_out, small_ff, wide_ff = motion_ff(
        places_row, zeds[2], st_columns, grad_columns,
        stack_rows([mgain[3], mshift[3], mshift[7], mshift[8]]), wide(mffbias),
        mproj_pieces, mffin_pieces, mffout_pieces,
    )
    output = places.columns_to_blocks(out_columns)
    d_attn = [None, None]
    small_back = [None, None]
    for block in (1, 0):
        results = motion_back(
            places_row, block, grad_zed, zeds[block], *kept[3 + 4 * block : 7 + 4 * block],
            motion_in if block == 0 else None, position, cell_bias,
            stack_rows([mgain[1 + block], mshift[1 + block]]), mproj_pieces, mattn_pieces,
        )
        grad_zed, d_attn[block], small_back[block] = (results[0], results[1:5], results[5])
    grad_motion, d_proj_in = (grad_zed, results[6])

    def share_rows(gradients):
        joined = jnp.concatenate(
            [d.reshape(places.frames, -1, channels) for d in gradients], axis=1
        )
        mine = lax.psum_scatter(joined, "frame", scatter_dimension=0, tiled=False)
        mine = lax.psum(mine, "rows").astype(jnp.float32)
        shares = []
        start = 0
        for d in gradients:
            size = d.size // places.frames // channels
            shares.append(mine[start : start + size].reshape(-1, d.shape[1]))
            start = start + size
        return shares

    ff_in_grad, ff_out_grad, share_out = share_rows([d_ff_in, d_ff_out, d_proj_out])
    shares = share_rows([*d_attn[0], *d_attn[1], d_proj_in])
    attn_grad = jnp.stack(shares[:8]).reshape(motion_attn.shape)
    proj_grad = jnp.stack([shares[8], share_out])

    grad_gn = to_low(places.columns_to_unit(grad_motion))
    grad_two, grad_st, small_gn = cross_backward(
        places_row, grad_gn, grad_unit, st_out, proj_three, proj_two, cross_query, cross_key,
        cross_value, masks, prompt_col, vec_cross, wide(sffbias), table, sproj_all, sattn_all,
        sffin_all, sffout_all,
    )
    grad_res = self_backward(
        places_row, grad_two, proj_one, query, key, value, resid, grad_st, masks, vec_self, table,
        sproj_all, sattn_all,
    )
    grad_conv = conv_backward(
        places_row, side, grad_res, conv_one, masks, vec_two, table, conv_all, 1, []
    )
    grad_field = conv_backward(
        places_row, side, grad_conv, field, masks, vec_one, table, conv_all, 0, [grad_res]
    )
    input_grad = places.unit_to_blocks(to_low(grad_field)).astype(jnp.float32)

    gain_rows = [small_gn[0], small_back[0][1], small_back[1][1], small_ff[2]]
    shift_rows = [
        small_gn[1], small_back[0][2], small_back[1][2], small_ff[3], small_back[0][3],
        small_back[0][0], small_back[1][0], small_ff[1], small_ff[0],
    ]
    small_grads = jnp.concatenate(
        [
            jnp.stack(gain_rows + shift_rows).reshape(13, places.frames, own),
            jnp.transpose(wide_ff[0].reshape(places.frames, -1, own), (1, 0, 2)),
        ]
    )
    small_grads = lax.psum(small_grads, ("frame", "rows"))
    small_mine = lax.dynamic_index_in_dim(small_grads, places.frame, 1, keepdims=False)
    gain_grad, shift_grad = (small_mine[:4], small_mine[4:13])
    ff_bias_grad = small_mine[13:].reshape(-1)
    return (
        output,
        input_grad,
        gain_grad,
        shift_grad,
        proj_grad,
        attn_grad,
        ff_in_grad,
        ff_bias_grad,
        ff_out_grad,
    )


def solution(mesh):
    return jax.shard_map(
        on_device,
        mesh=mesh,
        in_specs=(
            P("frame", "rows", None),
            P("frame", "rows", None),
            P(),
            P(),
            P(("frame", "rows"), None),
            P(),
            P(),
            P(None, None, None, "frame", None),
            P("frame", None),
            P(),
            P(),
            P(None, "frame", None),
            P(None, "frame", None),
            P(None, "frame", None),
            P("frame", None),
            P(),
            P("frame", None),
            P(None, "frame"),
            P(None, "frame"),
            P(None, "frame", None),
            P(None, None, "frame", None),
            P("frame", None),
            P("frame"),
            P("frame", None),
        ),
        out_specs=(
            P("frame", "rows", None),
            P("frame", "rows", None),
            P(None, "frame"),
            P(None, "frame"),
            P(None, "frame", None),
            P(None, None, "frame", None),
            P("frame", None),
            P("frame"),
            P("frame", None),
        ),
        check_vma=False,
    )
```

```python
import functools
import math

import jax
import jax.numpy as jnp
import numpy as np
from jax import lax
from jax.experimental import pallas as pl
from jax.experimental.pallas import tpu as pltpu
from jax.sharding import PartitionSpec as P

HEADS = 8
GROUPS = 32
FF_ST = 2560
TEMB = 1280
SIDE_BIG = 32
SIDE_MID = 24
SIDE_SMALL = 16


HIGHEST = lax.Precision.HIGHEST
EPSILON = 1e-05
FAR = -1e30
MESH = pl.DeviceIdType.MESH


def to_low(value):
    return value.astype(jnp.bfloat16)


def matmul(left, weight):
    return jnp.dot(left, weight, preferred_element_type=jnp.float32)


def matmul_back(gradient, weight):
    return lax.dot_general(
        gradient, weight, (((1,), (1,)), ((), ())), preferred_element_type=jnp.float32
    )


def matmul_left(left, right):
    return lax.dot_general(left, right, (((0,), (0,)), ((), ())), preferred_element_type=jnp.float32)


def token_sum(gradient):
    return jnp.sum(gradient, axis=0)


def clip_layout(row_devices):
    grid_cols = min(8, row_devices // 2)
    grid_rows = row_devices // grid_cols
    sides = (
        [SIDE_BIG] * (3 * (row_devices // 64))
        + [SIDE_MID] * max(1, row_devices // 16)
        + [SIDE_SMALL] * max(1, row_devices // 16)
    )
    layout = []
    offset = 0
    for side in sides:
        layout.append((side, side // grid_rows, side // grid_cols, offset))
        offset = offset + side // grid_rows * (side // grid_cols)
    return (layout, grid_rows, grid_cols)


def time_table(timesteps):
    half_count = TEMB // 2
    frequency = jnp.exp(
        jnp.arange(half_count, dtype=jnp.float32) * (-math.log(10000.0) / half_count)
    )
    angles = timesteps.astype(jnp.float32)[:, None] * frequency[None, :]
    return jnp.concatenate([jnp.cos(angles), jnp.sin(angles)], axis=1)


def frame_table(frames, channels):
    channel = np.arange(channels)
    frequency = np.exp((channel - channel % 2) * (-math.log(10000.0) / channels))
    angles = np.arange(frames)[:, None] * frequency[None, :]
    return np.where((channel % 2 == 0)[None, :], np.sin(angles), np.cos(angles)).astype(np.float32)


def group_table(channels):
    which = np.arange(channels) // (channels // GROUPS)
    return jnp.asarray((which[:, None] == which[None, :]).astype(np.float32))


def onehot(indices, width):
    return (indices[:, None] == jnp.arange(width, dtype=jnp.int32)[None, :]).astype(jnp.bfloat16)


class Places:
    def __init__(self, frames_here, channels):
        self.rows = lax.axis_size("rows")
        self.frames = lax.axis_size("frame")
        self.row = lax.axis_index("rows")
        self.frame = lax.axis_index("frame")
        self.frames_here = frames_here
        self.layout, self.grid_rows, self.grid_cols = clip_layout(self.rows)
        self.clips = len(self.layout)
        self.units = frames_here * self.clips
        assert self.units <= self.rows
        self.channels = channels
        self.side = max(entry[0] for entry in self.layout)
        self.block_max = max(entry[1] * entry[2] for entry in self.layout)
        self.shares = [-(-entry[1] * entry[2] // self.frames) for entry in self.layout]
        self.share_max = max(self.shares)
        self.share_total = sum(self.shares)
        self.clip = self.row % self.clips
        sides = jnp.array([entry[0] for entry in self.layout], jnp.int32)
        self.my_side = jnp.where(self.row < self.units, sides[self.clip], 0)
        self.safe_side = jnp.maximum(self.my_side, self.grid_rows * self.grid_cols)
        cells = jnp.arange(self.side * self.side, dtype=jnp.int32)
        self.cell_row, self.cell_col = cells // self.side, cells % self.side
        self.valid = (self.cell_row < self.my_side) & (self.cell_col < self.my_side)
        block_rows = sides[self.clip] // self.grid_rows
        block_cols = sides[self.clip] // self.grid_cols
        self.device = self.cell_row // block_rows * self.grid_cols + self.cell_col // block_cols
        self.in_block = self.cell_row % block_rows * block_cols + self.cell_col % block_cols
        shares = jnp.array(self.shares, jnp.int32)
        share = shares[self.clip]
        block_index = jnp.where(self.valid, self.device * self.block_max + self.in_block, -1)
        self.block_table = onehot(block_index, self.rows * self.block_max)
        column_index = (
            (self.in_block // share * self.rows + self.device) * self.share_max
            + self.in_block % share
        )
        column_index = jnp.where(self.valid, column_index, -1)
        self.column_table = onehot(column_index, self.frames * self.rows * self.share_max)
        picks = []
        for number in range(self.clips):
            cell = np.arange(self.shares[number])[:, None]
            when = np.arange(self.frames * frames_here)[None, :]
            source = (
                when // frames_here * self.rows + when % frames_here * self.clips + number
            ) * self.share_max + cell
            picks.append(source.reshape(-1))
        picks = np.concatenate(picks)
        slots = np.arange(self.frames * self.rows * self.share_max)
        self.pick_table = jnp.asarray((picks[:, None] == slots[None, :]).astype(jnp.bfloat16))

    def blocks_to_unit(self, blocks):
        pieces = []
        for frame in range(self.frames_here):
            for side, height, width, offset in self.layout:
                piece = blocks[frame, offset : offset + height * width]
                pieces.append(jnp.pad(piece, ((0, self.block_max - height * width), (0, 0))))
        for _ in range(self.units, self.rows):
            pieces.append(jnp.zeros_like(pieces[0]))
        received = lax.all_to_all(jnp.stack(pieces), "rows", 0, 0)
        return matmul(self.block_table, received.reshape(-1, self.channels))

    def unit_to_blocks(self, field_low):
        send = to_low(matmul_left(self.block_table, field_low))
        send = send.reshape(self.rows, self.block_max, self.channels)
        received = lax.all_to_all(send, "rows", 0, 0)
        frames = []
        for frame in range(self.frames_here):
            frames.append(
                jnp.concatenate(
                    [
                        received[frame * self.clips + number, : entry[1] * entry[2]]
                        for number, entry in enumerate(self.layout)
                    ]
                )
            )
        return jnp.stack(frames)

    def unit_to_columns(self, fields_low):
        width = sum(field.shape[-1] for field in fields_low)
        joined = jnp.concatenate(fields_low, axis=1)
        send = to_low(matmul_left(self.column_table, joined))
        send = send.reshape(self.frames * self.rows, self.share_max, width)
        received = lax.all_to_all(send, ("frame", "rows"), 0, 0)
        return received.reshape(-1, width)

    def columns_to_unit(self, field_low):
        send = to_low(matmul_left(self.pick_table, field_low))
        send = send.reshape(self.frames * self.rows, self.share_max, self.channels)
        received = lax.all_to_all(send, ("frame", "rows"), 0, 0)
        return matmul(self.column_table, received.reshape(-1, self.channels))

    def blocks_to_columns(self, blocks):
        parts = []
        for number, (side, height, width, offset) in enumerate(self.layout):
            share = self.shares[number]
            part = blocks[:, offset : offset + height * width]
            part = jnp.pad(part, ((0, 0), (0, share * self.frames - height * width), (0, 0)))
            parts.append(part.reshape(self.frames_here, self.frames, share, self.channels))
        send = jnp.transpose(jnp.concatenate(parts, axis=2), (1, 0, 2, 3))
        received = lax.all_to_all(send, "frame", 0, 0)
        received = received.reshape(-1, self.share_total, self.channels)
        return jnp.transpose(received, (1, 0, 2)).reshape(-1, self.channels)

    def columns_to_blocks(self, field_low):
        send = jnp.transpose(field_low.reshape(self.share_total, -1, self.channels), (1, 0, 2))
        send = send.reshape(self.frames, self.frames_here, self.share_total, self.channels)
        received = lax.all_to_all(send, "frame", 0, 0)
        parts = []
        start = 0
        for number, (side, height, width, offset) in enumerate(self.layout):
            share = self.shares[number]
            part = jnp.transpose(received[:, :, start : start + share], (1, 0, 2, 3))
            part = part.reshape(self.frames_here, self.frames * share, self.channels)
            parts.append(part[:, : height * width])
            start = start + share
        return jnp.concatenate(parts, axis=1)


def shard_order():
    frame = lax.axis_index("frame")
    return jnp.stack([frame, frame ^ 1, frame ^ 2, frame ^ 3]).astype(jnp.int32)


def start_load(order_ref, pieces, lead, target, sem):
    whole, own = pieces
    rows = own.shape[-2]
    for number in range(4):
        where = pl.ds(pl.multiple_of(order_ref[number] * rows, 16), rows)
        if lead is None:
            source = own if number == 0 else whole.at[where]
        elif number == 0:
            source = own.at[lead]
        else:
            source = whole.at[lead, where]
        goal = target.at[where] if len(target.shape) == 2 else target.at[:, where]
        pltpu.make_async_copy(source, goal, sem).start()


def pair_load(order_ref, groups, lead, target, sem):
    if lead < 2:
        start_load(order_ref, groups[0], lead, target, sem)
    else:
        start_load(order_ref, groups[1], lead - 2, target, sem)


def finish_load(target, sem):
    pltpu.make_async_copy(target, target, sem).wait()


def run_kernel(body, order_row, arrays, groups, outs, scratch, flops):
    count, pieces = len(arrays), sum(len(group) for group in groups)
    out_count = len(outs)

    def kernel(*refs):
        held = list(refs[1 + count : 1 + count + pieces])
        grouped = [[held.pop(0) for _ in group] for group in groups]
        outputs = refs[1 + count + pieces : 1 + count + pieces + out_count]
        body(
            refs[0],
            refs[1 : 1 + count],
            grouped,
            outputs,
            refs[1 + count + pieces + out_count :],
        )

    whole = pl.BlockSpec(memory_space=pltpu.VMEM)
    flat = [piece for group in groups for piece in group]
    return pl.pallas_call(
        kernel,
        out_shape=outs,
        in_specs=[pl.BlockSpec(memory_space=pltpu.SMEM)]
        + [whole] * count
        + [pl.BlockSpec(memory_space=pl.ANY)] * pieces,
        out_specs=[whole] * out_count,
        scratch_shapes=scratch,
        compiler_params=pltpu.CompilerParams(vmem_limit_bytes=56 * 2**20),
        cost_estimate=pl.CostEstimate(flops=flops // 1000, bytes_accessed=4096, transcendentals=0),
    )(order_row, *arrays, *flat)


def rows_of(ref):
    value = ref[...].astype(jnp.float32)
    return [value[number : number + 1] for number in range(value.shape[0])]


def f32(*shape):
    return jax.ShapeDtypeStruct(shape, jnp.float32)


def b16(*shape):
    return jax.ShapeDtypeStruct(shape, jnp.bfloat16)


def dot_nn(left, right):
    return jnp.dot(left, right, preferred_element_type=jnp.float32)


def dot_nt(left, right):
    return lax.dot_general(left, right, (((1,), (1,)), ((), ())), preferred_element_type=jnp.float32)


def dot_tn(left, right):
    return lax.dot_general(left, right, (((0,), (0,)), ((), ())), preferred_element_type=jnp.float32)


def spread_means(first, second, table, inv_count):
    rows = jnp.concatenate(
        [
            jnp.sum(first, axis=0, keepdims=True),
            jnp.sum(second, axis=0, keepdims=True),
            jnp.zeros((6, first.shape[1]), jnp.float32),
        ]
    )
    means = jnp.dot(rows, table, precision=HIGHEST, preferred_element_type=jnp.float32) * inv_count
    return (means[0:1], means[1:2])


def group_normed(field, valid, table, inv_count):
    kept = field * valid
    average, square = spread_means(kept, kept * field, table, inv_count)
    inv_std = lax.rsqrt(square - average * average + EPSILON)
    return ((field - average) * inv_std, inv_std)


def group_back(gradient, normed, inv_std, gain, valid, table, inv_count):
    scaled = gradient * gain * valid
    mean_one, mean_two = spread_means(scaled, scaled * normed, table, inv_count)
    return inv_std * (scaled - mean_one - normed * mean_two) * valid


def layer_normed(field):
    centred = field - jnp.mean(field, axis=1, keepdims=True)
    inv_std = lax.rsqrt(jnp.mean(centred * centred, axis=1, keepdims=True) + EPSILON)
    return (centred * inv_std, inv_std)


def layer_back(gradient, normed, inv_std, gain):
    scaled = gradient * gain
    mean_one = jnp.mean(scaled, axis=1, keepdims=True)
    mean_two = jnp.mean(scaled * normed, axis=1, keepdims=True)
    return inv_std * (scaled - mean_one - normed * mean_two)


def half_erf(field):
    return 0.5 + 0.5 * lax.erf(field * (0.5**0.5))


def gelu_slope(field, half):
    return half + field * (jnp.exp(-0.5 * field * field) * (1.0 / math.sqrt(2.0 * math.pi)))


def head_windows(channels):
    width = channels // HEADS
    windows = []
    for head in range(HEADS):
        start = head * width // 128 * 128
        stop = -(-(head + 1) * width // 128) * 128
        windows.append((start, stop, head * width - start, (head + 1) * width - start))
    return windows


def head_mask(window):
    start, stop, low, high = window
    lane = lax.broadcasted_iota(jnp.int32, (1, stop - start), 1)
    return ((lane >= low) & (lane < high)).astype(jnp.float32).astype(jnp.bfloat16)


def attend_into(query_ref, key_ref, value_ref, bias, out_ref, rows):
    channels = query_ref.shape[1]
    factor = (channels // HEADS) ** (-0.5) * math.log2(math.e)
    out_ref[rows, :] = jnp.zeros((query_ref[rows, :].shape[0], channels), jnp.float32)
    for window in head_windows(channels):
        lanes = slice(window[0], window[1])
        mask = head_mask(window)
        scores = dot_nt(query_ref[rows, lanes] * mask, key_ref[rows if bias.shape[0] > 1 else slice(None), lanes])
        scores = scores * factor + bias
        powers = jnp.exp2(scores - jnp.max(scores, axis=1, keepdims=True))
        inverse = 1.0 / jnp.sum(powers, axis=1, keepdims=True)
        values = value_ref[rows if bias.shape[0] > 1 else slice(None), lanes] * mask
        out_ref[rows, lanes] += dot_nn(to_low(powers), values) * inverse


def attend_back_into(query_ref, key_ref, value_ref, grad_ref, bias, outs, rows, key_rows):
    channels = query_ref.shape[1]
    scale = (channels // HEADS) ** (-0.5)
    factor = scale * math.log2(math.e)
    for number, out_ref in enumerate(outs):
        size = (rows if number == 0 else key_rows)
        out_ref[size, :] = jnp.zeros(
            ((query_ref if number == 0 else key_ref)[size, :].shape[0], channels), jnp.float32
        )
    for window in head_windows(channels):
        lanes = slice(window[0], window[1])
        mask = head_mask(window)
        queries = query_ref[rows, lanes] * mask
        keys = key_ref[key_rows, lanes] * mask
        grads = grad_ref[rows, lanes] * mask
        scores = dot_nt(keys, queries) * factor + bias
        powers = jnp.exp2(scores - jnp.max(scores, axis=0, keepdims=True))
        probs = powers * (1.0 / jnp.sum(powers, axis=0, keepdims=True))
        grad_probs = dot_nt(value_ref[key_rows, lanes], grads)
        inner = jnp.sum(probs * grad_probs, axis=0, keepdims=True)
        grad_scores = to_low(probs * (grad_probs - inner))
        outs[0][rows, lanes] += dot_tn(grad_scores, keys) * scale
        if len(outs) > 1:
            outs[1][key_rows, lanes] += dot_nn(grad_scores, queries) * scale
            outs[2][key_rows, lanes] += dot_nn(to_low(probs), grads)


ALL = slice(None)


def fill_taps(field, masks, pads, side):
    cells = field.shape[0]
    border = jnp.zeros((side, field.shape[1]), jnp.float32)
    left = pltpu.roll(field, 1, 0) * masks[:, 1:2]
    right = pltpu.roll(field, cells - 1, 0) * masks[:, 2:3]
    for number, moved in enumerate((left, field, right)):
        pads[number, :side, :] = border
        pads[number, side : side + cells, :] = moved
        pads[number, side + cells :, :] = border


def conv_rows(gains_ref, shifts_ref, stats_ref, which):
    gains, shifts, stats = rows_of(gains_ref), rows_of(shifts_ref), rows_of(stats_ref)
    bias = shifts[2 + which] + stats[1] if which == 0 else shifts[2 + which]
    return [gains[which], shifts[which], bias, stats[0]]


def conv_forward(order_row, side, field, masks, gains, shifts, stats, table, weights, which, residual, early):
    cells, channels = field.shape

    def body(order_ref, ins, groups, outs, scratch):
        field_ref, masks_ref, gains_ref, shifts_ref, stats_ref, table_ref = ins[:6]
        weight, pads, sem = scratch
        (out_ref,) = outs
        start_load(order_ref, groups[0], pl.ds(9 * which, 9), weight, sem.at[0])
        masks = masks_ref[...]
        valid = masks[:, 0:1]
        vec = conv_rows(gains_ref, shifts_ref, stats_ref, which)
        normed, _ = group_normed(
            field_ref[...].astype(jnp.float32), valid, table_ref[...], vec[3]
        )
        pre = normed * vec[0] + vec[1]
        act = pre / (1.0 + jnp.exp(-pre)) * valid
        fill_taps(act, masks, pads, side)
        out_ref[...] = jnp.broadcast_to(vec[2], (cells, channels))
        if residual:
            out_ref[...] += field_resid(ins)
        finish_load(weight, sem.at[0])

        def row_tap(step, carry):
            rows = pl.ds(pl.multiple_of(step * side, 8), cells)
            total = out_ref[...]
            for col in range(3):
                total += dot_nn(to_low(pads[col, rows, :]), weight[step * 3 + col])
            out_ref[...] = total
            return carry

        lax.fori_loop(0, 3, row_tap, 0)

    def field_resid(ins):
        return ins[6][...].astype(jnp.float32)

    arrays = [field, masks, gains, shifts, stats, table] + ([residual[0]] if residual else [])
    return run_kernel(
        body,
        order_row,
        arrays,
        [weights, early],
        [f32(cells, channels)],
        [
            pltpu.VMEM((9, channels, channels), jnp.bfloat16),
            pltpu.VMEM((3, cells + 2 * side, channels), jnp.float32),
            pltpu.SemaphoreType.DMA((1,)),
        ],
        18 * cells * channels * channels,
    )[0]


def conv_backward(order_row, side, gradient, field, masks, gains, shifts, stats, table, weights, which, extra):
    cells, channels = field.shape

    def body(order_ref, ins, groups, outs, scratch):
        grad_ref, field_ref, masks_ref, gains_ref, shifts_ref, stats_ref, table_ref = ins[:7]
        weight, pads, total_ref, sem = scratch
        (out_ref,) = outs
        start_load(order_ref, groups[0], pl.ds(9 * which, 9), weight, sem.at[0])
        masks = masks_ref[...]
        valid = masks[:, 0:1]
        vec = conv_rows(gains_ref, shifts_ref, stats_ref, which)
        fill_taps(grad_ref[...], masks, pads, side)
        total_ref[...] = jnp.zeros((cells, channels), jnp.float32)
        finish_load(weight, sem.at[0])

        def row_tap(step, carry):
            rows = pl.ds(pl.multiple_of(step * side, 8), cells)
            total = total_ref[...]
            for col in range(3):
                total += dot_nt(to_low(pads[col, rows, :]), weight[8 - (step * 3 + col)])
            total_ref[...] = total
            return carry

        lax.fori_loop(0, 3, row_tap, 0)
        normed, inv_std = group_normed(
            field_ref[...].astype(jnp.float32), valid, table_ref[...], vec[3]
        )
        pre = normed * vec[0] + vec[1]
        gate = 1.0 / (1.0 + jnp.exp(-pre))
        grad_pre = total_ref[...] * (gate * (1.0 + pre * (1.0 - gate)))
        result = group_back(
            grad_pre, normed, inv_std, vec[0], valid, table_ref[...], vec[3]
        )
        if extra:
            result += ins[7][...]
        out_ref[...] = result

    return run_kernel(
        body,
        order_row,
        [gradient, field, masks, gains, shifts, stats, table] + list(extra),
        [weights],
        [f32(cells, channels)],
        [
            pltpu.VMEM((9, channels, channels), jnp.bfloat16),
            pltpu.VMEM((3, cells + 2 * side, channels), jnp.float32),
            pltpu.VMEM((cells, channels), jnp.float32),
            pltpu.SemaphoreType.DMA((1,)),
        ],
        18 * cells * channels * channels,
    )[0]


def self_rows(gains_ref, shifts_ref, stats_ref):
    gains, shifts, stats = rows_of(gains_ref), rows_of(shifts_ref), rows_of(stats_ref)
    return [gains[0], shifts[0], shifts[4], gains[1], shifts[1], shifts[5], None, stats[0]]


def self_forward(order_row, resid, masks, bias, gains, shifts, stats, table, proj, attn):
    cells, channels = resid.shape
    needed = (0, 2, 3, 4, 5)

    def body(order_ref, ins, groups, outs, scratch):
        resid_ref, masks_ref, bias_ref, gains_ref, shifts_ref, stats_ref, table_ref = ins
        proj_ref, query_ref, key_ref, value_ref, two_ref = outs
        weight, att, sem = scratch
        for slot, lead in enumerate(needed):
            pair_load(order_ref, groups, lead, weight.at[slot], sem.at[slot])
        vec = self_rows(gains_ref, shifts_ref, stats_ref)
        normed, _ = group_normed(resid_ref[...], masks_ref[:, 0:1], table_ref[...], vec[7])
        low = to_low(normed * vec[0] + vec[1])
        finish_load(weight.at[0], sem.at[0])
        entered = dot_nn(low, weight[0]) + vec[2]
        proj_ref[...] = entered
        normed, _ = layer_normed(entered)
        low = to_low(normed * vec[3] + vec[4])
        for slot, out_ref in ((1, query_ref), (2, key_ref), (3, value_ref)):
            finish_load(weight.at[slot], sem.at[slot])
            out_ref[...] = to_low(dot_nn(low, weight[slot]))
        attend_into(query_ref, key_ref, value_ref, bias_ref[0:1, :], att, ALL)
        finish_load(weight.at[4], sem.at[4])
        two_ref[...] = proj_ref[...] + dot_nn(to_low(att[...]), weight[4]) + vec[5]

    return run_kernel(
        body,
        order_row,
        [resid, masks, bias, gains, shifts, stats, table],
        [proj, attn],
        [f32(cells, channels)] + [b16(cells, channels)] * 3 + [f32(cells, channels)],
        [
            pltpu.VMEM((5, channels, channels), jnp.bfloat16),
            pltpu.VMEM((cells, channels), jnp.float32),
            pltpu.SemaphoreType.DMA((5,)),
        ],
        10 * cells * channels * channels + 4 * cells * cells * channels,
    )


def self_backward(order_row, early, grad_two, proj_one, query, key, value, resid, grad_st, masks, gains, shifts, stats, table, proj, attn):
    cells, channels = resid.shape
    needed = (5, 2, 3, 4, 0)

    def body(order_ref, ins, groups, outs, scratch):
        grad_ref, proj_ref, query_ref, key_ref, value_ref, resid_ref, st_ref, masks_ref, gains_ref, shifts_ref, stats_ref, table_ref = ins
        (out_ref,) = outs
        weight, grad_att, grad_q, grad_k, grad_v, sem = scratch
        for slot, lead in enumerate(needed):
            pair_load(order_ref, groups, lead, weight.at[slot], sem.at[slot])
        vec = self_rows(gains_ref, shifts_ref, stats_ref)
        valid = masks_ref[:, 0:1]
        finish_load(weight.at[0], sem.at[0])
        grad_att[...] = to_low(dot_nt(to_low(grad_ref[...]), weight[0]))
        attend_back_into(
            query_ref, key_ref, value_ref, grad_att, (valid - 1.0) * -FAR,
            (grad_q, grad_k, grad_v), ALL, ALL,
        )
        total = None
        for slot, member in ((1, grad_q), (2, grad_k), (3, grad_v)):
            finish_load(weight.at[slot], sem.at[slot])
            part = dot_nt(to_low(member[...]), weight[slot])
            total = part if total is None else total + part
        normed, inv_std = layer_normed(proj_ref[...])
        grad_one = grad_ref[...] + layer_back(total, normed, inv_std, vec[3])
        finish_load(weight.at[4], sem.at[4])
        grad_gn = dot_nt(to_low(grad_one), weight[4])
        normed, inv_std = group_normed(resid_ref[...], valid, table_ref[...], vec[7])
        out_ref[...] = st_ref[...] + group_back(
            grad_gn, normed, inv_std, vec[0], valid, table_ref[...], vec[7]
        )

    return run_kernel(
        body,
        order_row,
        [grad_two, proj_one, query, key, value, resid, grad_st, masks, gains, shifts, stats, table],
        [proj, attn, early],
        [f32(cells, channels)],
        [
            pltpu.VMEM((5, channels, channels), jnp.bfloat16),
            pltpu.VMEM((cells, channels), jnp.bfloat16),
            pltpu.VMEM((cells, channels), jnp.float32),
            pltpu.VMEM((cells, channels), jnp.float32),
            pltpu.VMEM((cells, channels), jnp.float32),
            pltpu.SemaphoreType.DMA((5,)),
        ],
        10 * cells * channels * channels + 10 * cells * cells * channels,
    )[0]


CHUNK = 512


def cross_rows(gains_ref, shifts_ref, motion_rows_ref, stats_ref):
    gains, shifts = rows_of(gains_ref), rows_of(shifts_ref)
    motion, stats = rows_of(motion_rows_ref), rows_of(stats_ref)
    return [
        gains[2], shifts[2], shifts[6], gains[3], shifts[3], shifts[7], shifts[8],
        motion[0], motion[4], stats[0],
    ]


def cross_forward(order_row, early, two, resid, context, masks, bias, gains, shifts, motion_rows, stats, wide_bias, table, proj, attn, cross, w_in_all, w_out_all):
    cells, channels = resid.shape
    prompt, width = context.shape

    def body(order_ref, ins, groups, outs, scratch):
        two_ref, resid_ref, context_ref, masks_ref, bias_ref, gains_ref, shifts_ref, motion_rows_ref, stats_ref, wide_ref, table_ref = ins
        query_ref, key_ref, value_ref, three_ref, out_ref, motion_ref = outs
        weight, kv, w_in, w_out, att, total, sem = scratch
        for slot, lead in enumerate((6, 7, 1)):
            pair_load(order_ref, groups, lead, weight.at[slot], sem.at[slot])
        for slot in range(2):
            start_load(order_ref, groups[2], slot, kv.at[slot], sem.at[3 + slot])
        start_load(order_ref, groups[3], None, w_in, sem.at[5])
        start_load(order_ref, groups[4], None, w_out, sem.at[6])
        vec = cross_rows(gains_ref, shifts_ref, motion_rows_ref, stats_ref)
        normed, _ = layer_normed(two_ref[...])
        low = to_low(normed * vec[0] + vec[1])
        finish_load(weight.at[0], sem.at[0])
        query_ref[...] = to_low(dot_nn(low, weight[0]))
        for slot, ref in ((0, key_ref), (1, value_ref)):
            finish_load(kv.at[slot], sem.at[3 + slot])
            ref[...] = to_low(dot_nn(context_ref[...], kv[slot]))
        attend_into(query_ref, key_ref, value_ref, bias_ref[0:1, :], att, ALL)
        finish_load(weight.at[1], sem.at[1])
        three_ref[...] = two_ref[...] + dot_nn(to_low(att[...]), weight[1]) + vec[2]
        normed, _ = layer_normed(three_ref[...])
        low = to_low(normed * vec[3] + vec[4])
        finish_load(w_in, sem.at[5])
        finish_load(w_out, sem.at[6])
        total[...] = three_ref[...] + vec[5]

        def chunk(step, carry):
            lanes = pl.ds(pl.multiple_of(step * CHUNK, 128), CHUNK)
            gates = pl.ds(pl.multiple_of(FF_ST + step * CHUNK, 128), CHUNK)
            hidden = dot_nn(low_ref(att), w_in[:, lanes]) + wide_ref[0:1, lanes]
            gate = dot_nn(low_ref(att), w_in[:, gates]) + wide_ref[0:1, gates]
            act = to_low(hidden * (gate * half_erf(gate)))
            total[...] += dot_nn(act, w_out[lanes, :])
            return carry

        def low_ref(ref):
            return to_low(ref[...])

        att[...] = low.astype(jnp.float32)
        lax.fori_loop(0, FF_ST // CHUNK, chunk, 0)
        finish_load(weight.at[2], sem.at[2])
        st_out = dot_nn(to_low(total[...]), weight[2]) + vec[6] + resid_ref[...]
        out_ref[...] = st_out
        normed, _ = group_normed(st_out, masks_ref[:, 0:1], table_ref[...], vec[9])
        motion_ref[...] = to_low(normed * vec[7] + vec[8])

    return run_kernel(
        body,
        order_row,
        [two, resid, context, masks, bias, gains, shifts, motion_rows, stats, wide_bias, table],
        [proj, attn, cross, w_in_all, w_out_all, early],
        [
            b16(cells, channels),
            b16(prompt, channels),
            b16(prompt, channels),
            f32(cells, channels),
            f32(cells, channels),
            b16(cells, channels),
        ],
        [
            pltpu.VMEM((3, channels, channels), jnp.bfloat16),
            pltpu.VMEM((2, width, channels), jnp.bfloat16),
            pltpu.VMEM((channels, 2 * FF_ST), jnp.bfloat16),
            pltpu.VMEM((FF_ST, channels), jnp.bfloat16),
            pltpu.VMEM((cells, channels), jnp.float32),
            pltpu.VMEM((cells, channels), jnp.float32),
            pltpu.SemaphoreType.DMA((7,)),
        ],
        2 * cells * channels * (3 * channels + 3 * FF_ST),
    )


def cross_backward(order_row, grad_gn, grad_out, st_out, three, two, query, key, value, masks, bias_col, gains, shifts, motion_rows, stats, wide_bias, table, proj, attn, w_in_all, w_out_all):
    cells, channels = st_out.shape
    prompt = key.shape[0]

    def body(order_ref, ins, groups, outs, scratch):
        gn_ref, cot_ref, st_ref, three_ref, two_ref, query_ref, key_ref, value_ref, masks_ref, bias_ref, gains_ref, shifts_ref, motion_rows_ref, stats_ref, wide_ref, table_ref = ins
        grad_two_ref, grad_st_ref = outs
        weight, w_in, w_out, low, grad_low, total, grad_att, grad_q, sem = scratch
        pair_load(order_ref, groups, 1, weight.at[0], sem.at[0])
        start_load(order_ref, groups[3], None, w_out, sem.at[4])
        start_load(order_ref, groups[2], None, w_in, sem.at[3])
        pair_load(order_ref, groups, 7, weight.at[1], sem.at[1])
        pair_load(order_ref, groups, 6, weight.at[2], sem.at[2])
        vec = cross_rows(gains_ref, shifts_ref, motion_rows_ref, stats_ref)
        valid = masks_ref[:, 0:1]
        grad_motion = gn_ref[...].astype(jnp.float32)
        normed, inv_std = group_normed(st_ref[...], valid, table_ref[...], vec[9])
        grad_st_ref[...] = cot_ref[...].astype(jnp.float32) + group_back(
            grad_motion, normed, inv_std, vec[7], valid, table_ref[...], vec[9]
        )
        finish_load(weight.at[0], sem.at[0])
        grad_two_ref[...] = dot_nt(to_low(grad_st_ref[...]), weight[0])
        grad_low[...] = to_low(grad_two_ref[...])
        normed, inv_std = layer_normed(three_ref[...])
        low[...] = to_low(normed * vec[3] + vec[4])
        total[...] = jnp.zeros((cells, channels), jnp.float32)
        finish_load(w_out, sem.at[4])
        finish_load(w_in, sem.at[3])

        def chunk(step, carry):
            lanes = pl.ds(pl.multiple_of(step * CHUNK, 128), CHUNK)
            gates = pl.ds(pl.multiple_of(FF_ST + step * CHUNK, 128), CHUNK)
            hidden = dot_nn(low[...], w_in[:, lanes]) + wide_ref[0:1, lanes]
            gate = dot_nn(low[...], w_in[:, gates]) + wide_ref[0:1, gates]
            grad_act = dot_nt(grad_low[...], w_out[lanes, :])
            half = half_erf(gate)
            grad_hidden = to_low(grad_act * (gate * half))
            grad_gate = to_low(grad_act * hidden * gelu_slope(gate, half))
            total[...] += dot_nt(grad_hidden, w_in[:, lanes]) + dot_nt(grad_gate, w_in[:, gates])
            return carry

        lax.fori_loop(0, FF_ST // CHUNK, chunk, 0)
        normed, inv_std = layer_normed(three_ref[...])
        grad_two_ref[...] += layer_back(total[...], normed, inv_std, vec[3])
        finish_load(weight.at[1], sem.at[1])
        grad_att[...] = to_low(dot_nt(to_low(grad_two_ref[...]), weight[1]))
        attend_back_into(
            query_ref, key_ref, value_ref, grad_att, bias_ref[:, 0:1], (grad_q,), ALL, ALL
        )
        finish_load(weight.at[2], sem.at[2])
        grad_ln = dot_nt(to_low(grad_q[...]), weight[2])
        normed, inv_std = layer_normed(two_ref[...])
        grad_two_ref[...] += layer_back(grad_ln, normed, inv_std, vec[0])

    return run_kernel(
        body,
        order_row,
        [grad_gn, grad_out, st_out, three, two, query, key, value, masks, bias_col, gains, shifts, motion_rows, stats, wide_bias, table],
        [proj, attn, w_in_all, w_out_all],
        [f32(cells, channels), f32(cells, channels)],
        [
            pltpu.VMEM((3, channels, channels), jnp.bfloat16),
            pltpu.VMEM((channels, 2 * FF_ST), jnp.bfloat16),
            pltpu.VMEM((FF_ST, channels), jnp.bfloat16),
            pltpu.VMEM((cells, channels), jnp.bfloat16),
            pltpu.VMEM((cells, channels), jnp.bfloat16),
            pltpu.VMEM((cells, channels), jnp.float32),
            pltpu.VMEM((cells, channels), jnp.bfloat16),
            pltpu.VMEM((cells, channels), jnp.float32),
            pltpu.SemaphoreType.DMA((5,)),
        ],
        2 * cells * channels * (3 * channels + 6 * FF_ST),
    )


def group_rows(step, group_len):
    return pl.ds(pl.multiple_of(step * group_len, 16), group_len)


def motion_forward(order_row, moved, picks, position, bias, vectors, proj, attn):
    tokens, channels = position.shape
    group_len = bias.shape[0]

    def body(order_ref, ins, groups, outs, scratch):
        moved_ref, picks_ref, pos_ref, bias_ref, vec_ref = ins
        weight, att, sem = scratch
        for slot, lead in enumerate((0, 2, 3, 4, 5, 6, 7, 8, 9)):
            pair_load(order_ref, groups, lead, weight.at[slot], sem.at[slot])
        rows = rows_of(vec_ref)
        vec = [rows[number] for number in (8, 1, 5, 9, 2, 6, 10)]
        finish_load(weight.at[0], sem.at[0])
        entered = to_low(dot_nn(picks_ref[...], moved_ref[...]))
        outs[11][...] = entered
        outs[0][...] = dot_nn(entered, weight[0]) + vec[0]
        for block in range(2):
            zed_ref, next_ref = outs[block], outs[block + 1]
            qkv = outs[3 + 4 * block : 6 + 4 * block]
            time_ref = outs[6 + 4 * block]
            normed, _ = layer_normed(zed_ref[...])
            low = to_low(normed * vec[1 + 3 * block] + vec[2 + 3 * block] + pos_ref[...])
            for which in range(3):
                slot = 1 + 4 * block + which
                finish_load(weight.at[slot], sem.at[slot])
                qkv[which][...] = to_low(dot_nn(low, weight[slot]))

            def group(step, carry):
                attend_into(*qkv, bias_ref[...], att, group_rows(step, group_len))
                return carry

            lax.fori_loop(0, tokens // group_len, group, 0)
            time_ref[...] = to_low(att[...])
            slot = 4 + 4 * block
            finish_load(weight.at[slot], sem.at[slot])
            next_ref[...] = zed_ref[...] + dot_nn(time_ref[...], weight[slot]) + vec[3 + 3 * block]

    return run_kernel(
        body,
        order_row,
        [moved, picks, position, bias, vectors],
        [proj, attn],
        [f32(tokens, channels)] * 3 + [b16(tokens, channels)] * 9,
        [
            pltpu.VMEM((9, channels, channels), jnp.bfloat16),
            pltpu.VMEM((tokens, channels), jnp.float32),
            pltpu.SemaphoreType.DMA((9,)),
        ],
        18 * tokens * channels * channels,
    )


def motion_ff(order_row, zed, st_moved, picks, cotangent, vectors, wide_bias, proj, in_pieces, out_pieces):
    tokens, channels = zed.shape
    hidden_width = wide_bias.shape[1]
    frames = 4
    own = channels // frames
    joined = hidden_width // frames + own * (hidden_width // channels) + own
    second, third = own * (hidden_width // channels), joined - own
    assert hidden_width == frames * channels

    def body(order_ref, ins, groups, outs, scratch):
        zed_ref, st_ref, picks_ref, cot_ref, vec_ref, wide_ref = ins
        out_ref, grad_ref, d_all, small_ref, wide_out = outs
        weight, w_in, w_out, pre, low, grad_low, total, sem = scratch
        start_load(order_ref, groups[1], None, w_in, sem.at[0])
        start_load(order_ref, groups[2], None, w_out, sem.at[1])
        start_load(order_ref, groups[0], 1, weight, sem.at[2])
        rows = rows_of(vec_ref)
        vec = [rows[3], rows[7], rows[11], rows[12]]
        normed, inv_std = layer_normed(zed_ref[...])
        low[...] = to_low(normed * vec[0] + vec[1])
        total[...] = zed_ref[...] + vec[2]
        finish_load(w_in, sem.at[0])
        finish_load(w_out, sem.at[1])

        def forward(step, carry):
            lanes = pl.ds(pl.multiple_of(step * channels, 128), channels)
            before = dot_nn(low[...], w_in[:, lanes]) + wide_ref[0:1, lanes]
            pre[:, lanes] = before
            total[...] += dot_nn(to_low(before * half_erf(before)), w_out[lanes, :])
            return carry

        lax.fori_loop(0, hidden_width // channels, forward, 0)
        finish_load(weight, sem.at[2])
        zed_low = to_low(total[...])
        out_ref[...] = to_low(dot_nn(picks_ref[...], st_ref[...]) + dot_nn(zed_low, weight[...]) + vec[3])
        d_proj = to_low(dot_tn(zed_low, cot_ref[...]))
        for shard in range(frames):
            d_all[shard, third:, :] = d_proj[shard * own : (shard + 1) * own]
        grad_ref[...] = dot_nt(cot_ref[...], weight[...])
        grad_low[...] = to_low(grad_ref[...])
        total[...] = jnp.zeros((tokens, channels), jnp.float32)

        def backward(step, carry):
            lanes = pl.ds(pl.multiple_of(step * channels, 128), channels)
            before = pre[:, lanes]
            half = half_erf(before)
            d_all[step, second:third, :] = to_low(dot_tn(to_low(before * half), grad_low[...]))
            grad_pre = dot_nt(grad_low[...], w_out[lanes, :]) * gelu_slope(before, half)
            wide_out[0:1, lanes] = jnp.sum(grad_pre, axis=0, keepdims=True)
            pre_low = to_low(grad_pre)
            d_in = to_low(dot_tn(low[...], pre_low))
            for shard in range(frames):
                rows_in = pl.ds(pl.multiple_of(step * own, 16), own)
                d_all[shard, rows_in, :] = d_in[shard * own : (shard + 1) * own]
            total[...] += dot_nt(pre_low, w_in[:, lanes])
            return carry

        wide_out[...] = jnp.zeros((8, hidden_width), jnp.float32)
        lax.fori_loop(0, hidden_width // channels, backward, 0)
        normed, inv_std = layer_normed(zed_ref[...])
        grad_ln = total[...]
        small_ref[...] = jnp.concatenate(
            [
                jnp.sum(cot_ref[...].astype(jnp.float32), axis=0, keepdims=True),
                jnp.sum(grad_ref[...], axis=0, keepdims=True),
                jnp.sum(grad_ln * normed, axis=0, keepdims=True),
                jnp.sum(grad_ln, axis=0, keepdims=True),
                jnp.zeros((4, channels), jnp.float32),
            ]
        )
        grad_ref[...] += layer_back(grad_ln, normed, inv_std, vec[0])

    return run_kernel(
        body,
        order_row,
        [zed, st_moved, picks, cotangent, vectors, wide_bias],
        [proj, in_pieces, out_pieces],
        [
            b16(tokens, channels),
            f32(tokens, channels),
            b16(frames, joined, channels),
            f32(8, channels),
            f32(8, hidden_width),
        ],
        [
            pltpu.VMEM((channels, channels), jnp.bfloat16),
            pltpu.VMEM((channels, hidden_width), jnp.bfloat16),
            pltpu.VMEM((hidden_width, channels), jnp.bfloat16),
            pltpu.VMEM((tokens, hidden_width), jnp.float32),
            pltpu.VMEM((tokens, channels), jnp.bfloat16),
            pltpu.VMEM((tokens, channels), jnp.bfloat16),
            pltpu.VMEM((tokens, channels), jnp.float32),
            pltpu.SemaphoreType.DMA((3,)),
        ],
        12 * tokens * channels * hidden_width,
    )


def motion_back(order_row, block, grad_zed, zed, query, key, value, time_out, motion_in, small, position, bias, vectors, proj, attn):
    tokens, channels = zed.shape
    group_len = bias.shape[0]
    leads = [5 + 4 * block, 2 + 4 * block, 3 + 4 * block, 4 + 4 * block] + ([0] if motion_in is not None else [])
    last = motion_in is not None
    frames = 4
    own = channels // frames

    def body(order_ref, ins, groups, outs, scratch):
        grad_ref, zed_ref, query_ref, key_ref, value_ref, time_ref, pos_ref, bias_ref, vec_ref, small_in = ins[:10]
        out_ref, d_all, small_ref = outs
        weight, grad_att, grad_q, grad_k, grad_v, sem = scratch
        for slot, lead in enumerate(leads):
            pair_load(order_ref, groups, lead, weight.at[slot], sem.at[slot])
        rows = rows_of(vec_ref)
        vec = [rows[1 + block], rows[5 + block]]

        def put(slot, value):
            low_value = to_low(value)
            for shard in range(frames):
                d_all[shard, slot * own : (slot + 1) * own, :] = low_value[shard * own : (shard + 1) * own]

        grad_low = to_low(grad_ref[...])
        put(3, dot_tn(time_ref[...], grad_low))
        finish_load(weight.at[0], sem.at[0])
        grad_att[...] = to_low(dot_nt(grad_low, weight[0]))

        def group(step, carry):
            rows = group_rows(step, group_len)
            attend_back_into(
                query_ref, key_ref, value_ref, grad_att, bias_ref[...], (grad_q, grad_k, grad_v), rows, rows
            )
            return carry

        lax.fori_loop(0, tokens // group_len, group, 0)
        normed, inv_std = layer_normed(zed_ref[...])
        low = to_low(normed * vec[0] + vec[1] + pos_ref[...])
        grad_ln = None
        for slot, member in ((1, grad_q), (2, grad_k), (3, grad_v)):
            member_low = to_low(member[...])
            put(slot - 1, dot_tn(low, member_low))
            finish_load(weight.at[slot], sem.at[slot])
            part = dot_nt(member_low, weight[slot])
            grad_ln = part if grad_ln is None else grad_ln + part
        total = grad_ref[...] + layer_back(grad_ln, normed, inv_std, vec[0])
        before = rows_of(small_in)
        mine = [
            jnp.sum(grad_ref[...], axis=0, keepdims=True),
            jnp.sum(grad_ln * normed, axis=0, keepdims=True),
            jnp.sum(grad_ln, axis=0, keepdims=True),
        ]
        filler = [jnp.zeros((1, channels), jnp.float32)]
        if not last:
            small_ref[...] = jnp.concatenate(before[:4] + mine + filler * 9)
            out_ref[...] = total
            return
        total_low = to_low(total)
        put(4, dot_tn(ins[10][...], total_low))
        finish_load(weight.at[4], sem.at[4])
        entered = dot_nt(total_low, weight[4])
        out_ref[...] = to_low(entered)
        shift_sum = jnp.sum(entered, axis=0, keepdims=True)
        product = jnp.sum(entered * ins[10][...].astype(jnp.float32), axis=0, keepdims=True)
        gain_sum = (product - rows[4] * shift_sum) / rows[0]
        gains = [gain_sum, mine[1], before[5], before[2]]
        shifts = [
            shift_sum, mine[2], before[6], before[3], jnp.sum(total, axis=0, keepdims=True),
            mine[0], before[4], before[1], before[0],
        ]
        small_ref[...] = jnp.concatenate(gains + shifts + filler * 3)

    arrays = [grad_zed, zed, query, key, value, time_out, position, bias, vectors, small]
    extra_rows = 16 if last else 0
    outs = [
        b16(tokens, channels) if last else f32(tokens, channels),
        b16(frames, own * len(leads) + extra_rows, channels),
        f32(16, channels),
    ]
    if last:
        arrays.append(motion_in)
    return run_kernel(
        body,
        order_row,
        arrays,
        [proj, attn],
        outs,
        [
            pltpu.VMEM((len(leads), channels, channels), jnp.bfloat16),
            pltpu.VMEM((tokens, channels), jnp.bfloat16),
            pltpu.VMEM((tokens, channels), jnp.float32),
            pltpu.VMEM((tokens, channels), jnp.float32),
            pltpu.VMEM((tokens, channels), jnp.float32),
            pltpu.SemaphoreType.DMA((len(leads),)),
        ],
        18 * tokens * channels * channels,
    )


def part_rows(count, turn):
    units = count // 16
    sizes = [units // 3 + (1 if (part - turn) % 3 < units % 3 else 0) for part in range(3)]
    starts = [16 * sum(sizes[:part]) for part in range(3)]
    return [(start, 16 * size) for start, size in zip(starts, sizes)]


def gather_plan(shards):
    plan = []
    for number, (shape, pieces) in enumerate(shards):
        if len(shape) == 2:
            plan.append((number, None, None, part_rows(shape[0], len(plan))))
            continue
        step = shape[0] // pieces
        for piece in range(pieces):
            if step % 3 == 0:
                third = step // 3
                parts = [(piece * step + part * third, third) for part in range(3)]
                plan.append((number, "lead", None, parts))
            else:
                plan.append((number, "rows", (piece * step, step), part_rows(shape[1], len(plan))))
    return plan


def gather_all(shards, small):
    arrays = [array for array, _ in shards]
    plan = gather_plan([(array.shape, pieces) for array, pieces in shards])
    frames = lax.axis_size("frame")
    count = len(arrays)
    steps = len(plan)
    roles = ((0, 1, 2), (1, 0, 2), (2, 1, 0), (2, 0, 1))

    def kernel(*refs):
        sources, small_ref = refs[:count], refs[count]
        base = count + 1
        targets, small_out = refs[base : base + count], refs[base + count]
        send, recv, small_send, small_recv, own_sem = refs[base + count + 1 :]
        frame, row = lax.axis_index("frame"), lax.axis_index("rows")
        frame_bit, core_bit = frame // 2, frame % 2
        across = (1 - frame_bit) * 2 + core_bit
        beside = frame_bit * 2 + 1 - core_bit
        corner = (1 - frame_bit) * 2 + 1 - core_bit
        x_bit, z_bit = row % 2, row // 2 % 2
        over_x = row + 1 - 2 * x_bit
        over_z = row + 2 - 4 * z_bit
        over = {
            "y": (across, row),
            "core": (beside, row),
            "corner": (corner, row),
            "x": (frame, over_x),
            "z": (frame, over_z),
        }
        barrier = pltpu.get_barrier_semaphore()
        for place in over.values():
            pl.semaphore_signal(barrier, inc=1, device_id=place, device_id_type=MESH)
        pl.semaphore_wait(barrier, len(over))

        def view(ref, step, part, shard):
            number, kind, leads, parts = plan[step]
            rows = arrays[number].shape[-2]
            begin = 0 if shard is None else pl.multiple_of(shard * rows, 16)
            if kind == "lead":
                first, size = parts[0][0], sum(length for _, length in parts)
                if part is not None:
                    first, size = parts[part]
                where = pl.ds(first, size)
                return ref.at[where] if shard is None else ref.at[where, pl.ds(begin, rows)]
            start, size = (0, rows) if part is None else parts[part]
            where = pl.ds(begin + start, size)
            if kind is None:
                return ref.at[where]
            return ref.at[pl.ds(*leads), where]

        def move(step, part, shard, source, target, way, slot):
            number = plan[step][0]
            return pltpu.make_async_remote_copy(
                src_ref=source,
                dst_ref=view(targets[number], step, part, shard),
                send_sem=send.at[step, slot],
                recv_sem=recv.at[step, slot],
                device_id=over[way],
                device_id_type=MESH,
            )

        smalls = [
            pltpu.make_async_remote_copy(
                src_ref=small_ref,
                dst_ref=small_out.at[frame],
                send_sem=small_send.at[slot],
                recv_sem=small_recv.at[slot],
                device_id=over[way],
                device_id_type=MESH,
            )
            for slot, way in enumerate(("y", "core", "corner"))
        ]
        small_own = pltpu.make_async_copy(small_ref, small_out.at[frame], own_sem.at[0])

        def run(role):
            part_y, part_x, part_z = roles[role]
            forward = role >= 2

            def first(step):
                number = plan[step][0]
                return [
                    move(step, part_y, frame, view(sources[number], step, part_y, None), None, "y", 0),
                    move(step, None, frame, view(sources[number], step, None, None), None, "core", 3),
                ]

            def passed(step, part, way, slot):
                number = plan[step][0]
                return move(
                    step, part, across, view(targets[number], step, part, across), None, way, slot
                )

            started = [first(step) for step in range(steps)]
            for step in range(steps):
                started[step][0].start()
            for copy in smalls:
                copy.start()
            small_own.start()
            for step in range(steps):
                started[step][1].start()
            later = []
            for turn in range(steps + 2):
                if turn < steps:
                    started[turn][0].wait_recv()
                    sends = [passed(turn, part_y, "z", 2), passed(turn, part_y, "core", 4)]
                    if not forward:
                        sends.insert(1, passed(turn, part_y, "x", 1))
                    for copy in sends:
                        copy.start()
                    later.append(sends)
                if 1 <= turn <= steps:
                    step = turn - 1
                    arrival = passed(step, part_z, "z", 2)
                    arrival.wait_recv()
                    sends = [passed(step, part_z, "core", 6)]
                    if forward:
                        sends.insert(0, passed(step, part_z, "x", 1))
                    for copy in sends:
                        copy.start()
                    later.append(sends)
                if turn >= 2:
                    step = turn - 2
                    arrival = passed(step, part_x, "x", 1)
                    arrival.wait_recv()
                    sends = [passed(step, part_x, "core", 5)]
                    for copy in sends:
                        copy.start()
                    later.append(sends)
            for step in range(steps):
                for copy in started[step]:
                    copy.wait_send()
                move(step, None, frame, view(sources[plan[step][0]], step, None, None), None, "core", 3).wait_recv()
                for part, slot in ((part_y, 4), (part_x, 5), (part_z, 6)):
                    passed(step, part, "core", slot).wait_recv()
            for sends in later:
                for copy in sends:
                    copy.wait_send()
            for copy in smalls + [small_own]:
                copy.wait()

        for role in range(4):
            pl.when((z_bit == role // 2) & (x_bit == role % 2))(functools.partial(run, role))

    anywhere = pl.BlockSpec(memory_space=pl.ANY)
    outs = [
        b16(*array.shape[:-2], array.shape[-2] * frames, array.shape[-1]) for array in arrays
    ]
    outs.append(jax.ShapeDtypeStruct((frames,) + small.shape, small.dtype))
    dma = pltpu.SemaphoreType.DMA
    results = pl.pallas_call(
        kernel,
        out_shape=outs,
        in_specs=[anywhere] * (count + 1),
        out_specs=[anywhere] * len(outs),
        scratch_shapes=[
            dma((steps, 7)),
            dma((steps, 7)),
            dma((3,)),
            dma((3,)),
            dma((1,)),
        ],
        compiler_params=pltpu.CompilerParams(collective_id=0, has_side_effects=True),
        cost_estimate=pl.CostEstimate(
            flops=0, bytes_accessed=4096, transcendentals=0
        ),
    )(*arrays, small)
    return ([(whole, own) for whole, own in zip(results[:count], arrays)], results[count])


def reduce_piece(row_devices):
    return max(256, 16 * row_devices)


def reduce_all(parts, row_devices):
    frames, channels = parts[0].shape[0], parts[0].shape[2]
    sizes = [part.shape[1] for part in parts]
    piece = reduce_piece(row_devices)
    count = -(-sum(sizes) // piece)
    total = count * piece
    group = row_devices // 2
    half = piece // 2
    share = half // group

    def kernel(*refs):
        sources = refs[: len(parts)]
        out_ref = refs[len(parts)]
        (
            held, from_core, from_y, from_x, halves, from_z,
            load_sem, core_send, core_recv, y_send, y_recv, x_send, x_recv, z_send, z_recv,
            back_send, back_recv, last_send, last_recv,
        ) = refs[len(parts) + 1 :]
        frame, row = lax.axis_index("frame"), lax.axis_index("rows")
        frame_bit, core_bit = frame // 2, frame % 2
        across = (1 - frame_bit) * 2 + core_bit
        beside = frame_bit * 2 + 1 - core_bit
        corner = (1 - frame_bit) * 2 + 1 - core_bit
        x_bit, level = row % 2, row // 2
        over_x = (frame, row + 1 - 2 * x_bit)
        peers = [(level + step) % group for step in range(1, group)]
        barrier = pltpu.get_barrier_semaphore()
        places = [(beside, row), (across, row), over_x]
        places += [(frame, peer * 2 + x_bit) for peer in peers]
        for place in places:
            pl.semaphore_signal(barrier, inc=1, device_id=place, device_id_type=MESH)
        loads = []
        start = 0
        for number, source in enumerate(sources):
            loads.append(
                pltpu.make_async_copy(
                    source, held.at[:, pl.ds(start, sizes[number])], load_sem.at[number]
                )
            )
            loads[-1].start()
            start = start + sizes[number]
        if start < total:
            held[:, start:, :] = jnp.zeros((frames, total - start, channels), jnp.bfloat16)
        for load in loads:
            load.wait()
        pl.semaphore_wait(barrier, len(places))

        def send(source, target, send_sem, recv_sem, place):
            return pltpu.make_async_remote_copy(
                src_ref=source,
                dst_ref=target,
                send_sem=send_sem,
                recv_sem=recv_sem,
                device_id=place,
                device_id_type=MESH,
            )

        def add(first, second):
            return to_low(first.astype(jnp.float32) + second.astype(jnp.float32))

        def rows(number):
            return pl.ds(number * piece, piece)

        keep_start = pl.multiple_of(x_bit * half, 16)
        give_start = pl.multiple_of((1 - x_bit) * half, 16)

        def over_core(number):
            return [
                send(
                    held.at[shard, rows(number)],
                    from_core.at[slot, rows(number)],
                    core_send.at[number, slot],
                    core_recv.at[number, slot],
                    (beside, row),
                )
                for slot, shard in enumerate((beside, corner))
            ]

        def over_y(number):
            return send(
                held.at[across, rows(number)], from_y.at[rows(number)], y_send.at[number],
                y_recv.at[number], (across, row),
            )

        def along_x(number):
            return send(
                held.at[frame, pl.ds(number * piece + give_start, half)],
                from_x.at[pl.ds(number * half, half)],
                x_send.at[number],
                x_recv.at[number],
                over_x,
            )

        def along_z(number, step):
            peer = peers[step]
            start = pl.multiple_of(number * half + peer * share, 16)
            return send(
                halves.at[pl.ds(start, share)],
                from_z.at[number, step],
                z_send.at[number, step],
                z_recv.at[number, step],
                (frame, peer * 2 + x_bit),
            )

        def own_share(number):
            return pl.ds(
                pl.multiple_of(number * piece + keep_start + level * share, 16), share
            )

        def back_z(number, step):
            return send(
                out_ref.at[own_share(number)], out_ref.at[own_share(number)],
                back_send.at[number, step], back_recv.at[number, step],
                (frame, peers[step] * 2 + x_bit),
            )

        def back_x(number):
            keep = pl.ds(pl.multiple_of(number * piece + keep_start, 16), half)
            return send(
                out_ref.at[keep], out_ref.at[keep], last_send.at[number], last_recv.at[number],
                over_x,
            )

        for number in range(count):
            for copy in over_core(number):
                copy.start()
        for turn in range(count + 4):
            if turn < count:
                for copy in over_core(turn):
                    copy.wait_recv()
                held[across, rows(turn), :] = add(held[across, rows(turn), :], from_core[1, rows(turn), :])
                over_y(turn).start()
                held[frame, rows(turn), :] = add(held[frame, rows(turn), :], from_core[0, rows(turn), :])
            if 0 <= turn - 1 < count:
                number = turn - 1
                over_y(number).wait_recv()
                held[frame, rows(number), :] = add(held[frame, rows(number), :], from_y[rows(number), :])
                along_x(number).start()
            if 0 <= turn - 2 < count:
                number = turn - 2
                along_x(number).wait_recv()
                mine = held[frame, pl.ds(number * piece + keep_start, half), :]
                where = pl.ds(number * half, half)
                halves[where, :] = add(mine, from_x[where, :])
                for step in range(group - 1):
                    along_z(number, step).start()
            if 0 <= turn - 3 < count:
                number = turn - 3
                start = pl.multiple_of(number * half + level * share, 16)
                value = halves[pl.ds(start, share), :].astype(jnp.float32)
                for step in range(group - 1):
                    along_z(number, step).wait_recv()
                    value += from_z[number, step].astype(jnp.float32)
                out_ref[own_share(number), :] = to_low(value)
                for step in range(group - 1):
                    back_z(number, step).start()
            if 0 <= turn - 4 < count:
                number = turn - 4
                for step in range(group - 1):
                    back_z(number, step).wait_recv()
                back_x(number).start()
        for number in range(count):
            back_x(number).wait_recv()
            for copy in over_core(number) + [over_y(number), along_x(number), back_x(number)]:
                copy.wait_send()
            for step in range(group - 1):
                along_z(number, step).wait_send()
                back_z(number, step).wait_send()

    dma = pltpu.SemaphoreType.DMA
    low_type = jnp.bfloat16
    return pl.pallas_call(
        kernel,
        out_shape=b16(total, channels),
        in_specs=[pl.BlockSpec(memory_space=pl.ANY)] * len(parts),
        out_specs=pl.BlockSpec(memory_space=pltpu.VMEM),
        scratch_shapes=[
            pltpu.VMEM((frames, total, channels), low_type),
            pltpu.VMEM((2, total, channels), low_type),
            pltpu.VMEM((total, channels), low_type),
            pltpu.VMEM((total // 2, channels), low_type),
            pltpu.VMEM((total // 2, channels), low_type),
            pltpu.VMEM((count, group - 1, share, channels), low_type),
            dma((len(parts),)),
            dma((count, 2)),
            dma((count, 2)),
            dma((count,)),
            dma((count,)),
            dma((count,)),
            dma((count,)),
            dma((count, group - 1)),
            dma((count, group - 1)),
            dma((count, group - 1)),
            dma((count, group - 1)),
            dma((count,)),
            dma((count,)),
        ],
        compiler_params=pltpu.CompilerParams(
            collective_id=1, has_side_effects=True, vmem_limit_bytes=40 * 2**20
        ),
        cost_estimate=pl.CostEstimate(flops=0, bytes_accessed=4096, transcendentals=0),
    )(*parts)


def on_device(
    latents,
    cotangent,
    timesteps,
    prompt_ids,
    embed_table,
    res_gain,
    res_shift,
    res_conv,
    temb_weight,
    st_gain,
    st_shift,
    st_proj,
    st_attn,
    st_cross_kv,
    st_ff_in,
    st_ff_bias,
    st_ff_out,
    motion_gain,
    motion_shift,
    motion_proj,
    motion_attn,
    motion_ff_in,
    motion_ff_bias,
    motion_ff_out,
):
    frames_here, cell_count, channels = latents.shape
    places = Places(frames_here, channels)
    side = places.side
    cells = side * side
    valid = places.valid.astype(jnp.float32)
    table = group_table(channels)
    count = (places.safe_side * places.safe_side * (channels // GROUPS)).astype(jnp.float32)
    lanes = jnp.arange(128, dtype=jnp.int32)[None, :]
    masks = jnp.where(
        lanes == 0,
        valid[:, None],
        jnp.where(lanes == 1, places.cell_col[:, None] > 0, places.cell_col[:, None] < side - 1),
    ).astype(jnp.float32)
    key_bias = jnp.broadcast_to(((valid - 1.0) * -FAR)[None, :], (8, cells))
    order_row = shard_order()

    own = channels // places.frames
    clip_count, prompt_count = prompt_ids.shape
    own_temb = TEMB // places.frames
    time_low = to_low(jax.nn.silu(time_table(timesteps)))
    time_mine = lax.dynamic_slice_in_dim(time_low, places.frame * own_temb, own_temb, 1)
    time_part = matmul(time_mine, temb_weight)
    small = jnp.concatenate(
        [
            motion_gain.astype(jnp.float32),
            motion_shift.astype(jnp.float32),
            motion_ff_bias.astype(jnp.float32).reshape(-1, own),
            time_part.reshape(-1, own),
        ]
    )
    small_count = small.shape[0]
    small = jnp.pad(small, ((0, -small_count % 8), (0, -own % 128)))
    flat_attn = motion_attn.reshape((-1,) + motion_attn.shape[2:])
    whole, small_all = gather_all(
        [
            (res_conv.reshape((-1,) + res_conv.shape[3:]), 2),
            (st_proj, 1),
            (st_attn, 1),
            (st_cross_kv, 1),
            (st_ff_in, 1),
            (st_ff_out, 1),
            (motion_proj, 1),
            (flat_attn, 1),
            (motion_ff_in, 1),
            (motion_ff_out, 1),
        ],
        small,
    )
    conv_all, sproj_all, sattn_all, cross_all, sffin_all, sffout_all = whole[:6]
    mproj_all, mattn_all, mffin_all, mffout_all = whole[6:]
    small_all = small_all[:, :small_count, :own]
    bias_rows = motion_ff_bias.shape[0] // own
    motion_rows = jnp.transpose(small_all[:, :13], (1, 0, 2)).reshape(13, channels)
    mffbias = small_all[:, 13 : 13 + bias_rows].reshape(1, -1)
    temb_proj = jnp.sum(small_all[:, 13 + bias_rows :], axis=0).reshape(clip_count, channels)
    time_row = lax.dynamic_index_in_dim(temb_proj, places.clip, 0, keepdims=False)

    field = to_low(places.blocks_to_unit(latents))
    grad_unit = to_low(places.blocks_to_unit(cotangent))
    grad_columns = places.blocks_to_columns(cotangent)

    stats = jnp.stack([jnp.broadcast_to(1.0 / count, (channels,)), time_row])
    sffbias = st_ff_bias.astype(jnp.float32).reshape(1, -1)
    vocab_rows = embed_table.shape[0]
    local_ids = prompt_ids - lax.axis_index(("frame", "rows")) * vocab_rows
    ids_table = onehot(local_ids.reshape(-1), vocab_rows)
    context = lax.psum(to_low(matmul(ids_table, embed_table)), ("frame", "rows"))
    context = context.reshape(clip_count, prompt_count, -1)
    context_low = lax.dynamic_index_in_dim(context, places.clip, 0, keepdims=False)
    prompt_pad = -(-prompt_count // 128) * 128
    context_low = jnp.pad(context_low, ((0, prompt_pad - prompt_count), (0, 0)))
    prompt_bias = jnp.where(jnp.arange(prompt_pad) < prompt_count, 0.0, FAR)
    prompt_row = jnp.broadcast_to(prompt_bias[None, :], (8, prompt_pad))
    prompt_col = jnp.broadcast_to(prompt_bias[:, None], (prompt_pad, 128))

    conv_one = conv_forward(
        order_row, side, field, masks, res_gain, res_shift, stats, table, conv_all, 0, None,
        [],
    )
    resid = conv_forward(
        order_row, side, conv_one, masks, res_gain, res_shift, stats, table, conv_all, 1, [field],
        [],
    )
    proj_one, query, key, value, proj_two = self_forward(
        order_row, resid, masks, key_bias, st_gain, st_shift, stats, table, sproj_all, sattn_all
    )
    cross_query, cross_key, cross_value, proj_three, st_out, motion_low = cross_forward(
        order_row, [grad_unit], proj_two, resid, context_low, masks, prompt_row, st_gain, st_shift, motion_rows,
        stats, sffbias, table, sproj_all, sattn_all, cross_all, sffin_all, sffout_all,
    )

    motion_moved = places.unit_to_columns([motion_low])
    st_moved = places.unit_to_columns([to_low(st_out)])
    frame_total = places.frames * frames_here
    position = jnp.asarray(np.tile(frame_table(frame_total, channels), (places.share_total, 1)))
    per_group = max(n for n in range(1, 14) if places.share_total % n == 0)
    cell_of = np.arange(per_group * frame_total) // frame_total
    cell_bias = jnp.asarray(np.where(cell_of[:, None] == cell_of[None, :], 0.0, FAR).astype(np.float32))
    kept = motion_forward(
        order_row, motion_moved, places.pick_table, position, cell_bias, motion_rows, mproj_all,
        mattn_all,
    )
    zeds, motion_in = (kept[:3], kept[11])
    out_columns, grad_zed, d_ff, small_sums, wide_sums = motion_ff(
        order_row, zeds[2], st_moved, places.pick_table, grad_columns, motion_rows, mffbias, mproj_all, mffin_all,
        mffout_all,
    )
    output = places.columns_to_blocks(out_columns)
    d_blocks = [None, None]
    for block in (1, 0):
        grad_zed, d_blocks[block], small_sums = motion_back(
            order_row, block, grad_zed, zeds[block], *kept[3 + 4 * block : 7 + 4 * block],
            motion_in if block == 0 else None, small_sums, position, cell_bias, motion_rows,
            mproj_all, mattn_all,
        )
    grad_motion = grad_zed

    small_rows = jnp.transpose(small_sums[:13].reshape(13, places.frames, own), (1, 0, 2))
    small_rows = jnp.pad(small_rows, ((0, 0), (0, 0), (0, channels - own)))
    bias_sums = wide_sums[0].reshape(places.frames, 1, channels)
    tail = jnp.concatenate([small_rows, bias_sums, jnp.zeros_like(small_rows[:, :2])], axis=1)
    d_first = lax.dynamic_update_slice(d_blocks[0], to_low(tail), (0, 5 * own, 0))

    def over_frame(gradient):
        return lax.psum_scatter(gradient, "frame", scatter_dimension=0, tiled=False)

    ff_mine = over_frame(d_ff)
    ff_sum = lax.psum(ff_mine, "rows").astype(jnp.float32)
    ff_in_grad = jnp.concatenate([ff_sum[i * own : (i + 1) * own] for i in range(4)], axis=1)
    ff_out_grad = ff_sum[4 * own : 8 * own]
    grad_gn = to_low(places.columns_to_unit(grad_motion))
    grad_two, grad_st = cross_backward(
        order_row, grad_gn, grad_unit, st_out, proj_three, proj_two, cross_query, cross_key,
        cross_value, masks, prompt_col, st_gain, st_shift, motion_rows, stats, sffbias, table,
        sproj_all, sattn_all, sffin_all, sffout_all,
    )
    grad_res = self_backward(
        order_row, [ff_mine], grad_two, proj_one, query, key, value, resid, grad_st, masks, st_gain, st_shift,
        stats, table, sproj_all, sattn_all,
    )
    grad_conv = conv_backward(
        order_row, side, grad_res, conv_one, masks, res_gain, res_shift, stats, table, conv_all, 1,
        [],
    )
    grad_field = conv_backward(
        order_row, side, grad_conv, field, masks, res_gain, res_shift, stats, table, conv_all, 0,
        [grad_res],
    )
    input_grad = places.unit_to_blocks(to_low(grad_field)).astype(jnp.float32)

    d_first, grad_field = lax.optimization_barrier((d_first, grad_field))
    attn_sum = reduce_all([d_first, d_blocks[1]], places.rows).astype(jnp.float32)
    zero_sum, one_sum = (attn_sum[: 5 * own + 16], attn_sum[5 * own + 16 : 9 * own + 16])
    attn_grad = jnp.concatenate([zero_sum[: 4 * own], one_sum]).reshape(motion_attn.shape)
    proj_grad = jnp.stack([zero_sum[4 * own : 5 * own], ff_sum[8 * own :]])
    small_sum = zero_sum[5 * own :]
    gain_grad, shift_grad, ff_bias_grad = (small_sum[:4, :own], small_sum[4:13, :own], small_sum[13])

    return (
        output,
        input_grad,
        gain_grad,
        shift_grad,
        proj_grad,
        attn_grad,
        ff_in_grad,
        ff_bias_grad,
        ff_out_grad,
    )


def solution(mesh):
    return jax.shard_map(
        on_device,
        mesh=mesh,
        in_specs=(
            P("frame", "rows", None),
            P("frame", "rows", None),
            P(),
            P(),
            P(("frame", "rows"), None),
            P(),
            P(),
            P(None, None, None, "frame", None),
            P("frame", None),
            P(),
            P(),
            P(None, "frame", None),
            P(None, "frame", None),
            P(None, "frame", None),
            P("frame", None),
            P(),
            P("frame", None),
            P(None, "frame"),
            P(None, "frame"),
            P(None, "frame", None),
            P(None, None, "frame", None),
            P("frame", None),
            P("frame"),
            P("frame", None),
        ),
        out_specs=(
            P("frame", "rows", None),
            P("frame", "rows", None),
            P(None, "frame"),
            P(None, "frame"),
            P(None, "frame", None),
            P(None, None, "frame", None),
            P("frame", None),
            P("frame"),
            P("frame", None),
        ),
        check_vma=False,
    )
```

```python
import functools
import math

import jax
import jax.numpy as jnp
import numpy as np
from jax import lax
from jax.experimental import pallas as pl
from jax.experimental.pallas import tpu as pltpu
from jax.sharding import PartitionSpec as P

HEADS = 8
GROUPS = 32
FF_ST = 2560
TEMB = 1280
SIDE_BIG = 32
SIDE_MID = 24
SIDE_SMALL = 16


HIGHEST = lax.Precision.HIGHEST
EPSILON = 1e-05
FAR = -1e30
MESH = pl.DeviceIdType.MESH
RECORDING = []
HOOK = []
AHEAD = 32


def to_low(value):
    return value.astype(jnp.bfloat16)


def matmul(left, weight):
    return jnp.dot(left, weight, preferred_element_type=jnp.float32)


def matmul_back(gradient, weight):
    return lax.dot_general(
        gradient, weight, (((1,), (1,)), ((), ())), preferred_element_type=jnp.float32
    )


def matmul_left(left, right):
    return lax.dot_general(left, right, (((0,), (0,)), ((), ())), preferred_element_type=jnp.float32)


def token_sum(gradient):
    return jnp.sum(gradient, axis=0)


def clip_layout(row_devices):
    grid_cols = min(8, row_devices // 2)
    grid_rows = row_devices // grid_cols
    sides = (
        [SIDE_BIG] * (3 * (row_devices // 64))
        + [SIDE_MID] * max(1, row_devices // 16)
        + [SIDE_SMALL] * max(1, row_devices // 16)
    )
    layout = []
    offset = 0
    for side in sides:
        layout.append((side, side // grid_rows, side // grid_cols, offset))
        offset = offset + side // grid_rows * (side // grid_cols)
    return (layout, grid_rows, grid_cols)


def time_table(timesteps):
    half_count = TEMB // 2
    frequency = jnp.exp(
        jnp.arange(half_count, dtype=jnp.float32) * (-math.log(10000.0) / half_count)
    )
    angles = timesteps.astype(jnp.float32)[:, None] * frequency[None, :]
    return jnp.concatenate([jnp.cos(angles), jnp.sin(angles)], axis=1)


def frame_table(frames, channels):
    channel = np.arange(channels)
    frequency = np.exp((channel - channel % 2) * (-math.log(10000.0) / channels))
    angles = np.arange(frames)[:, None] * frequency[None, :]
    return np.where((channel % 2 == 0)[None, :], np.sin(angles), np.cos(angles)).astype(np.float32)


def group_table(channels):
    which = np.arange(channels) // (channels // GROUPS)
    return jnp.asarray((which[:, None] == which[None, :]).astype(np.float32))


def onehot(indices, width):
    return (indices[:, None] == jnp.arange(width, dtype=jnp.int32)[None, :]).astype(jnp.bfloat16)


class Places:
    def __init__(self, frames_here, channels):
        self.rows = lax.axis_size("rows")
        self.frames = lax.axis_size("frame")
        self.row = lax.axis_index("rows")
        self.frame = lax.axis_index("frame")
        self.frames_here = frames_here
        self.layout, self.grid_rows, self.grid_cols = clip_layout(self.rows)
        self.clips = len(self.layout)
        self.units = frames_here * self.clips
        assert self.units <= self.rows
        self.channels = channels
        self.side = max(entry[0] for entry in self.layout)
        self.block_max = -(-max(entry[1] * entry[2] for entry in self.layout) // 16) * 16
        self.shares = [-(-entry[1] * entry[2] // self.frames) for entry in self.layout]
        self.share_max = max(self.shares)
        self.share_total = sum(self.shares)
        self.clip = self.row % self.clips
        sides = jnp.array([entry[0] for entry in self.layout], jnp.int32)
        self.my_side = jnp.where(self.row < self.units, sides[self.clip], 0)
        self.safe_side = jnp.maximum(self.my_side, self.grid_rows * self.grid_cols)
        cells = jnp.arange(self.side * self.side, dtype=jnp.int32)
        self.cell_row, self.cell_col = cells // self.side, cells % self.side
        self.valid = (self.cell_row < self.my_side) & (self.cell_col < self.my_side)
        block_rows = sides[self.clip] // self.grid_rows
        block_cols = sides[self.clip] // self.grid_cols
        self.device = self.cell_row // block_rows * self.grid_cols + self.cell_col // block_cols
        self.in_block = self.cell_row % block_rows * block_cols + self.cell_col % block_cols
        shares = jnp.array(self.shares, jnp.int32)
        share = shares[self.clip]
        block_index = jnp.where(self.valid, self.device * self.block_max + self.in_block, -1)
        self.block_table = onehot(block_index, self.rows * self.block_max)
        column_index = (
            (self.in_block // share * self.rows + self.device) * self.share_max
            + self.in_block % share
        )
        column_index = jnp.where(self.valid, column_index, -1)
        self.column_table = onehot(column_index, self.frames * self.rows * self.share_max)
        picks = []
        for number in range(self.clips):
            cell = np.arange(self.shares[number])[:, None]
            when = np.arange(self.frames * frames_here)[None, :]
            source = (
                when // frames_here * self.rows + when % frames_here * self.clips + number
            ) * self.share_max + cell
            picks.append(source.reshape(-1))
        picks = np.concatenate(picks)
        slots = np.arange(self.frames * self.rows * self.share_max)
        self.pick_table = jnp.asarray((picks[:, None] == slots[None, :]).astype(jnp.bfloat16))

    def blocks_by_unit(self, blocks):
        pieces = []
        for side, height, width, offset in self.layout:
            piece = blocks[:, offset : offset + height * width]
            pieces.append(jnp.pad(piece, ((0, 0), (0, self.block_max - height * width), (0, 0))))
        packed = jnp.stack(pieces, axis=1).reshape(self.units, self.block_max, self.channels)
        return jnp.pad(packed, ((0, self.rows - self.units), (0, 0), (0, 0)))

    def blocks_from_units(self, received):
        received = received[: self.units].reshape(
            self.frames_here, self.clips, self.block_max, self.channels
        )
        return jnp.concatenate(
            [
                received[:, number, : entry[1] * entry[2]]
                for number, entry in enumerate(self.layout)
            ],
            axis=1,
        )

    def unit_to_columns(self, fields_low):
        width = sum(field.shape[-1] for field in fields_low)
        joined = jnp.concatenate(fields_low, axis=1)
        send = to_low(matmul_left(self.column_table, joined))
        send = send.reshape(self.frames * self.rows, self.share_max, width)
        received = lax.all_to_all(send, ("frame", "rows"), 0, 0)
        return received.reshape(-1, width)

    def columns_to_unit(self, field_low):
        send = to_low(matmul_left(self.pick_table, field_low))
        send = send.reshape(self.frames * self.rows, self.share_max, self.channels)
        received = lax.all_to_all(send, ("frame", "rows"), 0, 0)
        return matmul(self.column_table, received.reshape(-1, self.channels))

    def blocks_to_columns(self, blocks):
        parts = []
        for number, (side, height, width, offset) in enumerate(self.layout):
            share = self.shares[number]
            part = blocks[:, offset : offset + height * width]
            part = jnp.pad(part, ((0, 0), (0, share * self.frames - height * width), (0, 0)))
            parts.append(part.reshape(self.frames_here, self.frames, share, self.channels))
        send = jnp.transpose(jnp.concatenate(parts, axis=2), (1, 0, 2, 3))
        received = lax.all_to_all(send, "frame", 0, 0)
        received = received.reshape(-1, self.share_total, self.channels)
        return jnp.transpose(received, (1, 0, 2)).reshape(-1, self.channels)

    def columns_to_blocks(self, field_low):
        send = jnp.transpose(field_low.reshape(self.share_total, -1, self.channels), (1, 0, 2))
        send = send.reshape(self.frames, self.frames_here, self.share_total, self.channels)
        received = lax.all_to_all(send, "frame", 0, 0)
        parts = []
        start = 0
        for number, (side, height, width, offset) in enumerate(self.layout):
            share = self.shares[number]
            part = jnp.transpose(received[:, :, start : start + share], (1, 0, 2, 3))
            part = part.reshape(self.frames_here, self.frames * share, self.channels)
            parts.append(part[:, : height * width])
            start = start + share
        return jnp.concatenate(parts, axis=1)


def shard_order():
    frame = lax.axis_index("frame")
    return jnp.stack([frame, frame ^ 1, frame ^ 2, frame ^ 3]).astype(jnp.int32)


def start_load(order_ref, pieces, lead, target, sem):
    whole, own = pieces
    rows = own.shape[-2]
    for number in range(4):
        where = pl.ds(pl.multiple_of(order_ref[number] * rows, 16), rows)
        if lead is None:
            source = own if number == 0 else whole.at[where]
        elif number == 0:
            source = own.at[lead]
        else:
            source = whole.at[lead, where]
        goal = target.at[where] if len(target.shape) == 2 else target.at[:, where]
        pltpu.make_async_copy(source, goal, sem).start()


def pair_load(order_ref, groups, lead, target, sem):
    if lead < 2:
        start_load(order_ref, groups[0], lead, target, sem)
    else:
        start_load(order_ref, groups[1], lead - 2, target, sem)


def finish_load(target, sem):
    pltpu.make_async_copy(target, target, sem).wait()


def run_kernel(body, order_row, arrays, groups, outs, scratch, flops):
    if RECORDING:
        slots = [Slot(out) for out in outs]
        RECORDING[-1].append((body, arrays, groups, outs, scratch, slots))
        return slots
    count, pieces = len(arrays), sum(len(group) for group in groups)
    out_count = len(outs)

    def kernel(*refs):
        held = list(refs[1 + count : 1 + count + pieces])
        grouped = [[held.pop(0) for _ in group] for group in groups]
        outputs = refs[1 + count + pieces : 1 + count + pieces + out_count]
        body(
            refs[0],
            refs[1 : 1 + count],
            grouped,
            outputs,
            refs[1 + count + pieces + out_count :],
        )

    whole = pl.BlockSpec(memory_space=pltpu.VMEM)
    flat = [piece for group in groups for piece in group]
    return pl.pallas_call(
        kernel,
        out_shape=outs,
        in_specs=[pl.BlockSpec(memory_space=pltpu.SMEM)]
        + [whole] * count
        + [pl.BlockSpec(memory_space=pl.ANY)] * pieces,
        out_specs=[whole] * out_count,
        scratch_shapes=scratch,
        compiler_params=pltpu.CompilerParams(vmem_limit_bytes=56 * 2**20),
        cost_estimate=pl.CostEstimate(flops=flops // 1000, bytes_accessed=4096, transcendentals=0),
    )(order_row, *arrays, *flat)


def hook():
    if HOOK:
        HOOK[-1]()


def rows_of(ref):
    value = ref[...].astype(jnp.float32)
    return [value[number : number + 1] for number in range(value.shape[0])]


def f32(*shape):
    return jax.ShapeDtypeStruct(shape, jnp.float32)


def b16(*shape):
    return jax.ShapeDtypeStruct(shape, jnp.bfloat16)


def dot_nn(left, right):
    return jnp.dot(left, right, preferred_element_type=jnp.float32)


def dot_nt(left, right):
    return lax.dot_general(left, right, (((1,), (1,)), ((), ())), preferred_element_type=jnp.float32)


def dot_tn(left, right):
    return lax.dot_general(left, right, (((0,), (0,)), ((), ())), preferred_element_type=jnp.float32)


def spread_means(first, second, table, inv_count):
    rows = jnp.concatenate(
        [
            jnp.sum(first, axis=0, keepdims=True),
            jnp.sum(second, axis=0, keepdims=True),
            jnp.zeros((6, first.shape[1]), jnp.float32),
        ]
    )
    means = jnp.dot(rows, table, precision=HIGHEST, preferred_element_type=jnp.float32) * inv_count
    return (means[0:1], means[1:2])


def group_normed(field, valid, table, inv_count):
    kept = field * valid
    average, square = spread_means(kept, kept * field, table, inv_count)
    inv_std = lax.rsqrt(square - average * average + EPSILON)
    return ((field - average) * inv_std, inv_std)


def group_back(gradient, normed, inv_std, gain, valid, table, inv_count):
    scaled = gradient * gain * valid
    mean_one, mean_two = spread_means(scaled, scaled * normed, table, inv_count)
    return inv_std * (scaled - mean_one - normed * mean_two) * valid


def layer_normed(field):
    centred = field - jnp.mean(field, axis=1, keepdims=True)
    inv_std = lax.rsqrt(jnp.mean(centred * centred, axis=1, keepdims=True) + EPSILON)
    return (centred * inv_std, inv_std)


def layer_back(gradient, normed, inv_std, gain):
    scaled = gradient * gain
    mean_one = jnp.mean(scaled, axis=1, keepdims=True)
    mean_two = jnp.mean(scaled * normed, axis=1, keepdims=True)
    return inv_std * (scaled - mean_one - normed * mean_two)


def half_erf(field):
    return 0.5 + 0.5 * lax.erf(field * (0.5**0.5))


def gelu_slope(field, half):
    return half + field * (jnp.exp(-0.5 * field * field) * (1.0 / math.sqrt(2.0 * math.pi)))


def head_windows(channels):
    width = channels // HEADS
    windows = []
    for head in range(HEADS):
        start = head * width // 128 * 128
        stop = -(-(head + 1) * width // 128) * 128
        windows.append((start, stop, head * width - start, (head + 1) * width - start))
    return windows


def head_mask(window):
    start, stop, low, high = window
    lane = lax.broadcasted_iota(jnp.int32, (1, stop - start), 1)
    return ((lane >= low) & (lane < high)).astype(jnp.float32).astype(jnp.bfloat16)


def attend_into(query_ref, key_ref, value_ref, bias, out_ref, rows):
    channels = query_ref.shape[1]
    factor = (channels // HEADS) ** (-0.5) * math.log2(math.e)
    out_ref[rows, :] = jnp.zeros((query_ref[rows, :].shape[0], channels), jnp.float32)
    for window in head_windows(channels):
        lanes = slice(window[0], window[1])
        mask = head_mask(window)
        scores = dot_nt(query_ref[rows, lanes] * mask, key_ref[rows if bias.shape[0] > 1 else slice(None), lanes])
        scores = scores * factor + bias
        powers = jnp.exp2(scores - jnp.max(scores, axis=1, keepdims=True))
        inverse = 1.0 / jnp.sum(powers, axis=1, keepdims=True)
        values = value_ref[rows if bias.shape[0] > 1 else slice(None), lanes] * mask
        out_ref[rows, lanes] += dot_nn(to_low(powers), values) * inverse
        hook()


def attend_back_into(query_ref, key_ref, value_ref, grad_ref, bias, outs, rows, key_rows):
    channels = query_ref.shape[1]
    scale = (channels // HEADS) ** (-0.5)
    factor = scale * math.log2(math.e)
    for number, out_ref in enumerate(outs):
        size = (rows if number == 0 else key_rows)
        out_ref[size, :] = jnp.zeros(
            ((query_ref if number == 0 else key_ref)[size, :].shape[0], channels), jnp.float32
        )
    for window in head_windows(channels):
        lanes = slice(window[0], window[1])
        mask = head_mask(window)
        queries = query_ref[rows, lanes] * mask
        keys = key_ref[key_rows, lanes] * mask
        grads = grad_ref[rows, lanes] * mask
        scores = dot_nt(keys, queries) * factor + bias
        powers = jnp.exp2(scores - jnp.max(scores, axis=0, keepdims=True))
        probs = powers * (1.0 / jnp.sum(powers, axis=0, keepdims=True))
        grad_probs = dot_nt(value_ref[key_rows, lanes], grads)
        inner = jnp.sum(probs * grad_probs, axis=0, keepdims=True)
        grad_scores = to_low(probs * (grad_probs - inner))
        outs[0][rows, lanes] += dot_tn(grad_scores, keys) * scale
        if len(outs) > 1:
            outs[1][key_rows, lanes] += dot_nn(grad_scores, queries) * scale
            outs[2][key_rows, lanes] += dot_nn(to_low(probs), grads)
        hook()


ALL = slice(None)


def fill_taps(field, masks, pads, side):
    cells = field.shape[0]
    border = jnp.zeros((side, field.shape[1]), jnp.float32)
    left = pltpu.roll(field, 1, 0) * masks[:, 1:2]
    right = pltpu.roll(field, cells - 1, 0) * masks[:, 2:3]
    for number, moved in enumerate((left, field, right)):
        pads[number, :side, :] = border
        pads[number, side : side + cells, :] = moved
        pads[number, side + cells :, :] = border


def conv_rows(gains_ref, shifts_ref, stats_ref, which):
    gains, shifts, stats = rows_of(gains_ref), rows_of(shifts_ref), rows_of(stats_ref)
    return [gains[which], shifts[which], shifts[2 + which], stats[0]]


def conv_forward(order_row, side, field, masks, gains, shifts, stats, table, weights, which, residual, timed):
    cells, channels = field.shape

    def body(order_ref, ins, groups, outs, scratch):
        field_ref, masks_ref, gains_ref, shifts_ref, stats_ref, table_ref = ins[:6]
        weight, pads, sem = scratch
        (out_ref,) = outs
        start_load(order_ref, groups[0], pl.ds(9 * which, 9), weight, sem.at[0])
        masks = masks_ref[...]
        valid = masks[:, 0:1]
        vec = conv_rows(gains_ref, shifts_ref, stats_ref, which)
        normed, _ = group_normed(
            field_ref[...].astype(jnp.float32), valid, table_ref[...], vec[3]
        )
        pre = normed * vec[0] + vec[1]
        act = pre / (1.0 + jnp.exp(-pre)) * valid
        fill_taps(act, masks, pads, side)
        bias = vec[2]
        if timed:
            bias += ins[-1][pl.ds(timed[1] + lax.axis_index("rows") % timed[2], 1), :]
        out_ref[...] = jnp.broadcast_to(bias, (cells, channels))
        if residual:
            out_ref[...] += field_resid(ins)
        finish_load(weight, sem.at[0])

        for step in range(3):
            rows = pl.ds(step * side, cells)
            total = out_ref[...]
            for col in range(3):
                total += dot_nn(to_low(pads[col, rows, :]), weight[step * 3 + col])
            out_ref[...] = total
            hook()

    def field_resid(ins):
        return ins[6][...].astype(jnp.float32)

    arrays = [field, masks, gains, shifts, stats, table] + ([residual[0]] if residual else [])
    arrays += [timed[0]] if timed else []
    return run_kernel(
        body,
        order_row,
        arrays,
        [weights],
        [f32(cells, channels)],
        [
            pltpu.VMEM((9, channels, channels), jnp.bfloat16),
            pltpu.VMEM((3, cells + 2 * side, channels), jnp.float32),
            pltpu.SemaphoreType.DMA((1,)),
        ],
        18 * cells * channels * channels,
    )[0]


def conv_backward(order_row, side, gradient, field, masks, gains, shifts, stats, table, weights, which, extra):
    cells, channels = field.shape

    def body(order_ref, ins, groups, outs, scratch):
        grad_ref, field_ref, masks_ref, gains_ref, shifts_ref, stats_ref, table_ref = ins[:7]
        weight, pads, total_ref, sem = scratch
        (out_ref,) = outs
        start_load(order_ref, groups[0], pl.ds(9 * which, 9), weight, sem.at[0])
        masks = masks_ref[...]
        valid = masks[:, 0:1]
        vec = conv_rows(gains_ref, shifts_ref, stats_ref, which)
        fill_taps(grad_ref[...], masks, pads, side)
        total_ref[...] = jnp.zeros((cells, channels), jnp.float32)
        finish_load(weight, sem.at[0])

        for step in range(3):
            rows = pl.ds(step * side, cells)
            total = total_ref[...]
            for col in range(3):
                total += dot_nt(to_low(pads[col, rows, :]), weight[8 - (step * 3 + col)])
            total_ref[...] = total
            hook()
        normed, inv_std = group_normed(
            field_ref[...].astype(jnp.float32), valid, table_ref[...], vec[3]
        )
        pre = normed * vec[0] + vec[1]
        gate = 1.0 / (1.0 + jnp.exp(-pre))
        grad_pre = total_ref[...] * (gate * (1.0 + pre * (1.0 - gate)))
        result = group_back(
            grad_pre, normed, inv_std, vec[0], valid, table_ref[...], vec[3]
        )
        if extra:
            result += ins[7][...]
        out_ref[...] = result

    return run_kernel(
        body,
        order_row,
        [gradient, field, masks, gains, shifts, stats, table] + list(extra),
        [weights],
        [f32(cells, channels)],
        [
            pltpu.VMEM((9, channels, channels), jnp.bfloat16),
            pltpu.VMEM((3, cells + 2 * side, channels), jnp.float32),
            pltpu.VMEM((cells, channels), jnp.float32),
            pltpu.SemaphoreType.DMA((1,)),
        ],
        18 * cells * channels * channels,
    )[0]


def self_rows(gains_ref, shifts_ref, stats_ref):
    gains, shifts, stats = rows_of(gains_ref), rows_of(shifts_ref), rows_of(stats_ref)
    return [gains[0], shifts[0], shifts[4], gains[1], shifts[1], shifts[5], None, stats[0]]


def self_forward(order_row, resid, masks, bias, gains, shifts, stats, table, proj, attn):
    cells, channels = resid.shape
    needed = (0, 2, 3, 4, 5)

    def body(order_ref, ins, groups, outs, scratch):
        resid_ref, masks_ref, bias_ref, gains_ref, shifts_ref, stats_ref, table_ref = ins
        proj_ref, query_ref, key_ref, value_ref, two_ref = outs
        weight, att, sem = scratch
        for slot, lead in enumerate(needed):
            pair_load(order_ref, groups, lead, weight.at[slot], sem.at[slot])
        vec = self_rows(gains_ref, shifts_ref, stats_ref)
        normed, _ = group_normed(resid_ref[...], masks_ref[:, 0:1], table_ref[...], vec[7])
        low = to_low(normed * vec[0] + vec[1])
        finish_load(weight.at[0], sem.at[0])
        entered = dot_nn(low, weight[0]) + vec[2]
        proj_ref[...] = entered
        normed, _ = layer_normed(entered)
        low = to_low(normed * vec[3] + vec[4])
        for slot, out_ref in ((1, query_ref), (2, key_ref), (3, value_ref)):
            finish_load(weight.at[slot], sem.at[slot])
            out_ref[...] = to_low(dot_nn(low, weight[slot]))
        attend_into(query_ref, key_ref, value_ref, bias_ref[0:1, :], att, ALL)
        finish_load(weight.at[4], sem.at[4])
        two_ref[...] = proj_ref[...] + dot_nn(to_low(att[...]), weight[4]) + vec[5]

    return run_kernel(
        body,
        order_row,
        [resid, masks, bias, gains, shifts, stats, table],
        [proj, attn],
        [f32(cells, channels)] + [b16(cells, channels)] * 3 + [f32(cells, channels)],
        [
            pltpu.VMEM((5, channels, channels), jnp.bfloat16),
            pltpu.VMEM((cells, channels), jnp.float32),
            pltpu.SemaphoreType.DMA((5,)),
        ],
        10 * cells * channels * channels + 4 * cells * cells * channels,
    )


def self_backward(order_row, early, grad_two, proj_one, query, key, value, resid, grad_st, masks, gains, shifts, stats, table, proj, attn):
    cells, channels = resid.shape
    needed = (5, 2, 3, 4, 0)

    def body(order_ref, ins, groups, outs, scratch):
        grad_ref, proj_ref, query_ref, key_ref, value_ref, resid_ref, st_ref, masks_ref, gains_ref, shifts_ref, stats_ref, table_ref = ins
        (out_ref,) = outs
        weight, grad_att, grad_q, grad_k, grad_v, sem = scratch
        for slot, lead in enumerate(needed):
            pair_load(order_ref, groups, lead, weight.at[slot], sem.at[slot])
        vec = self_rows(gains_ref, shifts_ref, stats_ref)
        valid = masks_ref[:, 0:1]
        finish_load(weight.at[0], sem.at[0])
        grad_att[...] = to_low(dot_nt(to_low(grad_ref[...]), weight[0]))
        attend_back_into(
            query_ref, key_ref, value_ref, grad_att, (valid - 1.0) * -FAR,
            (grad_q, grad_k, grad_v), ALL, ALL,
        )
        total = None
        for slot, member in ((1, grad_q), (2, grad_k), (3, grad_v)):
            finish_load(weight.at[slot], sem.at[slot])
            part = dot_nt(to_low(member[...]), weight[slot])
            total = part if total is None else total + part
        normed, inv_std = layer_normed(proj_ref[...])
        grad_one = grad_ref[...] + layer_back(total, normed, inv_std, vec[3])
        finish_load(weight.at[4], sem.at[4])
        grad_gn = dot_nt(to_low(grad_one), weight[4])
        normed, inv_std = group_normed(resid_ref[...], valid, table_ref[...], vec[7])
        out_ref[...] = st_ref[...] + group_back(
            grad_gn, normed, inv_std, vec[0], valid, table_ref[...], vec[7]
        )

    return run_kernel(
        body,
        order_row,
        [grad_two, proj_one, query, key, value, resid, grad_st, masks, gains, shifts, stats, table],
        [proj, attn, early],
        [f32(cells, channels)],
        [
            pltpu.VMEM((5, channels, channels), jnp.bfloat16),
            pltpu.VMEM((cells, channels), jnp.bfloat16),
            pltpu.VMEM((cells, channels), jnp.float32),
            pltpu.VMEM((cells, channels), jnp.float32),
            pltpu.VMEM((cells, channels), jnp.float32),
            pltpu.SemaphoreType.DMA((5,)),
        ],
        10 * cells * channels * channels + 10 * cells * cells * channels,
    )[0]


CHUNK = 512


def cross_rows(gains_ref, shifts_ref, motion_rows_ref, stats_ref):
    gains, shifts = rows_of(gains_ref), rows_of(shifts_ref)
    motion, stats = rows_of(motion_rows_ref), rows_of(stats_ref)
    return [
        gains[2], shifts[2], shifts[6], gains[3], shifts[3], shifts[7], shifts[8],
        motion[0], motion[4], stats[0],
    ]


def cross_forward(order_row, two, resid, context, masks, bias, gains, shifts, motion_rows, stats, wide_bias, table, proj, attn, cross, w_in_all, w_out_all):
    cells, channels = resid.shape
    prompt, width = context.shape

    def body(order_ref, ins, groups, outs, scratch):
        two_ref, resid_ref, context_ref, masks_ref, bias_ref, gains_ref, shifts_ref, motion_rows_ref, stats_ref, wide_ref, table_ref = ins
        query_ref, key_ref, value_ref, three_ref, out_ref, motion_ref = outs
        weight, kv, w_in, w_out, att, low_in, total, sem = scratch
        for slot, lead in enumerate((6, 7, 1)):
            pair_load(order_ref, groups, lead, weight.at[slot], sem.at[slot])
        for slot in range(2):
            start_load(order_ref, groups[2], slot, kv.at[slot], sem.at[3 + slot])
        vec = cross_rows(gains_ref, shifts_ref, motion_rows_ref, stats_ref)
        normed, _ = layer_normed(two_ref[...])
        low = to_low(normed * vec[0] + vec[1])
        finish_load(weight.at[0], sem.at[0])
        query_ref[...] = to_low(dot_nn(low, weight[0]))
        for slot, ref in ((0, key_ref), (1, value_ref)):
            finish_load(kv.at[slot], sem.at[3 + slot])
            ref[...] = to_low(dot_nn(context_ref[...], kv[slot]))
        attend_into(query_ref, key_ref, value_ref, bias_ref[0:1, :], att, ALL)
        start_load(order_ref, groups[3], None, w_in, sem.at[5])
        start_load(order_ref, groups[4], None, w_out, sem.at[6])
        finish_load(weight.at[1], sem.at[1])
        three_ref[...] = two_ref[...] + dot_nn(to_low(att[...]), weight[1]) + vec[2]
        normed, _ = layer_normed(three_ref[...])
        low = to_low(normed * vec[3] + vec[4])
        finish_load(w_in, sem.at[5])
        finish_load(w_out, sem.at[6])
        total[...] = three_ref[...] + vec[5]
        low_in[...] = low

        for step in range(FF_ST // CHUNK):
            lanes = pl.ds(step * CHUNK, CHUNK)
            gates = pl.ds(FF_ST + step * CHUNK, CHUNK)
            hidden = dot_nn(low_in[...], w_in[:, lanes]) + wide_ref[0:1, lanes]
            gate = dot_nn(low_in[...], w_in[:, gates]) + wide_ref[0:1, gates]
            act = to_low(hidden * (gate * half_erf(gate)))
            total[...] += dot_nn(act, w_out[lanes, :])
            hook()
        finish_load(weight.at[2], sem.at[2])
        st_out = dot_nn(to_low(total[...]), weight[2]) + vec[6] + resid_ref[...]
        out_ref[...] = st_out
        normed, _ = group_normed(st_out, masks_ref[:, 0:1], table_ref[...], vec[9])
        motion_ref[...] = to_low(normed * vec[7] + vec[8])

    return run_kernel(
        body,
        order_row,
        [two, resid, context, masks, bias, gains, shifts, motion_rows, stats, wide_bias, table],
        [proj, attn, cross, w_in_all, w_out_all],
        [
            b16(cells, channels),
            b16(prompt, channels),
            b16(prompt, channels),
            f32(cells, channels),
            f32(cells, channels),
            b16(cells, channels),
        ],
        [
            pltpu.VMEM((3, channels, channels), jnp.bfloat16),
            pltpu.VMEM((2, width, channels), jnp.bfloat16),
            pltpu.VMEM((channels, 2 * FF_ST), jnp.bfloat16),
            pltpu.VMEM((FF_ST, channels), jnp.bfloat16),
            pltpu.VMEM((cells, channels), jnp.float32),
            pltpu.VMEM((cells, channels), jnp.bfloat16),
            pltpu.VMEM((cells, channels), jnp.float32),
            pltpu.SemaphoreType.DMA((7,)),
        ],
        2 * cells * channels * (3 * channels + 3 * FF_ST),
    )


def cross_backward(order_row, grad_gn, cot_blocks, block_table, st_out, three, two, query, key, value, masks, bias_col, gains, shifts, motion_rows, stats, wide_bias, table, proj, attn, w_in_all, w_out_all):
    cells, channels = st_out.shape
    prompt = key.shape[0]

    def body(order_ref, ins, groups, outs, scratch):
        gn_ref, cot_ref, blocks_ref, st_ref, three_ref, two_ref, query_ref, key_ref, value_ref, masks_ref, bias_ref, gains_ref, shifts_ref, motion_rows_ref, stats_ref, wide_ref, table_ref = ins
        grad_two_ref, grad_st_ref = outs
        weight, w_in, w_out, low, grad_low, total, grad_att, grad_q, sem = scratch
        pair_load(order_ref, groups, 1, weight.at[0], sem.at[0])
        start_load(order_ref, groups[3], None, w_out, sem.at[4])
        start_load(order_ref, groups[2], None, w_in, sem.at[3])
        pair_load(order_ref, groups, 7, weight.at[1], sem.at[1])
        pair_load(order_ref, groups, 6, weight.at[2], sem.at[2])
        vec = cross_rows(gains_ref, shifts_ref, motion_rows_ref, stats_ref)
        valid = masks_ref[:, 0:1]
        grad_motion = gn_ref[...].astype(jnp.float32)
        normed, inv_std = group_normed(st_ref[...], valid, table_ref[...], vec[9])
        grad_st_ref[...] = dot_nn(blocks_ref[...], cot_ref[...]) + group_back(
            grad_motion, normed, inv_std, vec[7], valid, table_ref[...], vec[9]
        )
        finish_load(weight.at[0], sem.at[0])
        grad_two_ref[...] = dot_nt(to_low(grad_st_ref[...]), weight[0])
        grad_low[...] = to_low(grad_two_ref[...])
        normed, inv_std = layer_normed(three_ref[...])
        low[...] = to_low(normed * vec[3] + vec[4])
        total[...] = jnp.zeros((cells, channels), jnp.float32)
        finish_load(w_out, sem.at[4])
        finish_load(w_in, sem.at[3])

        def chunk(step, carry):
            lanes = pl.ds(pl.multiple_of(step * CHUNK, 128), CHUNK)
            gates = pl.ds(pl.multiple_of(FF_ST + step * CHUNK, 128), CHUNK)
            hidden = dot_nn(low[...], w_in[:, lanes]) + wide_ref[0:1, lanes]
            gate = dot_nn(low[...], w_in[:, gates]) + wide_ref[0:1, gates]
            grad_act = dot_nt(grad_low[...], w_out[lanes, :])
            half = half_erf(gate)
            grad_hidden = to_low(grad_act * (gate * half))
            grad_gate = to_low(grad_act * hidden * gelu_slope(gate, half))
            total[...] += dot_nt(grad_hidden, w_in[:, lanes]) + dot_nt(grad_gate, w_in[:, gates])
            return carry

        lax.fori_loop(0, FF_ST // CHUNK, chunk, 0)
        normed, inv_std = layer_normed(three_ref[...])
        grad_two_ref[...] += layer_back(total[...], normed, inv_std, vec[3])
        finish_load(weight.at[1], sem.at[1])
        grad_att[...] = to_low(dot_nt(to_low(grad_two_ref[...]), weight[1]))
        attend_back_into(
            query_ref, key_ref, value_ref, grad_att, bias_ref[:, 0:1], (grad_q,), ALL, ALL
        )
        finish_load(weight.at[2], sem.at[2])
        grad_ln = dot_nt(to_low(grad_q[...]), weight[2])
        normed, inv_std = layer_normed(two_ref[...])
        grad_two_ref[...] += layer_back(grad_ln, normed, inv_std, vec[0])

    return run_kernel(
        body,
        order_row,
        [grad_gn, cot_blocks, block_table, st_out, three, two, query, key, value, masks, bias_col, gains, shifts, motion_rows, stats, wide_bias, table],
        [proj, attn, w_in_all, w_out_all],
        [f32(cells, channels), f32(cells, channels)],
        [
            pltpu.VMEM((3, channels, channels), jnp.bfloat16),
            pltpu.VMEM((channels, 2 * FF_ST), jnp.bfloat16),
            pltpu.VMEM((FF_ST, channels), jnp.bfloat16),
            pltpu.VMEM((cells, channels), jnp.bfloat16),
            pltpu.VMEM((cells, channels), jnp.bfloat16),
            pltpu.VMEM((cells, channels), jnp.float32),
            pltpu.VMEM((cells, channels), jnp.bfloat16),
            pltpu.VMEM((cells, channels), jnp.float32),
            pltpu.SemaphoreType.DMA((5,)),
        ],
        2 * cells * channels * (3 * channels + 6 * FF_ST),
    )


def group_rows(step, group_len):
    return pl.ds(pl.multiple_of(step * group_len, 16), group_len)


def motion_forward(order_row, moved, picks, position, bias, vectors, proj, attn):
    tokens, channels = position.shape
    group_len = bias.shape[0]

    def body(order_ref, ins, groups, outs, scratch):
        moved_ref, picks_ref, pos_ref, bias_ref, vec_ref = ins
        weight, att, sem = scratch
        for slot, lead in enumerate((0, 2, 3, 4, 5, 6, 7, 8, 9)):
            pair_load(order_ref, groups, lead, weight.at[slot], sem.at[slot])
        rows = rows_of(vec_ref)
        vec = [rows[number] for number in (8, 1, 5, 9, 2, 6, 10)]
        finish_load(weight.at[0], sem.at[0])
        entered = to_low(dot_nn(picks_ref[...], moved_ref[...]))
        outs[11][...] = entered
        outs[0][...] = dot_nn(entered, weight[0]) + vec[0]
        for block in range(2):
            zed_ref, next_ref = outs[block], outs[block + 1]
            qkv = outs[3 + 4 * block : 6 + 4 * block]
            time_ref = outs[6 + 4 * block]
            normed, _ = layer_normed(zed_ref[...])
            low = to_low(normed * vec[1 + 3 * block] + vec[2 + 3 * block] + pos_ref[...])
            for which in range(3):
                slot = 1 + 4 * block + which
                finish_load(weight.at[slot], sem.at[slot])
                qkv[which][...] = to_low(dot_nn(low, weight[slot]))

            def group(step, carry):
                attend_into(*qkv, bias_ref[...], att, group_rows(step, group_len))
                return carry

            lax.fori_loop(0, tokens // group_len, group, 0)
            time_ref[...] = to_low(att[...])
            slot = 4 + 4 * block
            finish_load(weight.at[slot], sem.at[slot])
            next_ref[...] = zed_ref[...] + dot_nn(time_ref[...], weight[slot]) + vec[3 + 3 * block]

    return run_kernel(
        body,
        order_row,
        [moved, picks, position, bias, vectors],
        [proj, attn],
        [f32(tokens, channels)] * 3 + [b16(tokens, channels)] * 9,
        [
            pltpu.VMEM((9, channels, channels), jnp.bfloat16),
            pltpu.VMEM((tokens, channels), jnp.float32),
            pltpu.SemaphoreType.DMA((9,)),
        ],
        18 * tokens * channels * channels,
    )


def motion_ff(order_row, zed, st_moved, picks, cotangent, vectors, bias_start, hidden_width, proj, in_pieces, out_pieces):
    tokens, channels = zed.shape
    frames = 4
    own = channels // frames
    joined = hidden_width // frames + own * (hidden_width // channels) + own
    second, third = own * (hidden_width // channels), joined - own
    assert hidden_width == frames * channels

    def body(order_ref, ins, groups, outs, scratch):
        zed_ref, st_ref, picks_ref, cot_ref, vec_ref = ins
        out_ref, grad_ref, d_all, small_ref, wide_out = outs
        weight, w_in, w_out, pre, low, grad_low, total, sem = scratch
        start_load(order_ref, groups[1], None, w_in, sem.at[0])
        start_load(order_ref, groups[2], None, w_out, sem.at[1])
        start_load(order_ref, groups[0], 1, weight, sem.at[2])
        rows = rows_of(vec_ref)
        vec = [rows[3], rows[7], rows[11], rows[12]]
        normed, inv_std = layer_normed(zed_ref[...])
        low[...] = to_low(normed * vec[0] + vec[1])
        total[...] = zed_ref[...] + vec[2]
        finish_load(w_in, sem.at[0])
        finish_load(w_out, sem.at[1])

        def forward(step, carry):
            lanes = pl.ds(pl.multiple_of(step * channels, 128), channels)
            before = dot_nn(low[...], w_in[:, lanes]) + vec_ref[pl.ds(bias_start + step, 1), :]
            pre[:, lanes] = before
            total[...] += dot_nn(to_low(before * half_erf(before)), w_out[lanes, :])
            return carry

        lax.fori_loop(0, hidden_width // channels, forward, 0)
        finish_load(weight, sem.at[2])
        zed_low = to_low(total[...])
        out_ref[...] = to_low(dot_nn(picks_ref[...], st_ref[...]) + dot_nn(zed_low, weight[...]) + vec[3])
        d_proj = to_low(dot_tn(zed_low, cot_ref[...]))
        for shard in range(frames):
            d_all[shard, third:, :] = d_proj[shard * own : (shard + 1) * own]
        grad_ref[...] = dot_nt(cot_ref[...], weight[...])
        grad_low[...] = to_low(grad_ref[...])
        total[...] = jnp.zeros((tokens, channels), jnp.float32)

        def backward(step, carry):
            lanes = pl.ds(pl.multiple_of(step * channels, 128), channels)
            before = pre[:, lanes]
            half = half_erf(before)
            d_all[step, second:third, :] = to_low(dot_tn(to_low(before * half), grad_low[...]))
            grad_pre = dot_nt(grad_low[...], w_out[lanes, :]) * gelu_slope(before, half)
            wide_out[0:1, lanes] = jnp.sum(grad_pre, axis=0, keepdims=True)
            pre_low = to_low(grad_pre)
            d_in = to_low(dot_tn(low[...], pre_low))
            for shard in range(frames):
                rows_in = pl.ds(pl.multiple_of(step * own, 16), own)
                d_all[shard, rows_in, :] = d_in[shard * own : (shard + 1) * own]
            total[...] += dot_nt(pre_low, w_in[:, lanes])
            return carry

        wide_out[...] = jnp.zeros((8, hidden_width), jnp.float32)
        lax.fori_loop(0, hidden_width // channels, backward, 0)
        normed, inv_std = layer_normed(zed_ref[...])
        grad_ln = total[...]
        small_ref[...] = jnp.concatenate(
            [
                jnp.sum(cot_ref[...].astype(jnp.float32), axis=0, keepdims=True),
                jnp.sum(grad_ref[...], axis=0, keepdims=True),
                jnp.sum(grad_ln * normed, axis=0, keepdims=True),
                jnp.sum(grad_ln, axis=0, keepdims=True),
                jnp.zeros((4, channels), jnp.float32),
            ]
        )
        grad_ref[...] += layer_back(grad_ln, normed, inv_std, vec[0])

    return run_kernel(
        body,
        order_row,
        [zed, st_moved, picks, cotangent, vectors],
        [proj, in_pieces, out_pieces],
        [
            b16(tokens, channels),
            f32(tokens, channels),
            b16(frames, joined, channels),
            f32(8, channels),
            f32(8, hidden_width),
        ],
        [
            pltpu.VMEM((channels, channels), jnp.bfloat16),
            pltpu.VMEM((channels, hidden_width), jnp.bfloat16),
            pltpu.VMEM((hidden_width, channels), jnp.bfloat16),
            pltpu.VMEM((tokens, hidden_width), jnp.float32),
            pltpu.VMEM((tokens, channels), jnp.bfloat16),
            pltpu.VMEM((tokens, channels), jnp.bfloat16),
            pltpu.VMEM((tokens, channels), jnp.float32),
            pltpu.SemaphoreType.DMA((3,)),
        ],
        12 * tokens * channels * hidden_width,
    )


def motion_back(order_row, block, grad_zed, zed, query, key, value, time_out, motion_in, small, position, bias, vectors, proj, attn, early):
    tokens, channels = zed.shape
    group_len = bias.shape[0]
    leads = [5 + 4 * block, 2 + 4 * block, 3 + 4 * block, 4 + 4 * block] + ([0] if motion_in is not None else [])
    last = motion_in is not None
    frames = 4
    own = channels // frames

    def body(order_ref, ins, groups, outs, scratch):
        grad_ref, zed_ref, query_ref, key_ref, value_ref, time_ref, pos_ref, bias_ref, vec_ref, small_in = ins[:10]
        out_ref, d_all, small_ref = outs
        weight, grad_att, grad_q, grad_k, grad_v, sem = scratch
        for slot, lead in enumerate(leads):
            pair_load(order_ref, groups, lead, weight.at[slot], sem.at[slot])
        rows = rows_of(vec_ref)
        vec = [rows[1 + block], rows[5 + block]]

        def put(slot, value):
            low_value = to_low(value)
            for shard in range(frames):
                d_all[shard, slot * own : (slot + 1) * own, :] = low_value[shard * own : (shard + 1) * own]

        grad_low = to_low(grad_ref[...])
        put(3, dot_tn(time_ref[...], grad_low))
        finish_load(weight.at[0], sem.at[0])
        grad_att[...] = to_low(dot_nt(grad_low, weight[0]))

        def group(step, carry):
            rows = group_rows(step, group_len)
            attend_back_into(
                query_ref, key_ref, value_ref, grad_att, bias_ref[...], (grad_q, grad_k, grad_v), rows, rows
            )
            return carry

        lax.fori_loop(0, tokens // group_len, group, 0)
        normed, inv_std = layer_normed(zed_ref[...])
        low = to_low(normed * vec[0] + vec[1] + pos_ref[...])
        grad_ln = None
        for slot, member in ((1, grad_q), (2, grad_k), (3, grad_v)):
            member_low = to_low(member[...])
            put(slot - 1, dot_tn(low, member_low))
            finish_load(weight.at[slot], sem.at[slot])
            part = dot_nt(member_low, weight[slot])
            grad_ln = part if grad_ln is None else grad_ln + part
        total = grad_ref[...] + layer_back(grad_ln, normed, inv_std, vec[0])
        before = rows_of(small_in)
        mine = [
            jnp.sum(grad_ref[...], axis=0, keepdims=True),
            jnp.sum(grad_ln * normed, axis=0, keepdims=True),
            jnp.sum(grad_ln, axis=0, keepdims=True),
        ]
        filler = [jnp.zeros((1, channels), jnp.float32)]
        if not last:
            small_ref[...] = jnp.concatenate(before[:4] + mine + filler * 9)
            out_ref[...] = total
            return
        total_low = to_low(total)
        put(4, dot_tn(ins[10][...], total_low))
        finish_load(weight.at[4], sem.at[4])
        entered = dot_nt(total_low, weight[4])
        out_ref[...] = to_low(entered)
        shift_sum = jnp.sum(entered, axis=0, keepdims=True)
        product = jnp.sum(entered * ins[10][...].astype(jnp.float32), axis=0, keepdims=True)
        gain_sum = (product - rows[4] * shift_sum) / rows[0]
        gains = [gain_sum, mine[1], before[5], before[2]]
        shifts = [
            shift_sum, mine[2], before[6], before[3], jnp.sum(total, axis=0, keepdims=True),
            mine[0], before[4], before[1], before[0],
        ]
        small_ref[...] = jnp.concatenate(gains + shifts + filler * 3)

    arrays = [grad_zed, zed, query, key, value, time_out, position, bias, vectors, small]
    extra_rows = 16 if last else 0
    outs = [
        b16(tokens, channels) if last else f32(tokens, channels),
        b16(frames, own * len(leads) + extra_rows, channels),
        f32(16, channels),
    ]
    if last:
        arrays.append(motion_in)
    return run_kernel(
        body,
        order_row,
        arrays,
        [proj, attn, early],
        outs,
        [
            pltpu.VMEM((len(leads), channels, channels), jnp.bfloat16),
            pltpu.VMEM((tokens, channels), jnp.bfloat16),
            pltpu.VMEM((tokens, channels), jnp.float32),
            pltpu.VMEM((tokens, channels), jnp.float32),
            pltpu.VMEM((tokens, channels), jnp.float32),
            pltpu.SemaphoreType.DMA((len(leads),)),
        ],
        18 * tokens * channels * channels,
    )


def part_rows(count, turn):
    units = count // 16
    sizes = [units // 3 + (1 if (part - turn) % 3 < units % 3 else 0) for part in range(3)]
    starts = [16 * sum(sizes[:part]) for part in range(3)]
    return [(start, 16 * size) for start, size in zip(starts, sizes)]


def gather_plan(shards):
    plan = []
    for number, (shape, pieces) in enumerate(shards):
        if len(shape) == 2:
            width = shape[1] // pieces
            for piece in range(pieces):
                lanes = (piece * width, width)
                plan.append((number, None, lanes, part_rows(shape[0], len(plan))))
            continue
        step = shape[0] // pieces
        for piece in range(pieces):
            if step % 3 == 0:
                third = step // 3
                parts = [(piece * step + part * third, third) for part in range(3)]
                plan.append((number, "lead", None, parts))
            else:
                plan.append((number, "rows", (piece * step, step), part_rows(shape[1], len(plan))))
    return plan


class Slot:
    def __init__(self, like):
        self.shape, self.dtype = like.shape, like.dtype
        self.ndim, self.size = len(like.shape), math.prod(like.shape)


def forward_all(places, shards, small, latent_blocks, block_table, build, plan_of_hooks):
    arrays = [array for array, _ in shards]
    plan = gather_plan([(array.shape, pieces) for array, pieces in shards])
    frames, row_devices = places.frames, places.rows
    count, steps = len(arrays), len(plan)
    channels = places.channels
    cells = places.side * places.side
    roles = ((0, 1, 2), (1, 0, 2), (2, 1, 0), (2, 0, 1))
    peers_count = row_devices - 1

    wholes = [
        Slot(b16(*array.shape[:-2], array.shape[-2] * frames, array.shape[-1])) for array in arrays
    ]
    field, params = Slot(b16(cells, channels)), Slot(f32(*small.shape))
    RECORDING.append([])
    kept = build(field, params, list(zip(wholes, arrays)))
    stages = RECORDING.pop()

    vmem_inputs = []
    for _, stage_arrays, _, _, _, _ in stages:
        for array in stage_arrays:
            if not isinstance(array, Slot) and all(array is not seen for seen in vmem_inputs):
                vmem_inputs.append(array)
    vmem_outs = [field, params] + list(kept)
    inner = []
    for _, _, _, _, _, slots in stages:
        for slot in slots:
            if all(slot is not seen for seen in vmem_outs):
                inner.append(slot)

    def kernel(*refs):
        refs = list(refs)

        def take(number):
            taken, refs[:] = refs[:number], refs[number:]
            return taken

        sources = take(count)
        small_ref, latent_ref, table_ref = take(3)
        in_refs = take(len(vmem_inputs))
        targets = take(count)
        out_refs = take(len(vmem_outs))
        inner_refs = take(len(inner))
        (
            small_all, latent_all,
            send, recv, small_send, small_recv, lat_send, lat_recv, own_sem,
        ) = refs
        frame, row = lax.axis_index("frame"), lax.axis_index("rows")
        frame_bit, core_bit = frame // 2, frame % 2
        across = (1 - frame_bit) * 2 + core_bit
        beside = frame_bit * 2 + 1 - core_bit
        corner = (1 - frame_bit) * 2 + 1 - core_bit
        x_bit, z_bit = row % 2, row // 2 % 2
        over = {
            "y": (across, row),
            "core": (beside, row),
            "corner": (corner, row),
            "x": (frame, row + 1 - 2 * x_bit),
            "z": (frame, row + 2 - 4 * z_bit),
        }
        peers = [(row + step) % row_devices for step in range(1, row_devices)]
        def remote(source, target, send_sem, recv_sem, place):
            return pltpu.make_async_remote_copy(
                src_ref=source,
                dst_ref=target,
                send_sem=send_sem,
                recv_sem=recv_sem,
                device_id=place,
                device_id_type=MESH,
            )

        barrier = pltpu.get_barrier_semaphore()
        greeted = [over["y"], over["core"], over["corner"]] + [(frame, peer) for peer in peers]
        for place in greeted:
            pl.semaphore_signal(barrier, inc=1, device_id=place, device_id_type=MESH)

        def view(ref, step, part, shard):
            number, kind, leads, parts = plan[step]
            rows = arrays[number].shape[-2]
            begin = 0 if shard is None else pl.multiple_of(shard * rows, 16)
            if kind == "lead":
                first, size = parts[0][0], sum(length for _, length in parts)
                if part is not None:
                    first, size = parts[part]
                where = pl.ds(first, size)
                return ref.at[where] if shard is None else ref.at[where, pl.ds(begin, rows)]
            start, size = (0, rows) if part is None else parts[part]
            where = pl.ds(begin + start, size)
            if kind is None:
                return ref.at[where, pl.ds(*leads)]
            return ref.at[pl.ds(*leads), where]

        def move(step, part, shard, source, way, slot):
            return remote(
                source, view(targets[plan[step][0]], step, part, shard), send.at[step, slot],
                recv.at[step, slot], over[way],
            )

        def fetched(step, part):
            source = view(sources[plan[step][0]], step, part, None)
            return move(step, part, frame, source, "y", 0)

        def shared(step):
            return move(step, None, frame, view(sources[plan[step][0]], step, None, None), "core", 3)

        def passed(step, part, way, slot):
            source = view(targets[plan[step][0]], step, part, across)
            return move(step, part, across, source, way, slot)

        def by_role(action):
            for role in range(4):
                pl.when((z_bit == role // 2) & (x_bit == role % 2))(functools.partial(action, role))

        def start_fetch(role):
            for step in range(min(AHEAD, steps)):
                fetched(step, roles[role][0]).start()

        def act(kind, step):
            def over_y(role):
                part = roles[role][0]
                fetched(step, part).wait_recv()
                if step + AHEAD < steps:
                    fetched(step + AHEAD, part).start()
                passed(step, part, "z", 2).start()
                if role < 2:
                    passed(step, part, "x", 1).start()
                passed(step, part, "core", 4).start()
                if step + AHEAD < steps:
                    shared(step + AHEAD).start()

            def over_z(role):
                part = roles[role][2]
                passed(step, part, "z", 2).wait_recv()
                if role >= 2:
                    passed(step, part, "x", 1).start()
                passed(step, part, "core", 6).start()

            def over_x(role):
                part = roles[role][1]
                passed(step, part, "x", 1).wait_recv()
                passed(step, part, "core", 5).start()

            def finish(role):
                shared(step).wait_recv()
                for part, slot in zip(roles[role], (4, 5, 6)):
                    passed(step, part, "core", slot).wait_recv()

            by_role({"y": over_y, "z": over_z, "x": over_x, "done": finish}[kind])

        def end_sends(role):
            part_y, part_x, part_z = roles[role]
            for step in range(steps):
                fetched(step, part_y).wait_send()
                shared(step).wait_send()
                passed(step, part_y, "z", 2).wait_send()
                passed(step, part_y if role < 2 else part_z, "x", 1).wait_send()
                for part, slot in ((part_y, 4), (part_x, 5), (part_z, 6)):
                    passed(step, part, "core", slot).wait_send()

        smalls = [
            remote(small_ref, small_all.at[frame], small_send.at[slot], small_recv.at[slot], over[way])
            for slot, way in enumerate(("y", "core", "corner"))
        ]
        latent_copies = [
            remote(latent_ref.at[peer], latent_all.at[row], lat_send.at[step], lat_recv.at[step], (frame, peer))
            for step, peer in enumerate(peers)
        ]
        owns = [
            pltpu.make_async_copy(small_ref, small_all.at[frame], own_sem.at[0]),
            pltpu.make_async_copy(latent_ref.at[row], latent_all.at[row], own_sem.at[1]),
        ]
        for copy in owns:
            copy.start()
        pl.semaphore_wait(barrier, len(greeted))
        for copy in smalls + latent_copies:
            copy.start()
        by_role(start_fetch)
        for step in range(min(AHEAD, steps)):
            shared(step).start()

        def run_actions(actions):
            for action in actions:
                act(*action)

        for copy in smalls:
            copy.wait_recv()
        owns[0].wait()
        field_ref, params_ref = out_refs[:2]
        total = small_all[0]
        for number in range(1, frames):
            total += small_all[number]
        params_ref[...] = total
        for copy in latent_copies:
            copy.wait_recv()
        owns[1].wait()
        blocks = latent_all[...].reshape(-1, channels)
        field_ref[...] = to_low(dot_nn(table_ref[...], blocks))

        order = [frame, across, beside, corner]
        known = [(field, field_ref), (params, params_ref)]
        known += list(zip(vmem_inputs, in_refs)) + list(zip(vmem_outs[2:], out_refs[2:]))
        known += list(zip(inner, inner_refs)) + list(zip(wholes, targets)) + list(zip(arrays, sources))

        def ref_of(array):
            return next(ref for held, ref in known if held is array)

        for number, (body, stage_arrays, groups, outs, scratch, slots) in enumerate(stages):
            before, hooks = plan_of_hooks[number]
            run_actions(before)
            pending = list(hooks)

            def hooked():
                if pending:
                    run_actions(pending.pop(0))

            HOOK.append(hooked)

            def stage(*scratch_refs):
                body(
                    order,
                    [ref_of(array) for array in stage_arrays],
                    [[ref_of(array) for array in group] for group in groups],
                    [ref_of(slot) for slot in slots],
                    scratch_refs,
                )

            pl.run_scoped(stage, *scratch)
            HOOK.pop()
            for rest in pending:
                run_actions(rest)
        run_actions(plan_of_hooks[len(stages)][0])
        by_role(end_sends)
        for copy in smalls + latent_copies:
            copy.wait_send()

    anywhere = pl.BlockSpec(memory_space=pl.ANY)
    whole_block = pl.BlockSpec(memory_space=pltpu.VMEM)
    as_shape = lambda slot: jax.ShapeDtypeStruct(slot.shape, slot.dtype)
    dma = pltpu.SemaphoreType.DMA
    results = pl.pallas_call(
        kernel,
        out_shape=[as_shape(slot) for slot in wholes] + [as_shape(slot) for slot in vmem_outs],
        in_specs=[anywhere] * (count + 2) + [whole_block] * (1 + len(vmem_inputs)),
        out_specs=[anywhere] * count + [whole_block] * len(vmem_outs),
        scratch_shapes=[pltpu.VMEM(slot.shape, slot.dtype) for slot in inner]
        + [
            pltpu.VMEM((frames,) + small.shape, jnp.float32),
            pltpu.VMEM(latent_blocks.shape, jnp.bfloat16),
            dma((steps, 7)),
            dma((steps, 7)),
            dma((3,)),
            dma((3,)),
            dma((peers_count,)),
            dma((peers_count,)),
            dma((2,)),
        ],
        compiler_params=pltpu.CompilerParams(
            collective_id=0, has_side_effects=True, vmem_limit_bytes=58 * 2**20
        ),
        cost_estimate=pl.CostEstimate(flops=0, bytes_accessed=4096, transcendentals=0),
    )(*arrays, small, latent_blocks, block_table, *vmem_inputs)
    wholes_out = list(zip(results[:count], arrays))
    return (wholes_out, results[count], results[count + 1], results[count + 2 :])


def reduce_piece(row_devices):
    return max(256, 16 * row_devices)


def reduce_all(parts, summed, row_devices, build, fused, plan_of_hooks, block_table, block_max):
    frames, channels = parts[0].shape[0], parts[0].shape[2]
    sizes = [part.shape[1] for part in parts]
    piece = reduce_piece(row_devices)
    count = -(-sum(sizes) // piece)
    total = count * piece
    more = -(-summed.shape[0] // piece)
    every = count + more
    group = row_devices // 2
    half = piece // 2
    share = half // group
    stages = []
    if fused:
        RECORDING.append(stages)
    (result,) = build()
    if fused:
        RECORDING.pop()
    vmem_inputs, any_inputs, inner = ([] if fused else [result]), [], []

    def note(array, seen):
        if all(array is not other for other in seen):
            seen.append(array)

    for _, stage_arrays, groups, _, _, slots in stages:
        for array in stage_arrays:
            if not isinstance(array, Slot):
                note(array, vmem_inputs)
        for array in [array for held_group in groups for array in held_group]:
            note(array, any_inputs)
        inner += slots

    def kernel(*refs):
        refs = list(refs)

        def take(number):
            taken, refs[:] = refs[:number], refs[number:]
            return taken

        sources = take(len(parts))
        any_refs = take(len(any_inputs))
        (summed_ref, blocks_ref) = take(2)
        in_refs = take(len(vmem_inputs))
        out_ref, moved_ref = take(2)
        inner_refs = take(len(inner))
        known = list(zip(any_inputs, any_refs)) + list(zip(vmem_inputs, in_refs))
        known += list(zip(inner, inner_refs))

        def ref_of(array):
            return next(ref for held_array, ref in known if held_array is array)

        (
            held, ready, leaving, from_core, from_y, from_x, halves, from_z,
            load_sem, core_send, core_recv, y_send, y_recv, x_send, x_recv, z_send, z_recv,
            back_send, back_recv, last_send, last_recv, move_send, move_recv,
        ) = refs
        frame, row = lax.axis_index("frame"), lax.axis_index("rows")
        frame_bit, core_bit = frame // 2, frame % 2
        across = (1 - frame_bit) * 2 + core_bit
        beside = frame_bit * 2 + 1 - core_bit
        corner = (1 - frame_bit) * 2 + 1 - core_bit
        x_bit, level = row % 2, row // 2
        over_x = (frame, row + 1 - 2 * x_bit)
        peers = [(level + step) % group for step in range(1, group)]
        barrier = pltpu.get_barrier_semaphore()
        places = [(beside, row), (across, row), over_x]
        row_peers = [(row + step) % row_devices for step in range(1, row_devices)]
        places = places[:2] + [(frame, peer) for peer in row_peers]
        for place in places:
            pl.semaphore_signal(barrier, inc=1, device_id=place, device_id_type=MESH)
        loads = []
        start = 0
        for number, source in enumerate(sources):
            loads.append(
                pltpu.make_async_copy(
                    source, held.at[:, pl.ds(start, sizes[number])], load_sem.at[number]
                )
            )
            loads[-1].start()
            start = start + sizes[number]
        loads.append(
            pltpu.make_async_copy(
                summed_ref, ready.at[pl.ds(0, summed.shape[0])], load_sem.at[len(sources)]
            )
        )
        loads[-1].start()
        if summed.shape[0] < more * piece:
            ready[summed.shape[0] :, :] = jnp.zeros(
                (more * piece - summed.shape[0], channels), jnp.bfloat16
            )
        if start < total:
            held[:, start:, :] = jnp.zeros((frames, total - start, channels), jnp.bfloat16)
        for load in loads:
            load.wait()
        pl.semaphore_wait(barrier, len(places))

        def send(source, target, send_sem, recv_sem, place):
            return pltpu.make_async_remote_copy(
                src_ref=source,
                dst_ref=target,
                send_sem=send_sem,
                recv_sem=recv_sem,
                device_id=place,
                device_id_type=MESH,
            )

        def add(first, second):
            return to_low(first.astype(jnp.float32) + second.astype(jnp.float32))

        def rows(number):
            return pl.ds(number * piece, piece)

        keep_start = pl.multiple_of(x_bit * half, 16)
        give_start = pl.multiple_of((1 - x_bit) * half, 16)

        def over_core(number):
            return [
                send(
                    held.at[shard, rows(number)],
                    from_core.at[slot, rows(number)],
                    core_send.at[number, slot],
                    core_recv.at[number, slot],
                    (beside, row),
                )
                for slot, shard in enumerate((beside, corner))
            ]

        def over_y(number):
            return send(
                held.at[across, rows(number)], from_y.at[rows(number)], y_send.at[number],
                y_recv.at[number], (across, row),
            )

        def own_rows(number, start):
            if number < count:
                return held.at[frame, pl.ds(number * piece + start, half)]
            return ready.at[pl.ds((number - count) * piece + start, half)]

        def along_x(number):
            return send(
                own_rows(number, give_start),
                from_x.at[pl.ds(number * half, half)],
                x_send.at[number],
                x_recv.at[number],
                over_x,
            )

        def along_z(number, step):
            peer = peers[step]
            start = pl.multiple_of(number * half + peer * share, 16)
            return send(
                halves.at[pl.ds(start, share)],
                from_z.at[number, step],
                z_send.at[number, step],
                z_recv.at[number, step],
                (frame, peer * 2 + x_bit),
            )

        def own_share(number):
            return pl.ds(
                pl.multiple_of(number * piece + keep_start + level * share, 16), share
            )

        def back_z(number, step):
            return send(
                out_ref.at[own_share(number)], out_ref.at[own_share(number)],
                back_send.at[number, step], back_recv.at[number, step],
                (frame, peers[step] * 2 + x_bit),
            )

        def back_x(number):
            keep = pl.ds(pl.multiple_of(number * piece + keep_start, 16), half)
            return send(
                out_ref.at[keep], out_ref.at[keep], last_send.at[number], last_recv.at[number],
                over_x,
            )

        for number in range(count):
            for copy in over_core(number):
                copy.start()

        def stage_core(number):
            for copy in over_core(number):
                copy.wait_recv()
            held[across, rows(number), :] = add(
                held[across, rows(number), :], from_core[1, rows(number), :]
            )
            over_y(number).start()
            held[frame, rows(number), :] = add(
                held[frame, rows(number), :], from_core[0, rows(number), :]
            )

        def stage_y(number):
            if number < count:
                over_y(number).wait_recv()
                held[frame, rows(number), :] = add(
                    held[frame, rows(number), :], from_y[rows(number), :]
                )
            along_x(number).start()

        def stage_x(number):
            along_x(number).wait_recv()
            where = pl.ds(number * half, half)
            halves[where, :] = add(own_rows(number, keep_start)[...], from_x[where, :])
            for step in range(group - 1):
                along_z(number, step).start()

        def stage_z(number):
            start = pl.multiple_of(number * half + level * share, 16)
            value = halves[pl.ds(start, share), :].astype(jnp.float32)
            for step in range(group - 1):
                along_z(number, step).wait_recv()
                value += from_z[number, step].astype(jnp.float32)
            out_ref[own_share(number), :] = to_low(value)
            for step in range(group - 1):
                back_z(number, step).start()

        def stage_back(number):
            for step in range(group - 1):
                back_z(number, step).wait_recv()
            back_x(number).start()

        steps_on = (stage_y, stage_x, stage_z, stage_back)

        def take_turn(turn):
            if turn < count:
                stage_core(turn)
            for late, step in enumerate(steps_on):
                if 0 <= turn - late < more:
                    step(count + turn - late)
                if 0 <= turn - 1 - late < count:
                    step(turn - 1 - late)

        order = [frame, across, beside, corner]
        turns = list(range(max(count + 4, more + 3)))
        for number, (body, stage_arrays, groups, outs, scratch, slots) in enumerate(stages):
            pending = list(plan_of_hooks[number])

            def hooked():
                if pending and pending.pop(0) and turns:
                    take_turn(turns.pop(0))

            HOOK.append(hooked)

            def stage(*scratch_refs):
                body(
                    order,
                    [ref_of(array) for array in stage_arrays],
                    [[ref_of(array) for array in held_group] for held_group in groups],
                    [ref_of(slot) for slot in slots],
                    scratch_refs,
                )

            pl.run_scoped(stage, *scratch)
            HOOK.pop()
        values = to_low(dot_tn(blocks_ref[...], to_low(ref_of(result)[...])))
        leaving[...] = values.reshape(row_devices, block_max, channels)
        moves = [
            send(
                leaving.at[peer], moved_ref.at[row], move_send.at[step], move_recv.at[step],
                (frame, peer),
            )
            for step, peer in enumerate(row_peers)
        ]
        for copy in moves:
            copy.start()
        moved_ref[row] = leaving[row]
        for turn in turns:
            take_turn(turn)
        for copy in moves:
            copy.wait()
        for number in range(count):
            for copy in over_core(number) + [over_y(number)]:
                copy.wait_send()
        for number in range(every):
            back_x(number).wait_recv()
            for copy in [along_x(number), back_x(number)]:
                copy.wait_send()
            for step in range(group - 1):
                along_z(number, step).wait_send()
                back_z(number, step).wait_send()

    dma = pltpu.SemaphoreType.DMA
    low_type = jnp.bfloat16
    anywhere = pl.BlockSpec(memory_space=pl.ANY)
    whole_block = pl.BlockSpec(memory_space=pltpu.VMEM)
    results = pl.pallas_call(
        kernel,
        out_shape=[b16(every * piece, channels), b16(row_devices, block_max, channels)],
        in_specs=[anywhere] * (len(parts) + len(any_inputs) + 1)
        + [whole_block] * (1 + len(vmem_inputs)),
        out_specs=[whole_block] * 2,
        scratch_shapes=[pltpu.VMEM(slot.shape, slot.dtype) for slot in inner]
        + [
            pltpu.VMEM((frames, total, channels), low_type),
            pltpu.VMEM((more * piece, channels), low_type),
            pltpu.VMEM((row_devices, block_max, channels), low_type),
            pltpu.VMEM((2, total, channels), low_type),
            pltpu.VMEM((total, channels), low_type),
            pltpu.VMEM((every * half, channels), low_type),
            pltpu.VMEM((every * half, channels), low_type),
            pltpu.VMEM((every, group - 1, share, channels), low_type),
            dma((len(parts) + 1,)),
            dma((count, 2)),
            dma((count, 2)),
            dma((count,)),
            dma((count,)),
            dma((every,)),
            dma((every,)),
            dma((every, group - 1)),
            dma((every, group - 1)),
            dma((every, group - 1)),
            dma((every, group - 1)),
            dma((every,)),
            dma((every,)),
            dma((row_devices - 1,)),
            dma((row_devices - 1,)),
        ],
        compiler_params=pltpu.CompilerParams(
            collective_id=1, has_side_effects=True, vmem_limit_bytes=60 * 2**20
        ),
        cost_estimate=pl.CostEstimate(flops=0, bytes_accessed=4096, transcendentals=0),
    )(*parts, *any_inputs, summed, block_table, *vmem_inputs)
    return (results[0][:total], results[0][total : total + summed.shape[0]], results[1])


def on_device(
    latents,
    cotangent,
    timesteps,
    prompt_ids,
    embed_table,
    res_gain,
    res_shift,
    res_conv,
    temb_weight,
    st_gain,
    st_shift,
    st_proj,
    st_attn,
    st_cross_kv,
    st_ff_in,
    st_ff_bias,
    st_ff_out,
    motion_gain,
    motion_shift,
    motion_proj,
    motion_attn,
    motion_ff_in,
    motion_ff_bias,
    motion_ff_out,
):
    frames_here, cell_count, channels = latents.shape
    places = Places(frames_here, channels)
    side = places.side
    cells = side * side
    valid = places.valid.astype(jnp.float32)
    table = group_table(channels)
    count = (places.safe_side * places.safe_side * (channels // GROUPS)).astype(jnp.float32)
    lanes = jnp.arange(128, dtype=jnp.int32)[None, :]
    masks = jnp.where(
        lanes == 0,
        valid[:, None],
        jnp.where(lanes == 1, places.cell_col[:, None] > 0, places.cell_col[:, None] < side - 1),
    ).astype(jnp.float32)
    key_bias = jnp.broadcast_to(((valid - 1.0) * -FAR)[None, :], (8, cells))
    order_row = shard_order()

    own = channels // places.frames
    clip_count, prompt_count = prompt_ids.shape
    own_temb = TEMB // places.frames
    time_low = to_low(jax.nn.silu(time_table(timesteps)))
    time_mine = lax.dynamic_slice_in_dim(time_low, places.frame * own_temb, own_temb, 1)
    time_part = matmul(time_mine, temb_weight)
    own_lanes = jnp.arange(channels, dtype=jnp.int32) // own == places.frame
    vectors = jnp.concatenate([motion_gain, motion_shift]).astype(jnp.float32)
    bias_rows = motion_ff_bias.shape[0] * places.frames // channels
    own_bias = jnp.arange(bias_rows)[:, None] == places.frame * (bias_rows // places.frames)
    small = jnp.concatenate(
        [
            jnp.where(own_lanes[None, :], jnp.tile(vectors, (1, places.frames)), 0.0),
            jnp.where(own_bias, motion_ff_bias.astype(jnp.float32).reshape(1, channels), 0.0),
            time_part,
        ]
    )
    small = jnp.pad(small, ((0, -small.shape[0] % 8), (0, 0)))
    flat_attn = motion_attn.reshape((-1,) + motion_attn.shape[2:])
    stats = jnp.broadcast_to(1.0 / count, (8, channels))
    sffbias = st_ff_bias.astype(jnp.float32).reshape(1, -1)
    grad_columns = places.blocks_to_columns(cotangent)
    cot_blocks = lax.all_to_all(places.blocks_by_unit(cotangent), "rows", 0, 0)

    vocab_rows = embed_table.shape[0]
    local_ids = prompt_ids - lax.axis_index(("frame", "rows")) * vocab_rows
    ids_table = onehot(local_ids.reshape(-1), vocab_rows)
    prompt_pad = -(-prompt_count // 16) * 16
    context = lax.psum(to_low(matmul(ids_table, embed_table)), ("frame", "rows"))
    context = context.reshape(clip_count, prompt_count, -1)
    context_low = lax.dynamic_index_in_dim(context, places.clip, 0, keepdims=False)
    context_low = jnp.pad(context_low, ((0, prompt_pad - prompt_count), (0, 0)))
    prompt_bias = jnp.where(jnp.arange(prompt_pad) < prompt_count, 0.0, FAR)
    prompt_row = jnp.broadcast_to(prompt_bias[None, :], (8, prompt_pad))
    prompt_col = jnp.broadcast_to(prompt_bias[:, None], (prompt_pad, 128))

    def build(field, params, whole):
        conv_all, sproj_all, sattn_all, cross_all, sffin_all, sffout_all = whole[:6]
        timed = (params, 13 + bias_rows, clip_count)
        conv_one = conv_forward(
            None, side, field, masks, res_gain, res_shift, stats, table, conv_all, 0, None, timed
        )
        resid = conv_forward(
            None, side, conv_one, masks, res_gain, res_shift, stats, table, conv_all, 1, [field],
            None,
        )
        proj_one, query, key, value, proj_two = self_forward(
            None, resid, masks, key_bias, st_gain, st_shift, stats, table, sproj_all, sattn_all
        )
        return [conv_one, resid, proj_one, query, key, value, proj_two]

    def acts(text):
        ways = {"y": "y", "z": "z", "x": "x", "d": "done"}
        return [(ways[word[0]], int(word[1:] or 0)) for word in text.split()]

    hooks = [
        (acts("y0 y1 z0") + acts("y2 x0 z1") + acts("d0"), [acts("y3 z2"), acts("y4 x2"), []]),
        (acts("x1 z3 d1"), [acts("y5 z4"), [], acts("y6")]),
        (acts("x3 d2 d3"), [acts("x4"), acts("y7"), acts("z5"), [], acts("z6"), acts("y8"), acts("x5"), []]),
        (acts("x6 z7 d4") + acts("y9 x7 z8") + acts("y10 d5 z9") + acts("x8 z10 d6") + acts("d7 x9 x10") + acts("d8 d9 d10"), []),
    ]
    whole, field, params, kept = forward_all(
        places,
        [
            (res_conv.reshape((-1,) + res_conv.shape[3:]), 2),
            (st_proj, 1),
            (st_attn, 1),
            (st_cross_kv, 1),
            (st_ff_in, 1),
            (st_ff_out, 1),
            (motion_proj, 1),
            (flat_attn, 1),
            (motion_ff_in, 1),
            (motion_ff_out, 1),
        ],
        small,
        places.blocks_by_unit(latents),
        places.block_table,
        build,
        hooks,
    )
    conv_all, sproj_all, sattn_all, cross_all, sffin_all, sffout_all = whole[:6]
    mproj_all, mattn_all, mffin_all, mffout_all = whole[6:]
    conv_one, resid, proj_one, query, key, value, proj_two = kept
    motion_rows = params
    cross_query, cross_key, cross_value, proj_three, st_out, motion_low = cross_forward(
        order_row, proj_two, resid, context_low, masks, prompt_row, st_gain, st_shift, params,
        stats, sffbias, table, sproj_all, sattn_all, cross_all, sffin_all, sffout_all,
    )

    motion_moved = places.unit_to_columns([motion_low])
    st_moved = places.unit_to_columns([to_low(st_out)])
    frame_total = places.frames * frames_here
    position = jnp.asarray(np.tile(frame_table(frame_total, channels), (places.share_total, 1)))
    per_group = max(n for n in range(1, 14) if places.share_total % n == 0)
    cell_of = np.arange(per_group * frame_total) // frame_total
    cell_bias = jnp.asarray(np.where(cell_of[:, None] == cell_of[None, :], 0.0, FAR).astype(np.float32))
    kept = motion_forward(
        order_row, motion_moved, places.pick_table, position, cell_bias, motion_rows, mproj_all,
        mattn_all,
    )
    zeds, motion_in = (kept[:3], kept[11])
    out_columns, grad_zed, d_ff, small_sums, wide_sums = motion_ff(
        order_row, zeds[2], st_moved, places.pick_table, grad_columns, motion_rows, 13, channels * bias_rows,
        mproj_all, mffin_all, mffout_all,
    )
    output = places.columns_to_blocks(out_columns)
    d_blocks = [None, None]
    for block in (1, 0):
        grad_zed, d_blocks[block], small_sums = motion_back(
            order_row, block, grad_zed, zeds[block], *kept[3 + 4 * block : 7 + 4 * block],
            motion_in if block == 0 else None, small_sums, position, cell_bias, motion_rows,
            mproj_all, mattn_all, [cot_blocks] if block == 1 else [],
        )
    grad_motion = grad_zed

    small_rows = jnp.transpose(small_sums[:13].reshape(13, places.frames, own), (1, 0, 2))
    small_rows = jnp.pad(small_rows, ((0, 0), (0, 0), (0, channels - own)))
    bias_sums = wide_sums[0].reshape(places.frames, 1, channels)
    tail = jnp.concatenate([small_rows, bias_sums, jnp.zeros_like(small_rows[:, :2])], axis=1)
    d_first = lax.dynamic_update_slice(d_blocks[0], to_low(tail), (0, 5 * own, 0))

    def over_frame(gradient):
        return lax.psum_scatter(gradient, "frame", scatter_dimension=0, tiled=False)

    ff_mine = over_frame(d_ff)
    grad_gn = to_low(places.columns_to_unit(grad_motion))
    grad_two, grad_st = cross_backward(
        order_row, grad_gn, cot_blocks.reshape(-1, channels), places.block_table, st_out, proj_three, proj_two, cross_query, cross_key,
        cross_value, masks, prompt_col, st_gain, st_shift, motion_rows, stats, sffbias, table,
        sproj_all, sattn_all, sffin_all, sffout_all,
    )

    def build_back():
        grad_res = self_backward(
            order_row, [], grad_two, proj_one, query, key, value, resid, grad_st, masks, st_gain,
            st_shift, stats, table, sproj_all, sattn_all,
        )
        grad_conv = conv_backward(
            order_row, side, grad_res, conv_one, masks, res_gain, res_shift, stats, table, conv_all, 1,
            [],
        )
        return [
            conv_backward(
                order_row, side, grad_conv, field, masks, res_gain, res_shift, stats, table, conv_all,
                0, [grad_res],
            )
        ]

    turns_in = [[0, 1, 0, 0, 1, 0, 0, 1], [1, 1, 1], [1, 1, 1]]
    attn_sum, ff_sum, moved = reduce_all(
        [d_first, d_blocks[1]], ff_mine, places.rows, build_back, cells <= 640, turns_in,
        places.block_table, places.block_max,
    )
    attn_sum, ff_sum = (attn_sum.astype(jnp.float32), ff_sum.astype(jnp.float32))
    input_grad = places.blocks_from_units(moved).astype(jnp.float32)
    ff_in_grad = jnp.concatenate([ff_sum[i * own : (i + 1) * own] for i in range(4)], axis=1)
    ff_out_grad = ff_sum[4 * own : 8 * own]
    zero_sum, one_sum = (attn_sum[: 5 * own + 16], attn_sum[5 * own + 16 : 9 * own + 16])
    attn_grad = jnp.concatenate([zero_sum[: 4 * own], one_sum]).reshape(motion_attn.shape)
    proj_grad = jnp.stack([zero_sum[4 * own : 5 * own], ff_sum[8 * own :]])
    small_sum = zero_sum[5 * own :]
    gain_grad, shift_grad, ff_bias_grad = (small_sum[:4, :own], small_sum[4:13, :own], small_sum[13])

    return (
        output,
        input_grad,
        gain_grad,
        shift_grad,
        proj_grad,
        attn_grad,
        ff_in_grad,
        ff_bias_grad,
        ff_out_grad,
    )


def solution(mesh):
    return jax.shard_map(
        on_device,
        mesh=mesh,
        in_specs=(
            P("frame", "rows", None),
            P("frame", "rows", None),
            P(),
            P(),
            P(("frame", "rows"), None),
            P(),
            P(),
            P(None, None, None, "frame", None),
            P("frame", None),
            P(),
            P(),
            P(None, "frame", None),
            P(None, "frame", None),
            P(None, "frame", None),
            P("frame", None),
            P(),
            P("frame", None),
            P(None, "frame"),
            P(None, "frame"),
            P(None, "frame", None),
            P(None, None, "frame", None),
            P("frame", None),
            P("frame"),
            P("frame", None),
        ),
        out_specs=(
            P("frame", "rows", None),
            P("frame", "rows", None),
            P(None, "frame"),
            P(None, "frame"),
            P(None, "frame", None),
            P(None, None, "frame", None),
            P("frame", None),
            P("frame"),
            P("frame", None),
        ),
        check_vma=False,
    )
```

```python
import functools
import math

import jax
import jax.numpy as jnp
import numpy as np
from jax import lax
from jax.experimental import pallas as pl
from jax.experimental.pallas import tpu as pltpu
from jax.sharding import PartitionSpec as P

HEADS = 8
GROUPS = 32
FF_ST = 2560
TEMB = 1280
SIDE_BIG = 32
SIDE_MID = 24
SIDE_SMALL = 16


HIGHEST = lax.Precision.HIGHEST
EPSILON = 1e-05
FAR = -1e30
MESH = pl.DeviceIdType.MESH
RECORDING = []
HOOK = []
AHEAD = 32


def to_low(value):
    return value.astype(jnp.bfloat16)


def matmul(left, weight):
    return jnp.dot(left, weight, preferred_element_type=jnp.float32)


def matmul_back(gradient, weight):
    return lax.dot_general(
        gradient, weight, (((1,), (1,)), ((), ())), preferred_element_type=jnp.float32
    )


def matmul_left(left, right):
    return lax.dot_general(left, right, (((0,), (0,)), ((), ())), preferred_element_type=jnp.float32)


def token_sum(gradient):
    return jnp.sum(gradient, axis=0)


def clip_layout(row_devices):
    grid_cols = min(8, row_devices // 2)
    grid_rows = row_devices // grid_cols
    sides = (
        [SIDE_BIG] * (3 * (row_devices // 64))
        + [SIDE_MID] * max(1, row_devices // 16)
        + [SIDE_SMALL] * max(1, row_devices // 16)
    )
    layout = []
    offset = 0
    for side in sides:
        layout.append((side, side // grid_rows, side // grid_cols, offset))
        offset = offset + side // grid_rows * (side // grid_cols)
    return (layout, grid_rows, grid_cols)


def time_table(timesteps):
    half_count = TEMB // 2
    frequency = jnp.exp(
        jnp.arange(half_count, dtype=jnp.float32) * (-math.log(10000.0) / half_count)
    )
    angles = timesteps.astype(jnp.float32)[:, None] * frequency[None, :]
    return jnp.concatenate([jnp.cos(angles), jnp.sin(angles)], axis=1)


def frame_table(frames, channels):
    channel = np.arange(channels)
    frequency = np.exp((channel - channel % 2) * (-math.log(10000.0) / channels))
    angles = np.arange(frames)[:, None] * frequency[None, :]
    return np.where((channel % 2 == 0)[None, :], np.sin(angles), np.cos(angles)).astype(np.float32)


def group_table(channels):
    which = np.arange(channels) // (channels // GROUPS)
    return jnp.asarray((which[:, None] == which[None, :]).astype(np.float32))


def onehot(indices, width):
    return (indices[:, None] == jnp.arange(width, dtype=jnp.int32)[None, :]).astype(jnp.bfloat16)


class Places:
    def __init__(self, frames_here, channels):
        self.rows = lax.axis_size("rows")
        self.frames = lax.axis_size("frame")
        self.row = lax.axis_index("rows")
        self.frame = lax.axis_index("frame")
        self.frames_here = frames_here
        self.layout, self.grid_rows, self.grid_cols = clip_layout(self.rows)
        self.clips = len(self.layout)
        self.units = frames_here * self.clips
        assert self.units <= self.rows
        self.channels = channels
        self.side = max(entry[0] for entry in self.layout)
        self.block_max = -(-max(entry[1] * entry[2] for entry in self.layout) // 16) * 16
        self.shares = [-(-entry[1] * entry[2] // self.frames) for entry in self.layout]
        self.share_max = max(self.shares)
        self.share_total = sum(self.shares)
        self.clip = self.row % self.clips
        sides = jnp.array([entry[0] for entry in self.layout], jnp.int32)
        self.my_side = jnp.where(self.row < self.units, sides[self.clip], 0)
        self.safe_side = jnp.maximum(self.my_side, self.grid_rows * self.grid_cols)
        cells = jnp.arange(self.side * self.side, dtype=jnp.int32)
        self.cell_row, self.cell_col = cells // self.side, cells % self.side
        self.valid = (self.cell_row < self.my_side) & (self.cell_col < self.my_side)
        block_rows = sides[self.clip] // self.grid_rows
        block_cols = sides[self.clip] // self.grid_cols
        self.device = self.cell_row // block_rows * self.grid_cols + self.cell_col // block_cols
        self.in_block = self.cell_row % block_rows * block_cols + self.cell_col % block_cols
        shares = jnp.array(self.shares, jnp.int32)
        share = shares[self.clip]
        block_index = jnp.where(self.valid, self.device * self.block_max + self.in_block, -1)
        self.block_table = onehot(block_index, self.rows * self.block_max)
        column_index = (
            (self.in_block // share * self.rows + self.device) * self.share_max
            + self.in_block % share
        )
        column_index = jnp.where(self.valid, column_index, -1)
        self.column_table = onehot(column_index, self.frames * self.rows * self.share_max)
        picks = []
        for number in range(self.clips):
            cell = np.arange(self.shares[number])[:, None]
            when = np.arange(self.frames * frames_here)[None, :]
            source = (
                when // frames_here * self.rows + when % frames_here * self.clips + number
            ) * self.share_max + cell
            picks.append(source.reshape(-1))
        picks = np.concatenate(picks)
        slots = np.arange(self.frames * self.rows * self.share_max)
        self.pick_table = jnp.asarray((picks[:, None] == slots[None, :]).astype(jnp.bfloat16))

    def blocks_by_unit(self, blocks):
        pieces = []
        for side, height, width, offset in self.layout:
            piece = blocks[:, offset : offset + height * width]
            pieces.append(jnp.pad(piece, ((0, 0), (0, self.block_max - height * width), (0, 0))))
        packed = jnp.stack(pieces, axis=1).reshape(self.units, self.block_max, self.channels)
        return jnp.pad(packed, ((0, self.rows - self.units), (0, 0), (0, 0)))

    def blocks_from_units(self, received):
        received = received[: self.units].reshape(
            self.frames_here, self.clips, self.block_max, self.channels
        )
        return jnp.concatenate(
            [
                received[:, number, : entry[1] * entry[2]]
                for number, entry in enumerate(self.layout)
            ],
            axis=1,
        )

    def unit_to_columns(self, fields_low):
        width = sum(field.shape[-1] for field in fields_low)
        joined = jnp.concatenate(fields_low, axis=1)
        send = to_low(matmul_left(self.column_table, joined))
        send = send.reshape(self.frames * self.rows, self.share_max, width)
        received = lax.all_to_all(send, ("frame", "rows"), 0, 0)
        return received.reshape(-1, width)

    def columns_to_unit(self, field_low):
        send = to_low(matmul_left(self.pick_table, field_low))
        send = send.reshape(self.frames * self.rows, self.share_max, self.channels)
        received = lax.all_to_all(send, ("frame", "rows"), 0, 0)
        return matmul(self.column_table, received.reshape(-1, self.channels))

    def blocks_to_columns(self, blocks):
        parts = []
        for number, (side, height, width, offset) in enumerate(self.layout):
            share = self.shares[number]
            part = blocks[:, offset : offset + height * width]
            part = jnp.pad(part, ((0, 0), (0, share * self.frames - height * width), (0, 0)))
            parts.append(part.reshape(self.frames_here, self.frames, share, self.channels))
        send = jnp.transpose(jnp.concatenate(parts, axis=2), (1, 0, 2, 3))
        received = lax.all_to_all(send, "frame", 0, 0)
        received = received.reshape(-1, self.share_total, self.channels)
        return jnp.transpose(received, (1, 0, 2)).reshape(-1, self.channels)

    def columns_to_blocks(self, field_low):
        send = jnp.transpose(field_low.reshape(self.share_total, -1, self.channels), (1, 0, 2))
        send = send.reshape(self.frames, self.frames_here, self.share_total, self.channels)
        received = lax.all_to_all(send, "frame", 0, 0)
        parts = []
        start = 0
        for number, (side, height, width, offset) in enumerate(self.layout):
            share = self.shares[number]
            part = jnp.transpose(received[:, :, start : start + share], (1, 0, 2, 3))
            part = part.reshape(self.frames_here, self.frames * share, self.channels)
            parts.append(part[:, : height * width])
            start = start + share
        return jnp.concatenate(parts, axis=1)


def shard_order():
    frame = lax.axis_index("frame")
    return jnp.stack([frame, frame ^ 1, frame ^ 2, frame ^ 3]).astype(jnp.int32)


def start_load(order_ref, pieces, lead, target, sem):
    whole, own = pieces
    rows = own.shape[-2]
    for number in range(4):
        where = pl.ds(pl.multiple_of(order_ref[number] * rows, 16), rows)
        if lead is None:
            source = own if number == 0 else whole.at[where]
        elif number == 0:
            source = own.at[lead]
        else:
            source = whole.at[lead, where]
        goal = target.at[where] if len(target.shape) == 2 else target.at[:, where]
        pltpu.make_async_copy(source, goal, sem).start()


def pair_load(order_ref, groups, lead, target, sem):
    if lead < 2:
        start_load(order_ref, groups[0], lead, target, sem)
    else:
        start_load(order_ref, groups[1], lead - 2, target, sem)


def finish_load(target, sem):
    pltpu.make_async_copy(target, target, sem).wait()


def run_kernel(body, order_row, arrays, groups, outs, scratch, flops):
    if RECORDING:
        slots = [Slot(out) for out in outs]
        RECORDING[-1].append((body, arrays, groups, outs, scratch, slots))
        return slots
    count, pieces = len(arrays), sum(len(group) for group in groups)
    out_count = len(outs)

    def kernel(*refs):
        held = list(refs[1 + count : 1 + count + pieces])
        grouped = [[held.pop(0) for _ in group] for group in groups]
        outputs = refs[1 + count + pieces : 1 + count + pieces + out_count]
        body(
            refs[0],
            refs[1 : 1 + count],
            grouped,
            outputs,
            refs[1 + count + pieces + out_count :],
        )

    whole = pl.BlockSpec(memory_space=pltpu.VMEM)
    flat = [piece for group in groups for piece in group]
    return pl.pallas_call(
        kernel,
        out_shape=outs,
        in_specs=[pl.BlockSpec(memory_space=pltpu.SMEM)]
        + [whole] * count
        + [pl.BlockSpec(memory_space=pl.ANY)] * pieces,
        out_specs=[whole] * out_count,
        scratch_shapes=scratch,
        compiler_params=pltpu.CompilerParams(vmem_limit_bytes=56 * 2**20),
        cost_estimate=pl.CostEstimate(flops=flops // 1000, bytes_accessed=4096, transcendentals=0),
    )(order_row, *arrays, *flat)


def hook():
    if HOOK:
        HOOK[-1]()


def rows_of(ref):
    value = ref[...].astype(jnp.float32)
    return [value[number : number + 1] for number in range(value.shape[0])]


def f32(*shape):
    return jax.ShapeDtypeStruct(shape, jnp.float32)


def b16(*shape):
    return jax.ShapeDtypeStruct(shape, jnp.bfloat16)


def dot_nn(left, right):
    return jnp.dot(left, right, preferred_element_type=jnp.float32)


def dot_nt(left, right):
    return lax.dot_general(left, right, (((1,), (1,)), ((), ())), preferred_element_type=jnp.float32)


def dot_tn(left, right):
    return lax.dot_general(left, right, (((0,), (0,)), ((), ())), preferred_element_type=jnp.float32)


def spread_means(first, second, table, inv_count):
    rows = jnp.concatenate(
        [
            jnp.sum(first, axis=0, keepdims=True),
            jnp.sum(second, axis=0, keepdims=True),
            jnp.zeros((6, first.shape[1]), jnp.float32),
        ]
    )
    means = jnp.dot(rows, table, precision=HIGHEST, preferred_element_type=jnp.float32) * inv_count
    return (means[0:1], means[1:2])


def group_normed(field, valid, table, inv_count):
    kept = field * valid
    average, square = spread_means(kept, kept * field, table, inv_count)
    inv_std = lax.rsqrt(square - average * average + EPSILON)
    return ((field - average) * inv_std, inv_std)


def group_back(gradient, normed, inv_std, gain, valid, table, inv_count):
    scaled = gradient * gain * valid
    mean_one, mean_two = spread_means(scaled, scaled * normed, table, inv_count)
    return inv_std * (scaled - mean_one - normed * mean_two) * valid


def layer_normed(field):
    centred = field - jnp.mean(field, axis=1, keepdims=True)
    inv_std = lax.rsqrt(jnp.mean(centred * centred, axis=1, keepdims=True) + EPSILON)
    return (centred * inv_std, inv_std)


def layer_back(gradient, normed, inv_std, gain):
    scaled = gradient * gain
    mean_one = jnp.mean(scaled, axis=1, keepdims=True)
    mean_two = jnp.mean(scaled * normed, axis=1, keepdims=True)
    return inv_std * (scaled - mean_one - normed * mean_two)


def half_erf(field):
    return 0.5 + 0.5 * lax.erf(field * (0.5**0.5))


def gelu_slope(field, half):
    return half + field * (jnp.exp(-0.5 * field * field) * (1.0 / math.sqrt(2.0 * math.pi)))


def head_windows(channels):
    width = channels // HEADS
    windows = []
    for head in range(HEADS):
        start = head * width // 128 * 128
        stop = -(-(head + 1) * width // 128) * 128
        windows.append((start, stop, head * width - start, (head + 1) * width - start))
    return windows


def head_mask(window):
    start, stop, low, high = window
    lane = lax.broadcasted_iota(jnp.int32, (1, stop - start), 1)
    return ((lane >= low) & (lane < high)).astype(jnp.float32).astype(jnp.bfloat16)


def attend_into(query_ref, key_ref, value_ref, bias, out_ref, rows):
    channels = query_ref.shape[1]
    factor = (channels // HEADS) ** (-0.5) * math.log2(math.e)
    out_ref[rows, :] = jnp.zeros((query_ref[rows, :].shape[0], channels), jnp.float32)
    for window in head_windows(channels):
        lanes = slice(window[0], window[1])
        mask = head_mask(window)
        scores = dot_nt(query_ref[rows, lanes] * mask, key_ref[rows if bias.shape[0] > 1 else slice(None), lanes])
        scores = scores * factor + bias
        powers = jnp.exp2(scores - jnp.max(scores, axis=1, keepdims=True))
        inverse = 1.0 / jnp.sum(powers, axis=1, keepdims=True)
        values = value_ref[rows if bias.shape[0] > 1 else slice(None), lanes] * mask
        out_ref[rows, lanes] += dot_nn(to_low(powers), values) * inverse
        hook()


def attend_back_into(query_ref, key_ref, value_ref, grad_ref, bias, outs, rows, key_rows):
    channels = query_ref.shape[1]
    scale = (channels // HEADS) ** (-0.5)
    factor = scale * math.log2(math.e)
    for number, out_ref in enumerate(outs):
        size = (rows if number == 0 else key_rows)
        out_ref[size, :] = jnp.zeros(
            ((query_ref if number == 0 else key_ref)[size, :].shape[0], channels), jnp.float32
        )
    for window in head_windows(channels):
        lanes = slice(window[0], window[1])
        mask = head_mask(window)
        queries = query_ref[rows, lanes] * mask
        keys = key_ref[key_rows, lanes] * mask
        grads = grad_ref[rows, lanes] * mask
        scores = dot_nt(keys, queries) * factor + bias
        powers = jnp.exp2(scores - jnp.max(scores, axis=0, keepdims=True))
        probs = powers * (1.0 / jnp.sum(powers, axis=0, keepdims=True))
        grad_probs = dot_nt(value_ref[key_rows, lanes], grads)
        inner = jnp.sum(probs * grad_probs, axis=0, keepdims=True)
        grad_scores = to_low(probs * (grad_probs - inner))
        outs[0][rows, lanes] += dot_tn(grad_scores, keys) * scale
        if len(outs) > 1:
            outs[1][key_rows, lanes] += dot_nn(grad_scores, queries) * scale
            outs[2][key_rows, lanes] += dot_nn(to_low(probs), grads)
        hook()


ALL = slice(None)


def fill_taps(field, masks, pads, side):
    cells = field.shape[0]
    border = jnp.zeros((side, field.shape[1]), jnp.float32)
    left = pltpu.roll(field, 1, 0) * masks[:, 1:2]
    right = pltpu.roll(field, cells - 1, 0) * masks[:, 2:3]
    for number, moved in enumerate((left, field, right)):
        pads[number, :side, :] = border
        pads[number, side : side + cells, :] = moved
        pads[number, side + cells :, :] = border


def conv_rows(gains_ref, shifts_ref, stats_ref, which):
    gains, shifts, stats = rows_of(gains_ref), rows_of(shifts_ref), rows_of(stats_ref)
    return [gains[which], shifts[which], shifts[2 + which], stats[0]]


def conv_forward(order_row, side, field, masks, gains, shifts, stats, table, weights, which, residual, timed):
    cells, channels = field.shape

    def body(order_ref, ins, groups, outs, scratch):
        field_ref, masks_ref, gains_ref, shifts_ref, stats_ref, table_ref = ins[:6]
        weight, pads, sem = scratch
        (out_ref,) = outs
        start_load(order_ref, groups[0], pl.ds(9 * which, 9), weight, sem.at[0])
        masks = masks_ref[...]
        valid = masks[:, 0:1]
        vec = conv_rows(gains_ref, shifts_ref, stats_ref, which)
        normed, _ = group_normed(
            field_ref[...].astype(jnp.float32), valid, table_ref[...], vec[3]
        )
        pre = normed * vec[0] + vec[1]
        act = pre / (1.0 + jnp.exp(-pre)) * valid
        fill_taps(act, masks, pads, side)
        bias = vec[2]
        if timed:
            bias += ins[-1][pl.ds(timed[1] + lax.axis_index("rows") % timed[2], 1), :]
        out_ref[...] = jnp.broadcast_to(bias, (cells, channels))
        if residual:
            out_ref[...] += field_resid(ins)
        finish_load(weight, sem.at[0])

        for step in range(3):
            rows = pl.ds(step * side, cells)
            total = out_ref[...]
            for col in range(3):
                total += dot_nn(to_low(pads[col, rows, :]), weight[step * 3 + col])
            out_ref[...] = total
            hook()

    def field_resid(ins):
        return ins[6][...].astype(jnp.float32)

    arrays = [field, masks, gains, shifts, stats, table] + ([residual[0]] if residual else [])
    arrays += [timed[0]] if timed else []
    return run_kernel(
        body,
        order_row,
        arrays,
        [weights],
        [f32(cells, channels)],
        [
            pltpu.VMEM((9, channels, channels), jnp.bfloat16),
            pltpu.VMEM((3, cells + 2 * side, channels), jnp.float32),
            pltpu.SemaphoreType.DMA((1,)),
        ],
        18 * cells * channels * channels,
    )[0]


def conv_backward(order_row, side, gradient, field, masks, gains, shifts, stats, table, weights, which, extra):
    cells, channels = field.shape

    def body(order_ref, ins, groups, outs, scratch):
        grad_ref, field_ref, masks_ref, gains_ref, shifts_ref, stats_ref, table_ref = ins[:7]
        weight, pads, total_ref, sem = scratch
        (out_ref,) = outs
        start_load(order_ref, groups[0], pl.ds(9 * which, 9), weight, sem.at[0])
        masks = masks_ref[...]
        valid = masks[:, 0:1]
        vec = conv_rows(gains_ref, shifts_ref, stats_ref, which)
        fill_taps(grad_ref[...], masks, pads, side)
        total_ref[...] = jnp.zeros((cells, channels), jnp.float32)
        finish_load(weight, sem.at[0])

        for step in range(3):
            rows = pl.ds(step * side, cells)
            total = total_ref[...]
            for col in range(3):
                total += dot_nt(to_low(pads[col, rows, :]), weight[8 - (step * 3 + col)])
            total_ref[...] = total
            hook()
        normed, inv_std = group_normed(
            field_ref[...].astype(jnp.float32), valid, table_ref[...], vec[3]
        )
        pre = normed * vec[0] + vec[1]
        gate = 1.0 / (1.0 + jnp.exp(-pre))
        grad_pre = total_ref[...] * (gate * (1.0 + pre * (1.0 - gate)))
        result = group_back(
            grad_pre, normed, inv_std, vec[0], valid, table_ref[...], vec[3]
        )
        if extra:
            result += ins[7][...]
        out_ref[...] = result

    return run_kernel(
        body,
        order_row,
        [gradient, field, masks, gains, shifts, stats, table] + list(extra),
        [weights],
        [f32(cells, channels)],
        [
            pltpu.VMEM((9, channels, channels), jnp.bfloat16),
            pltpu.VMEM((3, cells + 2 * side, channels), jnp.float32),
            pltpu.VMEM((cells, channels), jnp.float32),
            pltpu.SemaphoreType.DMA((1,)),
        ],
        18 * cells * channels * channels,
    )[0]


def self_rows(gains_ref, shifts_ref, stats_ref):
    gains, shifts, stats = rows_of(gains_ref), rows_of(shifts_ref), rows_of(stats_ref)
    return [gains[0], shifts[0], shifts[4], gains[1], shifts[1], shifts[5], None, stats[0]]


def self_forward(order_row, resid, masks, bias, gains, shifts, stats, table, proj, attn):
    cells, channels = resid.shape
    needed = (0, 2, 3, 4, 5)

    def body(order_ref, ins, groups, outs, scratch):
        resid_ref, masks_ref, bias_ref, gains_ref, shifts_ref, stats_ref, table_ref = ins
        proj_ref, query_ref, key_ref, value_ref, two_ref = outs
        weight, att, sem = scratch
        for slot, lead in enumerate(needed):
            pair_load(order_ref, groups, lead, weight.at[slot], sem.at[slot])
        vec = self_rows(gains_ref, shifts_ref, stats_ref)
        normed, _ = group_normed(resid_ref[...], masks_ref[:, 0:1], table_ref[...], vec[7])
        low = to_low(normed * vec[0] + vec[1])
        finish_load(weight.at[0], sem.at[0])
        entered = dot_nn(low, weight[0]) + vec[2]
        proj_ref[...] = entered
        normed, _ = layer_normed(entered)
        low = to_low(normed * vec[3] + vec[4])
        for slot, out_ref in ((1, query_ref), (2, key_ref), (3, value_ref)):
            finish_load(weight.at[slot], sem.at[slot])
            out_ref[...] = to_low(dot_nn(low, weight[slot]))
        attend_into(query_ref, key_ref, value_ref, bias_ref[0:1, :], att, ALL)
        finish_load(weight.at[4], sem.at[4])
        two_ref[...] = proj_ref[...] + dot_nn(to_low(att[...]), weight[4]) + vec[5]

    return run_kernel(
        body,
        order_row,
        [resid, masks, bias, gains, shifts, stats, table],
        [proj, attn],
        [f32(cells, channels)] + [b16(cells, channels)] * 3 + [f32(cells, channels)],
        [
            pltpu.VMEM((5, channels, channels), jnp.bfloat16),
            pltpu.VMEM((cells, channels), jnp.float32),
            pltpu.SemaphoreType.DMA((5,)),
        ],
        10 * cells * channels * channels + 4 * cells * cells * channels,
    )


def self_backward(order_row, early, grad_two, proj_one, query, key, value, resid, grad_st, masks, gains, shifts, stats, table, proj, attn):
    cells, channels = resid.shape
    needed = (5, 2, 3, 4, 0)

    def body(order_ref, ins, groups, outs, scratch):
        grad_ref, proj_ref, query_ref, key_ref, value_ref, resid_ref, st_ref, masks_ref, gains_ref, shifts_ref, stats_ref, table_ref = ins
        (out_ref,) = outs
        weight, grad_att, grad_q, grad_k, grad_v, sem = scratch
        for slot, lead in enumerate(needed):
            pair_load(order_ref, groups, lead, weight.at[slot], sem.at[slot])
        vec = self_rows(gains_ref, shifts_ref, stats_ref)
        valid = masks_ref[:, 0:1]
        finish_load(weight.at[0], sem.at[0])
        grad_att[...] = to_low(dot_nt(to_low(grad_ref[...]), weight[0]))
        attend_back_into(
            query_ref, key_ref, value_ref, grad_att, (valid - 1.0) * -FAR,
            (grad_q, grad_k, grad_v), ALL, ALL,
        )
        total = None
        for slot, member in ((1, grad_q), (2, grad_k), (3, grad_v)):
            finish_load(weight.at[slot], sem.at[slot])
            part = dot_nt(to_low(member[...]), weight[slot])
            total = part if total is None else total + part
        normed, inv_std = layer_normed(proj_ref[...])
        grad_one = grad_ref[...] + layer_back(total, normed, inv_std, vec[3])
        finish_load(weight.at[4], sem.at[4])
        grad_gn = dot_nt(to_low(grad_one), weight[4])
        normed, inv_std = group_normed(resid_ref[...], valid, table_ref[...], vec[7])
        out_ref[...] = st_ref[...] + group_back(
            grad_gn, normed, inv_std, vec[0], valid, table_ref[...], vec[7]
        )

    return run_kernel(
        body,
        order_row,
        [grad_two, proj_one, query, key, value, resid, grad_st, masks, gains, shifts, stats, table],
        [proj, attn, early],
        [f32(cells, channels)],
        [
            pltpu.VMEM((5, channels, channels), jnp.bfloat16),
            pltpu.VMEM((cells, channels), jnp.bfloat16),
            pltpu.VMEM((cells, channels), jnp.float32),
            pltpu.VMEM((cells, channels), jnp.float32),
            pltpu.VMEM((cells, channels), jnp.float32),
            pltpu.SemaphoreType.DMA((5,)),
        ],
        10 * cells * channels * channels + 10 * cells * cells * channels,
    )[0]


CHUNK = 512


def cross_rows(gains_ref, shifts_ref, motion_rows_ref, stats_ref):
    gains, shifts = rows_of(gains_ref), rows_of(shifts_ref)
    motion, stats = rows_of(motion_rows_ref), rows_of(stats_ref)
    return [
        gains[2], shifts[2], shifts[6], gains[3], shifts[3], shifts[7], shifts[8],
        motion[0], motion[4], stats[0],
    ]


def cross_forward(order_row, two, resid, context, masks, bias, gains, shifts, motion_rows, stats, wide_bias, table, proj, attn, cross, w_in_all, w_out_all):
    cells, channels = resid.shape
    prompt, width = context.shape

    def body(order_ref, ins, groups, outs, scratch):
        two_ref, resid_ref, context_ref, masks_ref, bias_ref, gains_ref, shifts_ref, motion_rows_ref, stats_ref, wide_ref, table_ref = ins
        query_ref, key_ref, value_ref, three_ref, out_ref, motion_ref = outs
        weight, kv, w_in, w_out, att, low_in, total, sem = scratch
        for slot, lead in enumerate((6, 7, 1)):
            pair_load(order_ref, groups, lead, weight.at[slot], sem.at[slot])
        for slot in range(2):
            start_load(order_ref, groups[2], slot, kv.at[slot], sem.at[3 + slot])
        vec = cross_rows(gains_ref, shifts_ref, motion_rows_ref, stats_ref)
        normed, _ = layer_normed(two_ref[...])
        low = to_low(normed * vec[0] + vec[1])
        finish_load(weight.at[0], sem.at[0])
        query_ref[...] = to_low(dot_nn(low, weight[0]))
        for slot, ref in ((0, key_ref), (1, value_ref)):
            finish_load(kv.at[slot], sem.at[3 + slot])
            ref[...] = to_low(dot_nn(context_ref[...], kv[slot]))
        attend_into(query_ref, key_ref, value_ref, bias_ref[0:1, :], att, ALL)
        start_load(order_ref, groups[3], None, w_in, sem.at[5])
        start_load(order_ref, groups[4], None, w_out, sem.at[6])
        finish_load(weight.at[1], sem.at[1])
        three_ref[...] = two_ref[...] + dot_nn(to_low(att[...]), weight[1]) + vec[2]
        normed, _ = layer_normed(three_ref[...])
        low = to_low(normed * vec[3] + vec[4])
        finish_load(w_in, sem.at[5])
        finish_load(w_out, sem.at[6])
        total[...] = three_ref[...] + vec[5]
        low_in[...] = low

        for step in range(FF_ST // CHUNK):
            lanes = pl.ds(step * CHUNK, CHUNK)
            gates = pl.ds(FF_ST + step * CHUNK, CHUNK)
            hidden = dot_nn(low_in[...], w_in[:, lanes]) + wide_ref[0:1, lanes]
            gate = dot_nn(low_in[...], w_in[:, gates]) + wide_ref[0:1, gates]
            act = to_low(hidden * (gate * half_erf(gate)))
            total[...] += dot_nn(act, w_out[lanes, :])
            hook()
        finish_load(weight.at[2], sem.at[2])
        st_out = dot_nn(to_low(total[...]), weight[2]) + vec[6] + resid_ref[...]
        out_ref[...] = st_out
        normed, _ = group_normed(st_out, masks_ref[:, 0:1], table_ref[...], vec[9])
        motion_ref[...] = to_low(normed * vec[7] + vec[8])

    return run_kernel(
        body,
        order_row,
        [two, resid, context, masks, bias, gains, shifts, motion_rows, stats, wide_bias, table],
        [proj, attn, cross, w_in_all, w_out_all],
        [
            b16(cells, channels),
            b16(prompt, channels),
            b16(prompt, channels),
            f32(cells, channels),
            f32(cells, channels),
            b16(cells, channels),
        ],
        [
            pltpu.VMEM((3, channels, channels), jnp.bfloat16),
            pltpu.VMEM((2, width, channels), jnp.bfloat16),
            pltpu.VMEM((channels, 2 * FF_ST), jnp.bfloat16),
            pltpu.VMEM((FF_ST, channels), jnp.bfloat16),
            pltpu.VMEM((cells, channels), jnp.float32),
            pltpu.VMEM((cells, channels), jnp.bfloat16),
            pltpu.VMEM((cells, channels), jnp.float32),
            pltpu.SemaphoreType.DMA((7,)),
        ],
        2 * cells * channels * (3 * channels + 3 * FF_ST),
    )


def cross_backward(order_row, grad_gn, cot_blocks, block_table, st_out, three, two, query, key, value, masks, bias_col, gains, shifts, motion_rows, stats, wide_bias, table, proj, attn, w_in_all, w_out_all):
    cells, channels = st_out.shape
    prompt = key.shape[0]

    def body(order_ref, ins, groups, outs, scratch):
        gn_ref, cot_ref, blocks_ref, st_ref, three_ref, two_ref, query_ref, key_ref, value_ref, masks_ref, bias_ref, gains_ref, shifts_ref, motion_rows_ref, stats_ref, wide_ref, table_ref = ins
        grad_two_ref, grad_st_ref = outs
        weight, w_in, w_out, low, grad_low, total, grad_att, grad_q, sem = scratch
        pair_load(order_ref, groups, 1, weight.at[0], sem.at[0])
        start_load(order_ref, groups[3], None, w_out, sem.at[4])
        start_load(order_ref, groups[2], None, w_in, sem.at[3])
        pair_load(order_ref, groups, 7, weight.at[1], sem.at[1])
        pair_load(order_ref, groups, 6, weight.at[2], sem.at[2])
        vec = cross_rows(gains_ref, shifts_ref, motion_rows_ref, stats_ref)
        valid = masks_ref[:, 0:1]
        grad_motion = gn_ref[...].astype(jnp.float32)
        normed, inv_std = group_normed(st_ref[...], valid, table_ref[...], vec[9])
        grad_st_ref[...] = dot_nn(blocks_ref[...], cot_ref[...]) + group_back(
            grad_motion, normed, inv_std, vec[7], valid, table_ref[...], vec[9]
        )
        finish_load(weight.at[0], sem.at[0])
        grad_two_ref[...] = dot_nt(to_low(grad_st_ref[...]), weight[0])
        grad_low[...] = to_low(grad_two_ref[...])
        normed, inv_std = layer_normed(three_ref[...])
        low[...] = to_low(normed * vec[3] + vec[4])
        total[...] = jnp.zeros((cells, channels), jnp.float32)
        finish_load(w_out, sem.at[4])
        finish_load(w_in, sem.at[3])

        def chunk(step, carry):
            lanes = pl.ds(pl.multiple_of(step * CHUNK, 128), CHUNK)
            gates = pl.ds(pl.multiple_of(FF_ST + step * CHUNK, 128), CHUNK)
            hidden = dot_nn(low[...], w_in[:, lanes]) + wide_ref[0:1, lanes]
            gate = dot_nn(low[...], w_in[:, gates]) + wide_ref[0:1, gates]
            grad_act = dot_nt(grad_low[...], w_out[lanes, :])
            half = half_erf(gate)
            grad_hidden = to_low(grad_act * (gate * half))
            grad_gate = to_low(grad_act * hidden * gelu_slope(gate, half))
            total[...] += dot_nt(grad_hidden, w_in[:, lanes]) + dot_nt(grad_gate, w_in[:, gates])
            return carry

        lax.fori_loop(0, FF_ST // CHUNK, chunk, 0)
        normed, inv_std = layer_normed(three_ref[...])
        grad_two_ref[...] += layer_back(total[...], normed, inv_std, vec[3])
        finish_load(weight.at[1], sem.at[1])
        grad_att[...] = to_low(dot_nt(to_low(grad_two_ref[...]), weight[1]))
        attend_back_into(
            query_ref, key_ref, value_ref, grad_att, bias_ref[:, 0:1], (grad_q,), ALL, ALL
        )
        finish_load(weight.at[2], sem.at[2])
        grad_ln = dot_nt(to_low(grad_q[...]), weight[2])
        normed, inv_std = layer_normed(two_ref[...])
        grad_two_ref[...] += layer_back(grad_ln, normed, inv_std, vec[0])

    return run_kernel(
        body,
        order_row,
        [grad_gn, cot_blocks, block_table, st_out, three, two, query, key, value, masks, bias_col, gains, shifts, motion_rows, stats, wide_bias, table],
        [proj, attn, w_in_all, w_out_all],
        [f32(cells, channels), f32(cells, channels)],
        [
            pltpu.VMEM((3, channels, channels), jnp.bfloat16),
            pltpu.VMEM((channels, 2 * FF_ST), jnp.bfloat16),
            pltpu.VMEM((FF_ST, channels), jnp.bfloat16),
            pltpu.VMEM((cells, channels), jnp.bfloat16),
            pltpu.VMEM((cells, channels), jnp.bfloat16),
            pltpu.VMEM((cells, channels), jnp.float32),
            pltpu.VMEM((cells, channels), jnp.bfloat16),
            pltpu.VMEM((cells, channels), jnp.float32),
            pltpu.SemaphoreType.DMA((5,)),
        ],
        2 * cells * channels * (3 * channels + 6 * FF_ST),
    )


def group_rows(step, group_len):
    return pl.ds(pl.multiple_of(step * group_len, 16), group_len)


def motion_forward(order_row, moved, picks, position, bias, vectors, proj, attn):
    tokens, channels = position.shape
    group_len = bias.shape[0]

    def body(order_ref, ins, groups, outs, scratch):
        moved_ref, picks_ref, pos_ref, bias_ref, vec_ref = ins
        weight, att, sem = scratch
        for slot, lead in enumerate((0, 2, 3, 4, 5, 6, 7, 8, 9)):
            pair_load(order_ref, groups, lead, weight.at[slot], sem.at[slot])
        rows = rows_of(vec_ref)
        vec = [rows[number] for number in (8, 1, 5, 9, 2, 6, 10)]
        finish_load(weight.at[0], sem.at[0])
        entered = to_low(dot_nn(picks_ref[...], moved_ref[...]))
        outs[11][...] = entered
        outs[0][...] = dot_nn(entered, weight[0]) + vec[0]
        for block in range(2):
            zed_ref, next_ref = outs[block], outs[block + 1]
            qkv = outs[3 + 4 * block : 6 + 4 * block]
            time_ref = outs[6 + 4 * block]
            normed, _ = layer_normed(zed_ref[...])
            low = to_low(normed * vec[1 + 3 * block] + vec[2 + 3 * block] + pos_ref[...])
            for which in range(3):
                slot = 1 + 4 * block + which
                finish_load(weight.at[slot], sem.at[slot])
                qkv[which][...] = to_low(dot_nn(low, weight[slot]))

            def group(step, carry):
                attend_into(*qkv, bias_ref[...], att, group_rows(step, group_len))
                return carry

            lax.fori_loop(0, tokens // group_len, group, 0)
            time_ref[...] = to_low(att[...])
            slot = 4 + 4 * block
            finish_load(weight.at[slot], sem.at[slot])
            next_ref[...] = zed_ref[...] + dot_nn(time_ref[...], weight[slot]) + vec[3 + 3 * block]

    return run_kernel(
        body,
        order_row,
        [moved, picks, position, bias, vectors],
        [proj, attn],
        [f32(tokens, channels)] * 3 + [b16(tokens, channels)] * 9,
        [
            pltpu.VMEM((9, channels, channels), jnp.bfloat16),
            pltpu.VMEM((tokens, channels), jnp.float32),
            pltpu.SemaphoreType.DMA((9,)),
        ],
        18 * tokens * channels * channels,
    )


def motion_ff(order_row, zed, st_moved, picks, cotangent, vectors, bias_start, hidden_width, proj, in_pieces, out_pieces):
    tokens, channels = zed.shape
    frames = 4
    own = channels // frames
    joined = hidden_width // frames + own * (hidden_width // channels) + own
    second, third = own * (hidden_width // channels), joined - own
    assert hidden_width == frames * channels

    def body(order_ref, ins, groups, outs, scratch):
        zed_ref, st_ref, picks_ref, cot_ref, vec_ref = ins
        out_ref, grad_ref, d_all, small_ref, wide_out = outs
        weight, w_in, w_out, pre, low, grad_low, total, sem = scratch
        start_load(order_ref, groups[1], None, w_in, sem.at[0])
        start_load(order_ref, groups[2], None, w_out, sem.at[1])
        start_load(order_ref, groups[0], 1, weight, sem.at[2])
        rows = rows_of(vec_ref)
        vec = [rows[3], rows[7], rows[11], rows[12]]
        normed, inv_std = layer_normed(zed_ref[...])
        low[...] = to_low(normed * vec[0] + vec[1])
        total[...] = zed_ref[...] + vec[2]
        finish_load(w_in, sem.at[0])
        finish_load(w_out, sem.at[1])

        def forward(step, carry):
            lanes = pl.ds(pl.multiple_of(step * channels, 128), channels)
            before = dot_nn(low[...], w_in[:, lanes]) + vec_ref[pl.ds(bias_start + step, 1), :]
            pre[:, lanes] = before
            total[...] += dot_nn(to_low(before * half_erf(before)), w_out[lanes, :])
            return carry

        lax.fori_loop(0, hidden_width // channels, forward, 0)
        finish_load(weight, sem.at[2])
        zed_low = to_low(total[...])
        out_ref[...] = to_low(dot_nn(picks_ref[...], st_ref[...]) + dot_nn(zed_low, weight[...]) + vec[3])
        d_proj = to_low(dot_tn(zed_low, cot_ref[...]))
        for shard in range(frames):
            d_all[shard, third:, :] = d_proj[shard * own : (shard + 1) * own]
        grad_ref[...] = dot_nt(cot_ref[...], weight[...])
        grad_low[...] = to_low(grad_ref[...])
        total[...] = jnp.zeros((tokens, channels), jnp.float32)

        def backward(step, carry):
            lanes = pl.ds(pl.multiple_of(step * channels, 128), channels)
            before = pre[:, lanes]
            half = half_erf(before)
            d_all[step, second:third, :] = to_low(dot_tn(to_low(before * half), grad_low[...]))
            grad_pre = dot_nt(grad_low[...], w_out[lanes, :]) * gelu_slope(before, half)
            wide_out[0:1, lanes] = jnp.sum(grad_pre, axis=0, keepdims=True)
            pre_low = to_low(grad_pre)
            d_in = to_low(dot_tn(low[...], pre_low))
            for shard in range(frames):
                rows_in = pl.ds(pl.multiple_of(step * own, 16), own)
                d_all[shard, rows_in, :] = d_in[shard * own : (shard + 1) * own]
            total[...] += dot_nt(pre_low, w_in[:, lanes])
            return carry

        wide_out[...] = jnp.zeros((8, hidden_width), jnp.float32)
        lax.fori_loop(0, hidden_width // channels, backward, 0)
        normed, inv_std = layer_normed(zed_ref[...])
        grad_ln = total[...]
        small_ref[...] = jnp.concatenate(
            [
                jnp.sum(cot_ref[...].astype(jnp.float32), axis=0, keepdims=True),
                jnp.sum(grad_ref[...], axis=0, keepdims=True),
                jnp.sum(grad_ln * normed, axis=0, keepdims=True),
                jnp.sum(grad_ln, axis=0, keepdims=True),
                jnp.zeros((4, channels), jnp.float32),
            ]
        )
        grad_ref[...] += layer_back(grad_ln, normed, inv_std, vec[0])

    return run_kernel(
        body,
        order_row,
        [zed, st_moved, picks, cotangent, vectors],
        [proj, in_pieces, out_pieces],
        [
            b16(tokens, channels),
            f32(tokens, channels),
            b16(frames, joined, channels),
            f32(8, channels),
            f32(8, hidden_width),
        ],
        [
            pltpu.VMEM((channels, channels), jnp.bfloat16),
            pltpu.VMEM((channels, hidden_width), jnp.bfloat16),
            pltpu.VMEM((hidden_width, channels), jnp.bfloat16),
            pltpu.VMEM((tokens, hidden_width), jnp.float32),
            pltpu.VMEM((tokens, channels), jnp.bfloat16),
            pltpu.VMEM((tokens, channels), jnp.bfloat16),
            pltpu.VMEM((tokens, channels), jnp.float32),
            pltpu.SemaphoreType.DMA((3,)),
        ],
        12 * tokens * channels * hidden_width,
    )


def motion_back(order_row, block, grad_zed, zed, query, key, value, time_out, motion_in, small, position, bias, vectors, proj, attn, early):
    tokens, channels = zed.shape
    group_len = bias.shape[0]
    leads = [5 + 4 * block, 2 + 4 * block, 3 + 4 * block, 4 + 4 * block] + ([0] if motion_in is not None else [])
    last = motion_in is not None
    frames = 4
    own = channels // frames

    def body(order_ref, ins, groups, outs, scratch):
        grad_ref, zed_ref, query_ref, key_ref, value_ref, time_ref, pos_ref, bias_ref, vec_ref, small_in = ins[:10]
        out_ref, d_all, small_ref = outs
        weight, grad_att, grad_q, grad_k, grad_v, sem = scratch
        for slot, lead in enumerate(leads):
            pair_load(order_ref, groups, lead, weight.at[slot], sem.at[slot])
        rows = rows_of(vec_ref)
        vec = [rows[1 + block], rows[5 + block]]

        def put(slot, value):
            low_value = to_low(value)
            for shard in range(frames):
                d_all[shard, slot * own : (slot + 1) * own, :] = low_value[shard * own : (shard + 1) * own]

        grad_low = to_low(grad_ref[...])
        put(3, dot_tn(time_ref[...], grad_low))
        finish_load(weight.at[0], sem.at[0])
        grad_att[...] = to_low(dot_nt(grad_low, weight[0]))

        def group(step, carry):
            rows = group_rows(step, group_len)
            attend_back_into(
                query_ref, key_ref, value_ref, grad_att, bias_ref[...], (grad_q, grad_k, grad_v), rows, rows
            )
            return carry

        lax.fori_loop(0, tokens // group_len, group, 0)
        normed, inv_std = layer_normed(zed_ref[...])
        low = to_low(normed * vec[0] + vec[1] + pos_ref[...])
        grad_ln = None
        for slot, member in ((1, grad_q), (2, grad_k), (3, grad_v)):
            member_low = to_low(member[...])
            put(slot - 1, dot_tn(low, member_low))
            finish_load(weight.at[slot], sem.at[slot])
            part = dot_nt(member_low, weight[slot])
            grad_ln = part if grad_ln is None else grad_ln + part
        total = grad_ref[...] + layer_back(grad_ln, normed, inv_std, vec[0])
        before = rows_of(small_in)
        mine = [
            jnp.sum(grad_ref[...], axis=0, keepdims=True),
            jnp.sum(grad_ln * normed, axis=0, keepdims=True),
            jnp.sum(grad_ln, axis=0, keepdims=True),
        ]
        filler = [jnp.zeros((1, channels), jnp.float32)]
        if not last:
            small_ref[...] = jnp.concatenate(before[:4] + mine + filler * 9)
            out_ref[...] = total
            return
        total_low = to_low(total)
        put(4, dot_tn(ins[10][...], total_low))
        finish_load(weight.at[4], sem.at[4])
        entered = dot_nt(total_low, weight[4])
        out_ref[...] = to_low(entered)
        shift_sum = jnp.sum(entered, axis=0, keepdims=True)
        product = jnp.sum(entered * ins[10][...].astype(jnp.float32), axis=0, keepdims=True)
        gain_sum = (product - rows[4] * shift_sum) / rows[0]
        gains = [gain_sum, mine[1], before[5], before[2]]
        shifts = [
            shift_sum, mine[2], before[6], before[3], jnp.sum(total, axis=0, keepdims=True),
            mine[0], before[4], before[1], before[0],
        ]
        small_ref[...] = jnp.concatenate(gains + shifts + filler * 3)

    arrays = [grad_zed, zed, query, key, value, time_out, position, bias, vectors, small]
    extra_rows = 16 if last else 0
    outs = [
        b16(tokens, channels) if last else f32(tokens, channels),
        b16(frames, own * len(leads) + extra_rows, channels),
        f32(16, channels),
    ]
    if last:
        arrays.append(motion_in)
    return run_kernel(
        body,
        order_row,
        arrays,
        [proj, attn, early],
        outs,
        [
            pltpu.VMEM((len(leads), channels, channels), jnp.bfloat16),
            pltpu.VMEM((tokens, channels), jnp.bfloat16),
            pltpu.VMEM((tokens, channels), jnp.float32),
            pltpu.VMEM((tokens, channels), jnp.float32),
            pltpu.VMEM((tokens, channels), jnp.float32),
            pltpu.SemaphoreType.DMA((len(leads),)),
        ],
        18 * tokens * channels * channels,
    )


def part_rows(count, turn):
    units = count // 16
    sizes = [units // 3 + (1 if (part - turn) % 3 < units % 3 else 0) for part in range(3)]
    starts = [16 * sum(sizes[:part]) for part in range(3)]
    return [(start, 16 * size) for start, size in zip(starts, sizes)]


def gather_plan(shards):
    plan = []
    for number, (shape, pieces) in enumerate(shards):
        if len(shape) == 2:
            width = shape[1] // pieces
            for piece in range(pieces):
                lanes = (piece * width, width)
                plan.append((number, None, lanes, part_rows(shape[0], len(plan))))
            continue
        step = shape[0] // pieces
        for piece in range(pieces):
            if step % 3 == 0:
                third = step // 3
                parts = [(piece * step + part * third, third) for part in range(3)]
                plan.append((number, "lead", None, parts))
            else:
                plan.append((number, "rows", (piece * step, step), part_rows(shape[1], len(plan))))
    return plan


class Slot:
    def __init__(self, like):
        self.shape, self.dtype = like.shape, like.dtype
        self.ndim, self.size = len(like.shape), math.prod(like.shape)


def forward_all(places, shards, small, latent_blocks, cotangent_blocks, block_table, build, plan_of_hooks):
    arrays = [array for array, _ in shards]
    plan = gather_plan([(array.shape, pieces) for array, pieces in shards])
    frames, row_devices = places.frames, places.rows
    count, steps = len(arrays), len(plan)
    channels = places.channels
    cells = places.side * places.side
    roles = ((0, 1, 2), (1, 0, 2), (2, 1, 0), (2, 0, 1))
    peers_count = row_devices - 1

    wholes = [
        Slot(b16(*array.shape[:-2], array.shape[-2] * frames, array.shape[-1])) for array in arrays
    ]
    field, params = Slot(b16(cells, channels)), Slot(f32(*small.shape))
    RECORDING.append([])
    kept = build(field, params, list(zip(wholes, arrays)))
    stages = RECORDING.pop()

    vmem_inputs = []
    for _, stage_arrays, _, _, _, _ in stages:
        for array in stage_arrays:
            if not isinstance(array, Slot) and all(array is not seen for seen in vmem_inputs):
                vmem_inputs.append(array)
    vmem_outs = [field, params] + list(kept)
    inner = []
    for _, _, _, _, _, slots in stages:
        for slot in slots:
            if all(slot is not seen for seen in vmem_outs):
                inner.append(slot)

    def kernel(*refs):
        refs = list(refs)

        def take(number):
            taken, refs[:] = refs[:number], refs[number:]
            return taken

        sources = take(count)
        small_ref, latent_ref, cot_ref, table_ref = take(4)
        in_refs = take(len(vmem_inputs))
        targets = take(count)
        (cot_out,) = take(1)
        out_refs = take(len(vmem_outs))
        inner_refs = take(len(inner))
        (
            small_all, latent_all,
            send, recv, small_send, small_recv, lat_send, lat_recv, cot_send, cot_recv, own_sem,
        ) = refs
        frame, row = lax.axis_index("frame"), lax.axis_index("rows")
        frame_bit, core_bit = frame // 2, frame % 2
        across = (1 - frame_bit) * 2 + core_bit
        beside = frame_bit * 2 + 1 - core_bit
        corner = (1 - frame_bit) * 2 + 1 - core_bit
        x_bit, z_bit = row % 2, row // 2 % 2
        over = {
            "y": (across, row),
            "core": (beside, row),
            "corner": (corner, row),
            "x": (frame, row + 1 - 2 * x_bit),
            "z": (frame, row + 2 - 4 * z_bit),
        }
        peers = [(row + step) % row_devices for step in range(1, row_devices)]
        def remote(source, target, send_sem, recv_sem, place):
            return pltpu.make_async_remote_copy(
                src_ref=source,
                dst_ref=target,
                send_sem=send_sem,
                recv_sem=recv_sem,
                device_id=place,
                device_id_type=MESH,
            )

        barrier = pltpu.get_barrier_semaphore()
        greeted = [over["y"], over["core"], over["corner"]] + [(frame, peer) for peer in peers]
        for place in greeted:
            pl.semaphore_signal(barrier, inc=1, device_id=place, device_id_type=MESH)

        def view(ref, step, part, shard):
            number, kind, leads, parts = plan[step]
            rows = arrays[number].shape[-2]
            begin = 0 if shard is None else pl.multiple_of(shard * rows, 16)
            if kind == "lead":
                first, size = parts[0][0], sum(length for _, length in parts)
                if part is not None:
                    first, size = parts[part]
                where = pl.ds(first, size)
                return ref.at[where] if shard is None else ref.at[where, pl.ds(begin, rows)]
            start, size = (0, rows) if part is None else parts[part]
            where = pl.ds(begin + start, size)
            if kind is None:
                return ref.at[where, pl.ds(*leads)]
            return ref.at[pl.ds(*leads), where]

        def move(step, part, shard, source, way, slot):
            return remote(
                source, view(targets[plan[step][0]], step, part, shard), send.at[step, slot],
                recv.at[step, slot], over[way],
            )

        def fetched(step, part):
            source = view(sources[plan[step][0]], step, part, None)
            return move(step, part, frame, source, "y", 0)

        def shared(step):
            return move(step, None, frame, view(sources[plan[step][0]], step, None, None), "core", 3)

        def passed(step, part, way, slot):
            source = view(targets[plan[step][0]], step, part, across)
            return move(step, part, across, source, way, slot)

        def by_role(action):
            for role in range(4):
                pl.when((z_bit == role // 2) & (x_bit == role % 2))(functools.partial(action, role))

        def start_fetch(role):
            for step in range(min(AHEAD, steps)):
                fetched(step, roles[role][0]).start()

        def act(kind, step):
            def over_y(role):
                part = roles[role][0]
                fetched(step, part).wait_recv()
                if step + AHEAD < steps:
                    fetched(step + AHEAD, part).start()
                passed(step, part, "z", 2).start()
                if role < 2:
                    passed(step, part, "x", 1).start()
                passed(step, part, "core", 4).start()
                if step + AHEAD < steps:
                    shared(step + AHEAD).start()

            def over_z(role):
                part = roles[role][2]
                passed(step, part, "z", 2).wait_recv()
                if role >= 2:
                    passed(step, part, "x", 1).start()
                passed(step, part, "core", 6).start()

            def over_x(role):
                part = roles[role][1]
                passed(step, part, "x", 1).wait_recv()
                passed(step, part, "core", 5).start()

            def finish(role):
                shared(step).wait_recv()
                for part, slot in zip(roles[role], (4, 5, 6)):
                    passed(step, part, "core", slot).wait_recv()

            by_role({"y": over_y, "z": over_z, "x": over_x, "done": finish}[kind])

        def end_sends(role):
            part_y, part_x, part_z = roles[role]
            for step in range(steps):
                fetched(step, part_y).wait_send()
                shared(step).wait_send()
                passed(step, part_y, "z", 2).wait_send()
                passed(step, part_y if role < 2 else part_z, "x", 1).wait_send()
                for part, slot in ((part_y, 4), (part_x, 5), (part_z, 6)):
                    passed(step, part, "core", slot).wait_send()

        smalls = [
            remote(small_ref, small_all.at[frame], small_send.at[slot], small_recv.at[slot], over[way])
            for slot, way in enumerate(("y", "core", "corner"))
        ]
        latent_copies = [
            remote(latent_ref.at[peer], latent_all.at[row], lat_send.at[step], lat_recv.at[step], (frame, peer))
            for step, peer in enumerate(peers)
        ]
        cot_copies = [
            remote(cot_ref.at[peer], cot_out.at[row], cot_send.at[step], cot_recv.at[step], (frame, peer))
            for step, peer in enumerate(peers)
        ]
        owns = [
            pltpu.make_async_copy(cot_ref.at[row], cot_out.at[row], own_sem.at[2]),
            pltpu.make_async_copy(small_ref, small_all.at[frame], own_sem.at[0]),
            pltpu.make_async_copy(latent_ref.at[row], latent_all.at[row], own_sem.at[1]),
        ]
        for copy in owns:
            copy.start()
        pl.semaphore_wait(barrier, len(greeted))
        for copy in smalls + latent_copies:
            copy.start()
        by_role(start_fetch)
        for step in range(min(AHEAD, steps)):
            shared(step).start()

        def run_actions(actions):
            for action in actions:
                if action[0] == "cotangent":
                    for copy in cot_copies:
                        copy.start()
                else:
                    act(*action)

        for copy in smalls:
            copy.wait_recv()
        owns[1].wait()
        field_ref, params_ref = out_refs[:2]
        total = small_all[0]
        for number in range(1, frames):
            total += small_all[number]
        params_ref[...] = total
        for copy in latent_copies:
            copy.wait_recv()
        owns[2].wait()
        blocks = latent_all[...].reshape(-1, channels)
        field_ref[...] = to_low(dot_nn(table_ref[...], blocks))

        order = [frame, across, beside, corner]
        known = [(field, field_ref), (params, params_ref)]
        known += list(zip(vmem_inputs, in_refs)) + list(zip(vmem_outs[2:], out_refs[2:]))
        known += list(zip(inner, inner_refs)) + list(zip(wholes, targets)) + list(zip(arrays, sources))

        def ref_of(array):
            return next(ref for held, ref in known if held is array)

        for number, (body, stage_arrays, groups, outs, scratch, slots) in enumerate(stages):
            before, hooks = plan_of_hooks[number]
            run_actions(before)
            pending = list(hooks)

            def hooked():
                if pending:
                    run_actions(pending.pop(0))

            HOOK.append(hooked)

            def stage(*scratch_refs):
                body(
                    order,
                    [ref_of(array) for array in stage_arrays],
                    [[ref_of(array) for array in group] for group in groups],
                    [ref_of(slot) for slot in slots],
                    scratch_refs,
                )

            pl.run_scoped(stage, *scratch)
            HOOK.pop()
            for rest in pending:
                run_actions(rest)
        run_actions(plan_of_hooks[len(stages)][0])
        by_role(end_sends)
        for copy in smalls + latent_copies:
            copy.wait_send()
        for copy in cot_copies:
            copy.wait()
        owns[0].wait()

    anywhere = pl.BlockSpec(memory_space=pl.ANY)
    whole_block = pl.BlockSpec(memory_space=pltpu.VMEM)
    as_shape = lambda slot: jax.ShapeDtypeStruct(slot.shape, slot.dtype)
    dma = pltpu.SemaphoreType.DMA
    results = pl.pallas_call(
        kernel,
        out_shape=[as_shape(slot) for slot in wholes] + [b16(*cotangent_blocks.shape)] + [as_shape(slot) for slot in vmem_outs],
        in_specs=[anywhere] * (count + 3) + [whole_block] * (1 + len(vmem_inputs)),
        out_specs=[anywhere] * (count + 1) + [whole_block] * len(vmem_outs),
        scratch_shapes=[pltpu.VMEM(slot.shape, slot.dtype) for slot in inner]
        + [
            pltpu.VMEM((frames,) + small.shape, jnp.float32),
            pltpu.VMEM(latent_blocks.shape, jnp.bfloat16),
            dma((steps, 7)),
            dma((steps, 7)),
            dma((3,)),
            dma((3,)),
            dma((peers_count,)),
            dma((peers_count,)),
            dma((peers_count,)),
            dma((peers_count,)),
            dma((3,)),
        ],
        compiler_params=pltpu.CompilerParams(
            collective_id=0, has_side_effects=True, vmem_limit_bytes=58 * 2**20
        ),
        cost_estimate=pl.CostEstimate(flops=0, bytes_accessed=4096, transcendentals=0),
    )(*arrays, small, latent_blocks, cotangent_blocks, block_table, *vmem_inputs)
    wholes_out = list(zip(results[:count], arrays))
    return (wholes_out, results[count], results[count + 1], results[count + 2], results[count + 3 :])


def reduce_piece(row_devices):
    return max(256, 16 * row_devices)


def reduce_all(parts, summed, row_devices, build, fused, plan_of_hooks, block_table, block_max):
    frames, channels = parts[0].shape[0], parts[0].shape[2]
    sizes = [part.shape[1] for part in parts]
    piece = reduce_piece(row_devices)
    count = -(-sum(sizes) // piece)
    total = count * piece
    more = -(-summed.shape[0] // piece)
    every = count + more
    group = row_devices // 2
    half = piece // 2
    share = half // group
    stages = []
    if fused:
        RECORDING.append(stages)
    (result,) = build()
    if fused:
        RECORDING.pop()
    vmem_inputs, any_inputs, inner = ([] if fused else [result]), [], []

    def note(array, seen):
        if all(array is not other for other in seen):
            seen.append(array)

    for _, stage_arrays, groups, _, _, slots in stages:
        for array in stage_arrays:
            if not isinstance(array, Slot):
                note(array, vmem_inputs)
        for array in [array for held_group in groups for array in held_group]:
            note(array, any_inputs)
        inner += slots

    def kernel(*refs):
        refs = list(refs)

        def take(number):
            taken, refs[:] = refs[:number], refs[number:]
            return taken

        sources = take(len(parts))
        any_refs = take(len(any_inputs))
        (summed_ref, blocks_ref) = take(2)
        in_refs = take(len(vmem_inputs))
        out_ref, moved_ref = take(2)
        inner_refs = take(len(inner))
        known = list(zip(any_inputs, any_refs)) + list(zip(vmem_inputs, in_refs))
        known += list(zip(inner, inner_refs))

        def ref_of(array):
            return next(ref for held_array, ref in known if held_array is array)

        (
            held, ready, leaving, from_core, from_y, from_x, halves, from_z,
            load_sem, core_send, core_recv, y_send, y_recv, x_send, x_recv, z_send, z_recv,
            back_send, back_recv, last_send, last_recv, move_send, move_recv,
        ) = refs
        frame, row = lax.axis_index("frame"), lax.axis_index("rows")
        frame_bit, core_bit = frame // 2, frame % 2
        across = (1 - frame_bit) * 2 + core_bit
        beside = frame_bit * 2 + 1 - core_bit
        corner = (1 - frame_bit) * 2 + 1 - core_bit
        x_bit, level = row % 2, row // 2
        over_x = (frame, row + 1 - 2 * x_bit)
        peers = [(level + step) % group for step in range(1, group)]
        barrier = pltpu.get_barrier_semaphore()
        places = [(beside, row), (across, row), over_x]
        row_peers = [(row + step) % row_devices for step in range(1, row_devices)]
        places = places[:2] + [(frame, peer) for peer in row_peers]
        for place in places:
            pl.semaphore_signal(barrier, inc=1, device_id=place, device_id_type=MESH)
        loads = []
        start = 0
        for number, source in enumerate(sources):
            loads.append(
                pltpu.make_async_copy(
                    source, held.at[:, pl.ds(start, sizes[number])], load_sem.at[number]
                )
            )
            loads[-1].start()
            start = start + sizes[number]
        loads.append(
            pltpu.make_async_copy(
                summed_ref, ready.at[pl.ds(0, summed.shape[0])], load_sem.at[len(sources)]
            )
        )
        loads[-1].start()
        if summed.shape[0] < more * piece:
            ready[summed.shape[0] :, :] = jnp.zeros(
                (more * piece - summed.shape[0], channels), jnp.bfloat16
            )
        if start < total:
            held[:, start:, :] = jnp.zeros((frames, total - start, channels), jnp.bfloat16)
        for load in loads:
            load.wait()
        pl.semaphore_wait(barrier, len(places))

        def send(source, target, send_sem, recv_sem, place):
            return pltpu.make_async_remote_copy(
                src_ref=source,
                dst_ref=target,
                send_sem=send_sem,
                recv_sem=recv_sem,
                device_id=place,
                device_id_type=MESH,
            )

        def add(first, second):
            return to_low(first.astype(jnp.float32) + second.astype(jnp.float32))

        def rows(number):
            return pl.ds(number * piece, piece)

        keep_start = pl.multiple_of(x_bit * half, 16)
        give_start = pl.multiple_of((1 - x_bit) * half, 16)

        def over_core(number):
            return [
                send(
                    held.at[shard, rows(number)],
                    from_core.at[slot, rows(number)],
                    core_send.at[number, slot],
                    core_recv.at[number, slot],
                    (beside, row),
                )
                for slot, shard in enumerate((beside, corner))
            ]

        def over_y(number):
            return send(
                held.at[across, rows(number)], from_y.at[rows(number)], y_send.at[number],
                y_recv.at[number], (across, row),
            )

        def own_rows(number, start):
            if number < count:
                return held.at[frame, pl.ds(number * piece + start, half)]
            return ready.at[pl.ds((number - count) * piece + start, half)]

        def along_x(number):
            return send(
                own_rows(number, give_start),
                from_x.at[pl.ds(number * half, half)],
                x_send.at[number],
                x_recv.at[number],
                over_x,
            )

        def along_z(number, step):
            peer = peers[step]
            start = pl.multiple_of(number * half + peer * share, 16)
            return send(
                halves.at[pl.ds(start, share)],
                from_z.at[number, step],
                z_send.at[number, step],
                z_recv.at[number, step],
                (frame, peer * 2 + x_bit),
            )

        def own_share(number):
            return pl.ds(
                pl.multiple_of(number * piece + keep_start + level * share, 16), share
            )

        def back_z(number, step):
            return send(
                out_ref.at[own_share(number)], out_ref.at[own_share(number)],
                back_send.at[number, step], back_recv.at[number, step],
                (frame, peers[step] * 2 + x_bit),
            )

        def back_x(number):
            keep = pl.ds(pl.multiple_of(number * piece + keep_start, 16), half)
            return send(
                out_ref.at[keep], out_ref.at[keep], last_send.at[number], last_recv.at[number],
                over_x,
            )

        for number in range(count):
            for copy in over_core(number):
                copy.start()

        def stage_core(number):
            for copy in over_core(number):
                copy.wait_recv()
            held[across, rows(number), :] = add(
                held[across, rows(number), :], from_core[1, rows(number), :]
            )
            over_y(number).start()
            held[frame, rows(number), :] = add(
                held[frame, rows(number), :], from_core[0, rows(number), :]
            )

        def stage_y(number):
            if number < count:
                over_y(number).wait_recv()
                held[frame, rows(number), :] = add(
                    held[frame, rows(number), :], from_y[rows(number), :]
                )
            along_x(number).start()

        def stage_x(number):
            along_x(number).wait_recv()
            where = pl.ds(number * half, half)
            halves[where, :] = add(own_rows(number, keep_start)[...], from_x[where, :])
            for step in range(group - 1):
                along_z(number, step).start()

        def stage_z(number):
            start = pl.multiple_of(number * half + level * share, 16)
            value = halves[pl.ds(start, share), :].astype(jnp.float32)
            for step in range(group - 1):
                along_z(number, step).wait_recv()
                value += from_z[number, step].astype(jnp.float32)
            out_ref[own_share(number), :] = to_low(value)
            for step in range(group - 1):
                back_z(number, step).start()

        def stage_back(number):
            for step in range(group - 1):
                back_z(number, step).wait_recv()
            back_x(number).start()

        steps_on = (stage_y, stage_x, stage_z, stage_back)

        def take_turn(turn):
            if turn < count:
                stage_core(turn)
            for late, step in enumerate(steps_on):
                if 0 <= turn - late < more:
                    step(count + turn - late)
                if 0 <= turn - 1 - late < count:
                    step(turn - 1 - late)

        order = [frame, across, beside, corner]
        turns = list(range(max(count + 4, more + 3)))
        for number, (body, stage_arrays, groups, outs, scratch, slots) in enumerate(stages):
            pending = list(plan_of_hooks[number])

            def hooked():
                if pending and pending.pop(0) and turns:
                    take_turn(turns.pop(0))

            HOOK.append(hooked)

            def stage(*scratch_refs):
                body(
                    order,
                    [ref_of(array) for array in stage_arrays],
                    [[ref_of(array) for array in held_group] for held_group in groups],
                    [ref_of(slot) for slot in slots],
                    scratch_refs,
                )

            pl.run_scoped(stage, *scratch)
            HOOK.pop()
        values = to_low(dot_tn(blocks_ref[...], to_low(ref_of(result)[...])))
        leaving[...] = values.reshape(row_devices, block_max, channels)
        moves = [
            send(
                leaving.at[peer], moved_ref.at[row], move_send.at[step], move_recv.at[step],
                (frame, peer),
            )
            for step, peer in enumerate(row_peers)
        ]
        for copy in moves:
            copy.start()
        moved_ref[row] = leaving[row]
        for turn in turns:
            take_turn(turn)
        for copy in moves:
            copy.wait()
        for number in range(count):
            for copy in over_core(number) + [over_y(number)]:
                copy.wait_send()
        for number in range(every):
            back_x(number).wait_recv()
            for copy in [along_x(number), back_x(number)]:
                copy.wait_send()
            for step in range(group - 1):
                along_z(number, step).wait_send()
                back_z(number, step).wait_send()

    dma = pltpu.SemaphoreType.DMA
    low_type = jnp.bfloat16
    anywhere = pl.BlockSpec(memory_space=pl.ANY)
    whole_block = pl.BlockSpec(memory_space=pltpu.VMEM)
    results = pl.pallas_call(
        kernel,
        out_shape=[b16(every * piece, channels), b16(row_devices, block_max, channels)],
        in_specs=[anywhere] * (len(parts) + len(any_inputs) + 1)
        + [whole_block] * (1 + len(vmem_inputs)),
        out_specs=[whole_block] * 2,
        scratch_shapes=[pltpu.VMEM(slot.shape, slot.dtype) for slot in inner]
        + [
            pltpu.VMEM((frames, total, channels), low_type),
            pltpu.VMEM((more * piece, channels), low_type),
            pltpu.VMEM((row_devices, block_max, channels), low_type),
            pltpu.VMEM((2, total, channels), low_type),
            pltpu.VMEM((total, channels), low_type),
            pltpu.VMEM((every * half, channels), low_type),
            pltpu.VMEM((every * half, channels), low_type),
            pltpu.VMEM((every, group - 1, share, channels), low_type),
            dma((len(parts) + 1,)),
            dma((count, 2)),
            dma((count, 2)),
            dma((count,)),
            dma((count,)),
            dma((every,)),
            dma((every,)),
            dma((every, group - 1)),
            dma((every, group - 1)),
            dma((every, group - 1)),
            dma((every, group - 1)),
            dma((every,)),
            dma((every,)),
            dma((row_devices - 1,)),
            dma((row_devices - 1,)),
        ],
        compiler_params=pltpu.CompilerParams(
            collective_id=1, has_side_effects=True, vmem_limit_bytes=60 * 2**20
        ),
        cost_estimate=pl.CostEstimate(flops=0, bytes_accessed=4096, transcendentals=0),
    )(*parts, *any_inputs, summed, block_table, *vmem_inputs)
    return (results[0][:total], results[0][total : total + summed.shape[0]], results[1])


def on_device(
    latents,
    cotangent,
    timesteps,
    prompt_ids,
    embed_table,
    res_gain,
    res_shift,
    res_conv,
    temb_weight,
    st_gain,
    st_shift,
    st_proj,
    st_attn,
    st_cross_kv,
    st_ff_in,
    st_ff_bias,
    st_ff_out,
    motion_gain,
    motion_shift,
    motion_proj,
    motion_attn,
    motion_ff_in,
    motion_ff_bias,
    motion_ff_out,
):
    frames_here, cell_count, channels = latents.shape
    places = Places(frames_here, channels)
    side = places.side
    cells = side * side
    valid = places.valid.astype(jnp.float32)
    table = group_table(channels)
    count = (places.safe_side * places.safe_side * (channels // GROUPS)).astype(jnp.float32)
    lanes = jnp.arange(128, dtype=jnp.int32)[None, :]
    masks = jnp.where(
        lanes == 0,
        valid[:, None],
        jnp.where(lanes == 1, places.cell_col[:, None] > 0, places.cell_col[:, None] < side - 1),
    ).astype(jnp.float32)
    key_bias = jnp.broadcast_to(((valid - 1.0) * -FAR)[None, :], (8, cells))
    order_row = shard_order()

    own = channels // places.frames
    clip_count, prompt_count = prompt_ids.shape
    own_temb = TEMB // places.frames
    time_low = to_low(jax.nn.silu(time_table(timesteps)))
    time_mine = lax.dynamic_slice_in_dim(time_low, places.frame * own_temb, own_temb, 1)
    time_part = matmul(time_mine, temb_weight)
    own_lanes = jnp.arange(channels, dtype=jnp.int32) // own == places.frame
    vectors = jnp.concatenate([motion_gain, motion_shift]).astype(jnp.float32)
    bias_rows = motion_ff_bias.shape[0] * places.frames // channels
    own_bias = jnp.arange(bias_rows)[:, None] == places.frame * (bias_rows // places.frames)
    small = jnp.concatenate(
        [
            jnp.where(own_lanes[None, :], jnp.tile(vectors, (1, places.frames)), 0.0),
            jnp.where(own_bias, motion_ff_bias.astype(jnp.float32).reshape(1, channels), 0.0),
            time_part,
        ]
    )
    small = jnp.pad(small, ((0, -small.shape[0] % 8), (0, 0)))
    flat_attn = motion_attn.reshape((-1,) + motion_attn.shape[2:])
    stats = jnp.broadcast_to(1.0 / count, (8, channels))
    sffbias = st_ff_bias.astype(jnp.float32).reshape(1, -1)
    grad_columns = places.blocks_to_columns(cotangent)

    vocab_rows = embed_table.shape[0]
    local_ids = prompt_ids - lax.axis_index(("frame", "rows")) * vocab_rows
    ids_table = onehot(local_ids.reshape(-1), vocab_rows)
    prompt_pad = -(-prompt_count // 16) * 16
    context = lax.psum(to_low(matmul(ids_table, embed_table)), ("frame", "rows"))
    context = context.reshape(clip_count, prompt_count, -1)
    context_low = lax.dynamic_index_in_dim(context, places.clip, 0, keepdims=False)
    context_low = jnp.pad(context_low, ((0, prompt_pad - prompt_count), (0, 0)))
    prompt_bias = jnp.where(jnp.arange(prompt_pad) < prompt_count, 0.0, FAR)
    prompt_row = jnp.broadcast_to(prompt_bias[None, :], (8, prompt_pad))
    prompt_col = jnp.broadcast_to(prompt_bias[:, None], (prompt_pad, 128))

    def build(field, params, whole):
        conv_all, sproj_all, sattn_all, cross_all, sffin_all, sffout_all = whole[:6]
        timed = (params, 13 + bias_rows, clip_count)
        conv_one = conv_forward(
            None, side, field, masks, res_gain, res_shift, stats, table, conv_all, 0, None, timed
        )
        resid = conv_forward(
            None, side, conv_one, masks, res_gain, res_shift, stats, table, conv_all, 1, [field],
            None,
        )
        proj_one, query, key, value, proj_two = self_forward(
            None, resid, masks, key_bias, st_gain, st_shift, stats, table, sproj_all, sattn_all
        )
        return [conv_one, resid, proj_one, query, key, value, proj_two]

    def acts(text):
        ways = {"y": "y", "z": "z", "x": "x", "d": "done", "c": "cotangent"}
        return [(ways[word[0]], int(word[1:] or 0)) for word in text.split()]

    hooks = [
        (acts("y0 y1 z0") + acts("y2 x0 z1") + acts("d0"), [acts("y3 z2"), acts("y4 x2"), []]),
        (acts("x1 z3 d1"), [acts("y5 z4"), [], acts("y6")]),
        (acts("x3 d2 d3") + acts("c"), [acts("x4"), acts("y7"), acts("z5"), [], acts("z6"), acts("y8"), acts("x5"), []]),
        (acts("x6 z7 d4") + acts("y9 x7 z8") + acts("y10 d5 z9") + acts("x8 z10 d6") + acts("d7 x9 x10") + acts("d8 d9 d10"), []),
    ]
    whole, cot_blocks, field, params, kept = forward_all(
        places,
        [
            (res_conv.reshape((-1,) + res_conv.shape[3:]), 2),
            (st_proj, 1),
            (st_attn, 1),
            (st_cross_kv, 1),
            (st_ff_in, 1),
            (st_ff_out, 1),
            (motion_proj, 1),
            (flat_attn, 1),
            (motion_ff_in, 1),
            (motion_ff_out, 1),
        ],
        small,
        places.blocks_by_unit(latents),
        places.blocks_by_unit(cotangent),
        places.block_table,
        build,
        hooks,
    )
    conv_all, sproj_all, sattn_all, cross_all, sffin_all, sffout_all = whole[:6]
    mproj_all, mattn_all, mffin_all, mffout_all = whole[6:]
    conv_one, resid, proj_one, query, key, value, proj_two = kept
    motion_rows = params
    cross_query, cross_key, cross_value, proj_three, st_out, motion_low = cross_forward(
        order_row, proj_two, resid, context_low, masks, prompt_row, st_gain, st_shift, params,
        stats, sffbias, table, sproj_all, sattn_all, cross_all, sffin_all, sffout_all,
    )

    motion_moved = places.unit_to_columns([motion_low])
    st_moved = places.unit_to_columns([to_low(st_out)])
    frame_total = places.frames * frames_here
    position = jnp.asarray(np.tile(frame_table(frame_total, channels), (places.share_total, 1)))
    per_group = max(n for n in range(1, 14) if places.share_total % n == 0)
    cell_of = np.arange(per_group * frame_total) // frame_total
    cell_bias = jnp.asarray(np.where(cell_of[:, None] == cell_of[None, :], 0.0, FAR).astype(np.float32))
    kept = motion_forward(
        order_row, motion_moved, places.pick_table, position, cell_bias, motion_rows, mproj_all,
        mattn_all,
    )
    zeds, motion_in = (kept[:3], kept[11])
    out_columns, grad_zed, d_ff, small_sums, wide_sums = motion_ff(
        order_row, zeds[2], st_moved, places.pick_table, grad_columns, motion_rows, 13, channels * bias_rows,
        mproj_all, mffin_all, mffout_all,
    )
    output = places.columns_to_blocks(out_columns)
    d_blocks = [None, None]
    for block in (1, 0):
        grad_zed, d_blocks[block], small_sums = motion_back(
            order_row, block, grad_zed, zeds[block], *kept[3 + 4 * block : 7 + 4 * block],
            motion_in if block == 0 else None, small_sums, position, cell_bias, motion_rows,
            mproj_all, mattn_all, [],
        )
    grad_motion = grad_zed

    small_rows = jnp.transpose(small_sums[:13].reshape(13, places.frames, own), (1, 0, 2))
    small_rows = jnp.pad(small_rows, ((0, 0), (0, 0), (0, channels - own)))
    bias_sums = wide_sums[0].reshape(places.frames, 1, channels)
    tail = jnp.concatenate([small_rows, bias_sums, jnp.zeros_like(small_rows[:, :2])], axis=1)
    d_first = lax.dynamic_update_slice(d_blocks[0], to_low(tail), (0, 5 * own, 0))

    def over_frame(gradient):
        return lax.psum_scatter(gradient, "frame", scatter_dimension=0, tiled=False)

    ff_mine = over_frame(d_ff)
    grad_gn = to_low(places.columns_to_unit(grad_motion))
    grad_two, grad_st = cross_backward(
        order_row, grad_gn, cot_blocks.reshape(-1, channels), places.block_table, st_out, proj_three, proj_two, cross_query, cross_key,
        cross_value, masks, prompt_col, st_gain, st_shift, motion_rows, stats, sffbias, table,
        sproj_all, sattn_all, sffin_all, sffout_all,
    )

    def build_back():
        grad_res = self_backward(
            order_row, [], grad_two, proj_one, query, key, value, resid, grad_st, masks, st_gain,
            st_shift, stats, table, sproj_all, sattn_all,
        )
        grad_conv = conv_backward(
            order_row, side, grad_res, conv_one, masks, res_gain, res_shift, stats, table, conv_all, 1,
            [],
        )
        return [
            conv_backward(
                order_row, side, grad_conv, field, masks, res_gain, res_shift, stats, table, conv_all,
                0, [grad_res],
            )
        ]

    turns_in = [[0, 1, 0, 0, 1, 0, 0, 1], [1, 1, 1], [1, 1, 1]]
    attn_sum, ff_sum, moved = reduce_all(
        [d_first, d_blocks[1]], ff_mine, places.rows, build_back, cells <= 640, turns_in,
        places.block_table, places.block_max,
    )
    attn_sum, ff_sum = (attn_sum.astype(jnp.float32), ff_sum.astype(jnp.float32))
    input_grad = places.blocks_from_units(moved).astype(jnp.float32)
    ff_in_grad = jnp.concatenate([ff_sum[i * own : (i + 1) * own] for i in range(4)], axis=1)
    ff_out_grad = ff_sum[4 * own : 8 * own]
    zero_sum, one_sum = (attn_sum[: 5 * own + 16], attn_sum[5 * own + 16 : 9 * own + 16])
    attn_grad = jnp.concatenate([zero_sum[: 4 * own], one_sum]).reshape(motion_attn.shape)
    proj_grad = jnp.stack([zero_sum[4 * own : 5 * own], ff_sum[8 * own :]])
    small_sum = zero_sum[5 * own :]
    gain_grad, shift_grad, ff_bias_grad = (small_sum[:4, :own], small_sum[4:13, :own], small_sum[13])

    return (
        output,
        input_grad,
        gain_grad,
        shift_grad,
        proj_grad,
        attn_grad,
        ff_in_grad,
        ff_bias_grad,
        ff_out_grad,
    )


def solution(mesh):
    return jax.shard_map(
        on_device,
        mesh=mesh,
        in_specs=(
            P("frame", "rows", None),
            P("frame", "rows", None),
            P(),
            P(),
            P(("frame", "rows"), None),
            P(),
            P(),
            P(None, None, None, "frame", None),
            P("frame", None),
            P(),
            P(),
            P(None, "frame", None),
            P(None, "frame", None),
            P(None, "frame", None),
            P("frame", None),
            P(),
            P("frame", None),
            P(None, "frame"),
            P(None, "frame"),
            P(None, "frame", None),
            P(None, None, "frame", None),
            P("frame", None),
            P("frame"),
            P("frame", None),
        ),
        out_specs=(
            P("frame", "rows", None),
            P("frame", "rows", None),
            P(None, "frame"),
            P(None, "frame"),
            P(None, "frame", None),
            P(None, None, "frame", None),
            P("frame", None),
            P("frame"),
            P("frame", None),
        ),
        check_vma=False,
    )
```
